32 devices in a mesh: groups: 2 (over y), tensor: 4 (over z), expert: 4 (over x, core).
Axes of the slice: x: 2, y: 2, z: 4, core: 2. Of those that a mesh axis runs over, the one named last changes fastest.
Arguments:
- tokens: bfloat16 [1024, 3072], P(('groups', 'expert'), 'tensor'), parts along dimension 0, may hold values from -6 to 6
- expert_ids: int32 [1024, 2], P(('groups', 'expert')), parts along dimension 0, may hold values from 0 to 3, all different within a row; in each aligned block of 128 rows (0 to 127, 128 to 255, ...) at most 64 rows name the same one
- route_logits: float32 [1024, 2], P(('groups', 'expert')), parts along dimension 0, may hold values from -6 to 6
- gate_weight: bfloat16 [4, 3072, 8192], P('expert', None, 'tensor'), may hold values from -0.109375 to 0.109375
- up_weight: bfloat16 [4, 3072, 8192], P('expert', None, 'tensor'), may hold values from -0.109375 to 0.109375
- down_weight: bfloat16 [4, 8192, 3072], P('expert', 'tensor'), may hold values from -0.09375 to 0.09375
Outputs:
- mixed: bfloat16 [1024, 3072], P(('groups', 'expert'), 'tensor'), parts along dimension 0
The draws below stay inside these ranges and needn't reach their ends.
There are 2 independent parts, one for each index of `groups`. The reference program is written for one: setup_inputs(seed, part) draws one part's arguments, and reference() takes and returns one part's arrays. A program takes and returns all parts, laid end to end along the dimension named above; an argument that names none is the same for every part. Nothing has to cross between parts.
Inputs may be any that keep to these rules, and one draw needn't show every extreme that they name: `expert_ids`: each row names two different experts. In each aligned block of 128 rows (the rows of one device) no expert is named by more than 64 rows, a bound that some block reaches.
All inputs are finite; a program needn't handle non-finite values.
Results may differ from the reference program's by a relative error of at most 0.012.
Values may be sent and summed in bfloat16 or wider, within the bound.
No kernel may reach another device: no remote copies, remote signals or barrier semaphores. Data moves between devices by JAX's collectives and lax.ppermute only.
A program may use at most 128 MiB of HBM per device.

```python
import math
import jax
import jax.numpy as jnp
import numpy as np
from jax import lax

D = 3072
FF = 8192
TOK_DEV = 128
CAP = 64
EXPERTS = 4
TOKENS = 512
N_TENSOR = 4
N_EXPERT = 4


def raised(values, own_key, source, target, blocks, factor):
    def block_of(dim):
        return (jnp.arange(values.shape[dim]) // (values.shape[dim] // blocks)).reshape((-1,) + (1,) * (values.ndim - 1 - dim))

    one_side = jax.random.permutation(own_key, blocks)[block_of(target)]
    other_side = (block_of(target) + blocks // 2) % blocks
    return jnp.where((block_of(source) == one_side) | (block_of(source) == other_side), factor * values, values)


def block_scale(own_key, extent, cuts, least, largest):
    factor_of, own = 1.0, jax.random.fold_in(own_key, 6)
    for dim, shards_of in cuts:
        steps = jnp.exp(jax.random.uniform(jax.random.fold_in(own, dim), (shards_of,), jnp.float32, least / len(cuts), largest / len(cuts)))
        factor_of = factor_of * jnp.repeat(steps, extent[dim] // shards_of).reshape([-1 if axis == dim else 1 for axis in range(len(extent))])
    return factor_of


def shared_out(own_key, own, number, rows, number_of, top, most, lean):
    sequence = jax.random.permutation(own_key, number_of)
    crowded, common = load_shares(number_of, rows * top, most, lean, True), load_shares(number_of, rows * top, most, lean, False)
    places = jnp.arange(number_of)

    def named(tallies, rotation):
        used = int((tallies > 0).sum())
        fixed = max(1, used // 4)
        passed = fixed + (places - fixed + rotation * (used - fixed)) % max(1, number_of - fixed)
        return jnp.zeros((number_of,), jnp.int32).at[sequence[jnp.where(places < fixed, places, passed)]].set(jnp.asarray(tallies, jnp.int32))

    tallies = jnp.where(number % 4 == 0, named(crowded, number // 4), named(common, number - number // 4 - 1))
    mixed = jax.random.permutation(jax.random.fold_in(own, 3), number_of)
    giver, receiver = mixed[0:number_of // 2 * 2:2], mixed[1:number_of // 2 * 2:2]
    margin = jnp.minimum(tallies[giver] - 1, most - tallies[receiver]) // 2
    margin = jnp.where((giver == sequence[0]) | (receiver == sequence[0]) | (tallies[receiver] == 0), 0, jnp.maximum(margin, 0))
    passed = jax.random.randint(jax.random.fold_in(own, 4), (number_of // 2,), 0, 1 << 20) % (margin + 1)
    tallies = tallies.at[giver].add(-passed).at[receiver].add(passed)
    labels = jnp.searchsorted(jnp.cumsum(tallies), jnp.arange(rows * top), side="right").astype(jnp.int32)
    listing = labels.reshape(top, rows).T
    listing = listing[jax.random.permutation(jax.random.fold_in(own, 1), rows)]
    rotation = jax.random.randint(jax.random.fold_in(own, 2), (rows, 1), 0, top)
    return jnp.take_along_axis(listing, (jnp.arange(top)[None, :] + rotation) % top, axis=1)


def load_shares(number_of, total, reach, slope, full):
    loads = [(1 << 20) // math.isqrt(standing ** slope) + 1 for standing in range(1, number_of + 1)]
    largest = reach if full else min(reach, max(-(-total // number_of), total * loads[0] // sum(loads)))
    least = 1 if total - largest >= number_of - 1 else 0
    given, surplus = [largest] + [least] * (number_of - 1), total - largest - least * (number_of - 1)
    while surplus > 0:
        candidates = [i for i in range(1, number_of) if given[i] < largest] or [i for i in range(1, number_of) if given[i] < reach]
        mass, budget = sum([loads[i] for i in candidates]), surplus
        for i in candidates:
            more = min(reach - given[i], max(1, budget * loads[i] // mass), surplus)
            given[i] = given[i] + more
            surplus = surplus - more
    return np.array(given)


def noise(own_key, shape, spread, bound, cuts=(), kind=jnp.bfloat16):
    level = block_scale(own_key, shape, cuts, -0.22, 0.18) if cuts else 1.0
    result = jax.random.normal(own_key, shape, jnp.float32) * spread * level
    return jnp.minimum(jnp.maximum(result, -bound), bound).astype(kind)


def bell_draw_with(own_key, shape, spread, limit, cuts, heavy, kind=jnp.bfloat16):
    result = spread * jax.random.normal(own_key, shape, jnp.float32)
    if cuts:
        result = result * block_scale(own_key, shape, cuts, -0.22, 0.18)
    return jnp.clip(raised(result, jax.random.fold_in(own_key, 3), *heavy), -limit, limit).astype(kind)


def setup_inputs(seed: int = 0, part: int = 0) -> dict:
    streams_of = jax.random.split(jax.random.key(seed), 7)
    part_splits = jax.random.split(jax.random.fold_in(streams_of[6], part), 7)
    tokens = noise(part_splits[0], (TOKENS, D), 1.0, 6.0, ((0, 4), (1, 4)))
    expert_ids_keys = jax.random.split(jax.random.fold_in(part_splits[1], 1), TOKENS // TOK_DEV)
    expert_ids_turns = jax.random.permutation(jax.random.fold_in(part_splits[1], 3), TOKENS // TOK_DEV)
    expert_ids = jax.vmap(lambda own, number: shared_out(jax.random.fold_in(part_splits[1], 2), own, number, TOK_DEV, EXPERTS, 2, CAP, 2))(expert_ids_keys, expert_ids_turns).reshape((TOKENS, 2))
    route_logits = noise(part_splits[2], (TOKENS, 2), 1.5, 6.0, ((0, 4),), jnp.float32)
    gate_weight = noise(streams_of[3], (EXPERTS, D, FF), D ** -0.5, 0.109375, ((0, 4), (2, 4)))
    up_weight = noise(streams_of[4], (EXPERTS, D, FF), D ** -0.5, 0.109375, ((0, 4), (2, 4)))
    down_weight = bell_draw_with(streams_of[5], (EXPERTS, FF, D), FF ** -0.5, 0.09375, ((0, 4), (1, 4)), (1, 2, 4, 2.0))
    return dict(tokens=tokens, expert_ids=expert_ids, route_logits=route_logits, gate_weight=gate_weight, up_weight=up_weight, down_weight=down_weight)


def reference(tokens, expert_ids, route_logits, gate_weight, up_weight, down_weight):
    blocks = expert_ids.reshape(N_EXPERT, TOK_DEV * 2)
    onehot = (blocks[:, :, None] == jnp.arange(EXPERTS, dtype=jnp.int32)[None, None, :]).astype(jnp.int32)
    before = jnp.cumsum(onehot, axis=1) - onehot
    position = jnp.sum(before * onehot, axis=2).reshape(TOKENS, 2).astype(jnp.int32)
    source = (jnp.arange(TOKENS, dtype=jnp.int32) // TOK_DEV).astype(jnp.int32)
    source_two = jnp.broadcast_to(source[:, None], (TOKENS, 2))
    rows_two = jnp.broadcast_to(tokens[:, None, :], (TOKENS, 2, D))
    buffer = jnp.zeros((EXPERTS, N_EXPERT, CAP, D), jnp.bfloat16)
    buffer = buffer.at[expert_ids, source_two, position].set(rows_two)
    width = FF // N_TENSOR

    def one_expert(index):
        inputs = buffer[index].reshape(N_EXPERT * CAP, D)
        gate = jnp.dot(inputs, gate_weight[index], preferred_element_type=jnp.float32)
        up = jnp.dot(inputs, up_weight[index], preferred_element_type=jnp.float32)
        hidden = (jax.nn.silu(gate) * up).astype(jnp.bfloat16)
        pieces = hidden.reshape(N_EXPERT * CAP, N_TENSOR, width).astype(jnp.float32)
        down = down_weight[index].reshape(N_TENSOR, width, D).astype(jnp.float32)
        partial_value = jnp.einsum("rjf,jfd->jrd", pieces, down)
        rounded = lax.optimization_barrier(partial_value.astype(jnp.bfloat16)).astype(jnp.float32)
        return jnp.sum(rounded, axis=0).reshape(N_EXPERT, CAP, D)

    outputs = lax.map(one_expert, jnp.arange(EXPERTS, dtype=jnp.int32))
    picked = outputs[expert_ids, source_two, position]
    share = jax.nn.sigmoid(route_logits[:, 0] - route_logits[:, 1])
    mixing = jnp.stack([share, 1.0 - share], axis=1)
    return jnp.sum(picked * mixing[:, :, None], axis=1).astype(jnp.bfloat16)
```

```python
import functools

import jax
import jax.numpy as jnp
from jax import lax
from jax.experimental import pallas as pl
from jax.experimental.pallas import tpu as pltpu
from jax.sharding import PartitionSpec as P

F32 = jnp.float32
BF16 = jnp.bfloat16
VMEM_LIMIT = 24 * 1024 * 1024


def params():
    return pltpu.CompilerParams(vmem_limit_bytes=VMEM_LIMIT)


def cost(flops, moved):
    return pl.CostEstimate(flops=flops, bytes_accessed=moved, transcendentals=0)


def whole(shape):
    return pl.BlockSpec(shape, lambda *_: (0,) * len(shape))


def routing_kernel(me_ref, ids_ref, placed_ref, *, experts, capacity):
    rows = ids_ref.shape[1]
    relative = lax.bitwise_xor(ids_ref[...], me_ref[0])
    lane = lax.broadcasted_iota(jnp.int32, (experts, rows), 0)
    names = (lane == relative[0:1]) | (lane == relative[1:2])
    earlier = lax.broadcasted_iota(jnp.int32, (rows, rows), 0) < lax.broadcasted_iota(
        jnp.int32, (rows, rows), 1
    )
    before = jnp.dot(
        names.astype(BF16), earlier.astype(BF16), preferred_element_type=F32
    ).astype(jnp.int32)
    position = jnp.where(names, before, -1)
    slot = lax.broadcasted_iota(jnp.int32, (capacity, rows), 0)
    for d in range(experts):
        hit = position[d : d + 1] == slot
        placed_ref[d * capacity : (d + 1) * capacity, :] = jnp.where(hit, 1.0, 0.0).astype(BF16)


def place(me, expert_ids, experts, capacity):
    rows = expert_ids.shape[0]
    return pl.pallas_call(
        functools.partial(routing_kernel, experts=experts, capacity=capacity),
        out_shape=jax.ShapeDtypeStruct((experts * capacity, rows), BF16),
        in_specs=[
            pl.BlockSpec(memory_space=pltpu.SMEM),
            pl.BlockSpec(memory_space=pltpu.VMEM),
        ],
        out_specs=pl.BlockSpec(memory_space=pltpu.VMEM),
        compiler_params=params(),
        name="routing",
    )(me.reshape(1), expert_ids.T)


def dispatch_kernel(placed_ref, block_ref, *out_refs):
    capacity = out_refs[0].shape[0]
    for d, out in enumerate(out_refs):
        out[...] = jnp.dot(
            placed_ref[d * capacity : (d + 1) * capacity, :],
            block_ref[...],
            preferred_element_type=F32,
        ).astype(BF16)


def dispatch(placed, block, experts, capacity):
    rows, width = block.shape
    return pl.pallas_call(
        dispatch_kernel,
        out_shape=[jax.ShapeDtypeStruct((capacity, width), BF16)] * experts,
        in_specs=[pl.BlockSpec(memory_space=pltpu.VMEM)] * 2,
        out_specs=[pl.BlockSpec(memory_space=pltpu.VMEM)] * experts,
        cost_estimate=cost(2 * experts * capacity * rows * width, 4 * rows * width),
        compiler_params=params(),
        name="dispatch",
    )(placed, block)


def gate_up_kernel(*refs, experts, first, last):
    x_refs = refs[1 : 1 + experts]
    gate_w, up_w = refs[1 + experts : 3 + experts]
    rest = refs[3 + experts :]
    if not first:
        old_gate, old_up = rest[:2]
        rest = rest[2:]
    x = jnp.concatenate([r[...] for r in x_refs], axis=0)
    gate = jnp.dot(x, gate_w[0], preferred_element_type=F32)
    up = jnp.dot(x, up_w[0], preferred_element_type=F32)
    if not first:
        gate = gate + old_gate[...]
        up = up + old_up[...]
    if last:
        rest[0][...] = (gate / (1.0 + jnp.exp(-gate)) * up).astype(BF16)
    else:
        rest[0][...] = gate
        rest[1][...] = up


def gate_up(part, x_blocks, gate_w, up_w, sums, last):
    experts = len(x_blocks)
    capacity, width = x_blocks[0].shape
    rows = experts * capacity
    hidden = gate_w.shape[2]
    tile = min(512, hidden)
    first = sums is None
    weight = pl.BlockSpec((1, width, tile), lambda n, part: (0, part[0], n))
    column = pl.BlockSpec((rows, tile), lambda n, part: (0, n))
    if last:
        out_shape = jax.ShapeDtypeStruct((rows, hidden), BF16)
        out_specs = column
    else:
        out_shape = [jax.ShapeDtypeStruct((rows, hidden), F32)] * 2
        out_specs = [column] * 2
    return pl.pallas_call(
        functools.partial(gate_up_kernel, experts=experts, first=first, last=last),
        out_shape=out_shape,
        grid_spec=pltpu.PrefetchScalarGridSpec(
            num_scalar_prefetch=1,
            grid=(hidden // tile,),
            in_specs=[whole((capacity, width))] * experts
            + [weight] * 2
            + ([] if first else [column] * 2),
            out_specs=out_specs,
        ),
        cost_estimate=cost(4 * rows * width * hidden, 4 * width * hidden + 16 * rows * hidden),
        compiler_params=params(),
        name="gate_up",
    )(part.reshape(1), *x_blocks, gate_w, up_w, *(() if first else sums))


def down_kernel(part_ref, h_ref, w_ref, *out_refs):
    capacity = out_refs[0].shape[0]
    y = jnp.dot(h_ref[...], w_ref[0], preferred_element_type=F32).astype(BF16)
    for d, out in enumerate(out_refs):
        out[...] = y[d * capacity : (d + 1) * capacity]


def down(part, hidden, down_w, width, experts):
    rows, depth = hidden.shape
    capacity = rows // experts
    tile = min(256, width)
    steps = width // tile
    return pl.pallas_call(
        down_kernel,
        out_shape=[jax.ShapeDtypeStruct((capacity, width), BF16)] * experts,
        grid_spec=pltpu.PrefetchScalarGridSpec(
            num_scalar_prefetch=1,
            grid=(steps,),
            in_specs=[
                whole((rows, depth)),
                pl.BlockSpec((1, depth, tile), lambda n, part: (0, 0, part[0] * steps + n)),
            ],
            out_specs=[pl.BlockSpec((capacity, tile), lambda n, part: (0, n))] * experts,
        ),
        cost_estimate=cost(2 * rows * depth * width, 2 * depth * width + 2 * rows * width),
        compiler_params=params(),
        name="down",
    )(part.reshape(1), hidden, down_w)


def combine_kernel(pick_ref, mix_ref, *refs):
    out = refs[-1]
    rows = out.shape[0]
    y = jnp.concatenate([r[...] for r in refs[:-1]], axis=0)
    picked = jnp.dot(pick_ref[...], y, preferred_element_type=F32)
    out[...] = (
        picked[:rows] * mix_ref[:, 0:1] + picked[rows:] * mix_ref[:, 1:2]
    ).astype(BF16)


def combine(pick, mixing, blocks):
    rows = mixing.shape[0]
    width = blocks[0].shape[1]
    return pl.pallas_call(
        combine_kernel,
        out_shape=jax.ShapeDtypeStruct((rows, width), BF16),
        in_specs=[pl.BlockSpec(memory_space=pltpu.VMEM)] * (2 + len(blocks)),
        out_specs=pl.BlockSpec(memory_space=pltpu.VMEM),
        cost_estimate=cost(4 * rows * pick.shape[1] * width, 6 * rows * width),
        compiler_params=params(),
        name="combine",
    )(pick, mixing, *blocks)


def swap(value, axis, distance):
    if distance == 0:
        return value
    count = lax.axis_size(axis)
    return lax.ppermute(value, axis, [(i, i ^ distance) for i in range(count)])


def per_device(tokens, expert_ids, route_logits, gate_weight, up_weight, down_weight):
    rows, own_width = tokens.shape
    experts = lax.axis_size("expert")
    shards = lax.axis_size("tensor")
    capacity = rows // 2
    me = lax.axis_index("expert").astype(jnp.int32)
    column = lax.axis_index("tensor").astype(jnp.int32)
    direct = shards <= 8
    distances = list(range(shards)) if direct else [0]
    width = own_width if direct else own_width * shards

    def part_of(distance):
        return lax.bitwise_xor(column, jnp.int32(distance)) if direct else jnp.int32(0)

    if direct:
        blocks = [swap(tokens, "tensor", d) for d in distances]
    else:
        blocks = [lax.all_gather(tokens, "tensor", axis=1, tiled=True)]
    placed = place(me, expert_ids, experts, capacity)

    sums = None
    for d in distances:
        outgoing = dispatch(placed, blocks[d], experts, capacity)
        arrived = [swap(block, "expert", e) for e, block in enumerate(outgoing)]
        sums = gate_up(part_of(d), arrived, gate_weight, up_weight, sums, d == distances[-1])
    hidden = sums

    names = expert_ids[:, :, None] == jnp.arange(experts, dtype=jnp.int32)[None, None, :]
    named = jnp.sum(names.astype(F32), axis=1)
    earlier = (jnp.arange(rows)[:, None] > jnp.arange(rows)[None, :]).astype(F32)
    before = jnp.dot(earlier, named).astype(jnp.int32)
    position = jnp.sum(jnp.where(names, before[:, None, :], 0), axis=2)
    slots = lax.bitwise_xor(expert_ids, me) * capacity + position
    pick = (
        slots.T[:, :, None] == jnp.arange(experts * capacity, dtype=jnp.int32)[None, None, :]
    ).astype(BF16).reshape(2 * rows, experts * capacity)
    share = jax.nn.sigmoid(route_logits[:, 0] - route_logits[:, 1])
    mixing = jnp.stack([share, 1.0 - share], axis=1)

    total = []
    for d in reversed(distances):
        terms = down(part_of(d), hidden, down_weight, width, experts)
        returned = [swap(block, "expert", e) for e, block in enumerate(terms)]
        mixed = combine(pick, mixing, returned)
        if not direct:
            return lax.psum_scatter(mixed, "tensor", scatter_dimension=1, tiled=True)
        total.append(swap(mixed, "tensor", d))
    out = total[0].astype(F32)
    for term in total[1:]:
        out = out + term.astype(F32)
    return out.astype(BF16)


def solution(mesh):
    in_specs = (
        P(("groups", "expert"), "tensor"),
        P(("groups", "expert"), None),
        P(("groups", "expert"), None),
        P("expert", None, "tensor"),
        P("expert", None, "tensor"),
        P("expert", "tensor", None),
    )
    out_specs = P(("groups", "expert"), "tensor")
    return jax.shard_map(
        per_device, mesh=mesh, in_specs=in_specs, out_specs=out_specs, check_vma=False
    )
```

```python
import functools

import jax
import jax.numpy as jnp
from jax import lax
from jax.experimental import pallas as pl
from jax.experimental.pallas import tpu as pltpu
from jax.sharding import PartitionSpec as P

F32 = jnp.float32
BF16 = jnp.bfloat16
MIB = 1024 * 1024


def params(mib=16):
    return pltpu.CompilerParams(vmem_limit_bytes=mib * MIB)


def cost(flops, moved):
    return pl.CostEstimate(flops=flops, bytes_accessed=moved, transcendentals=0)


def whole(shape):
    return pl.BlockSpec(shape, lambda *_: (0,) * len(shape))


def routing_kernel(me_ref, ids_ref, placed_ref, pick_ref, *, experts, capacity):
    rows = ids_ref.shape[1]
    relative = lax.bitwise_xor(ids_ref[...], me_ref[0])
    lane = lax.broadcasted_iota(jnp.int32, (experts, rows), 0)
    names = [lane == relative[k : k + 1] for k in range(2)]
    named = names[0] | names[1]
    earlier = lax.broadcasted_iota(jnp.int32, (rows, rows), 0) < lax.broadcasted_iota(
        jnp.int32, (rows, rows), 1
    )
    before = jnp.dot(
        jnp.where(named, 1.0, 0.0).astype(BF16),
        jnp.where(earlier, 1.0, 0.0).astype(BF16),
        preferred_element_type=F32,
    ).astype(jnp.int32)
    slot = lax.broadcasted_iota(jnp.int32, (capacity, rows), 0)
    for d in range(experts):
        here = slice(d * capacity, (d + 1) * capacity)
        both = None
        for k in range(2):
            position = jnp.where(names[k], before, -1)
            hit = jnp.where(position[d : d + 1] == slot, 1.0, 0.0)
            pick_ref[here, k * rows : (k + 1) * rows] = hit.astype(BF16)
            both = hit if k == 0 else both + hit
        placed_ref[here, :] = both.astype(BF16)


def place(me, expert_ids, experts, capacity):
    rows = expert_ids.shape[0]
    return pl.pallas_call(
        functools.partial(routing_kernel, experts=experts, capacity=capacity),
        out_shape=[
            jax.ShapeDtypeStruct((experts * capacity, rows), BF16),
            jax.ShapeDtypeStruct((experts * capacity, 2 * rows), BF16),
        ],
        in_specs=[
            pl.BlockSpec(memory_space=pltpu.SMEM),
            pl.BlockSpec(memory_space=pltpu.VMEM),
        ],
        out_specs=[pl.BlockSpec(memory_space=pltpu.VMEM)] * 2,
        compiler_params=params(),
        name="routing",
    )(me.reshape(1), expert_ids.T)


def dispatch_kernel(placed_ref, block_ref, *out_refs):
    capacity = out_refs[0].shape[0]
    for d, out in enumerate(out_refs):
        out[...] = jnp.dot(
            placed_ref[d * capacity : (d + 1) * capacity, :],
            block_ref[...],
            preferred_element_type=F32,
        ).astype(BF16)


def dispatch(placed, block, experts, capacity):
    rows, width = block.shape
    return pl.pallas_call(
        dispatch_kernel,
        out_shape=[jax.ShapeDtypeStruct((capacity, width), BF16)] * experts,
        in_specs=[pl.BlockSpec(memory_space=pltpu.VMEM)] * 2,
        out_specs=[pl.BlockSpec(memory_space=pltpu.VMEM)] * experts,
        cost_estimate=cost(2 * experts * capacity * rows * width, 4 * rows * width),
        compiler_params=params(),
        name="dispatch",
    )(placed, block)


def gate_up_kernel(*refs, experts, first, last):
    x_refs = refs[1 : 1 + experts]
    gate_w, up_w = refs[1 + experts : 3 + experts]
    rest = refs[3 + experts :]
    if not first:
        old_gate, old_up = rest[:2]
        rest = rest[2:]
    x = jnp.concatenate([r[...] for r in x_refs], axis=0)
    gate = jnp.dot(x, gate_w[0], preferred_element_type=F32)
    up = jnp.dot(x, up_w[0], preferred_element_type=F32)
    if not first:
        gate = gate + old_gate[...]
        up = up + old_up[...]
    if last:
        rest[0][...] = (gate / (1.0 + jnp.exp(-gate)) * up).astype(BF16)
    else:
        rest[0][...] = gate
        rest[1][...] = up


def gate_up(part, x_blocks, gate_w, up_w, sums, last):
    experts = len(x_blocks)
    capacity, width = x_blocks[0].shape
    rows = experts * capacity
    hidden = gate_w.shape[2]
    tile = min(512, hidden)
    first = sums is None
    weight = pl.BlockSpec((1, width, tile), lambda n, part: (0, part[0], n))
    column = pl.BlockSpec((rows, tile), lambda n, part: (0, n))
    if last:
        out_shape = jax.ShapeDtypeStruct((rows, hidden), BF16)
        out_specs = column
    else:
        out_shape = [jax.ShapeDtypeStruct((rows, hidden), F32)] * 2
        out_specs = [column] * 2
    return pl.pallas_call(
        functools.partial(gate_up_kernel, experts=experts, first=first, last=last),
        out_shape=out_shape,
        grid_spec=pltpu.PrefetchScalarGridSpec(
            num_scalar_prefetch=1,
            grid=(hidden // tile,),
            in_specs=[whole((capacity, width))] * experts
            + [weight] * 2
            + ([] if first else [column] * 2),
            out_specs=out_specs,
        ),
        cost_estimate=cost(4 * rows * width * hidden, 4 * width * hidden + 16 * rows * hidden),
        compiler_params=params(53),
        name="gate_up",
    )(part.reshape(1), *x_blocks, gate_w, up_w, *(() if first else sums))


def down_kernel(part_ref, h_ref, w_ref, *out_refs):
    capacity = out_refs[0].shape[0]
    y = jnp.dot(h_ref[...], w_ref[0], preferred_element_type=F32).astype(BF16)
    for d, out in enumerate(out_refs):
        out[...] = y[d * capacity : (d + 1) * capacity]


def down(part, hidden, down_w, width, experts):
    rows, depth = hidden.shape
    capacity = rows // experts
    tile = min(256, width)
    steps = width // tile
    return pl.pallas_call(
        down_kernel,
        out_shape=[jax.ShapeDtypeStruct((capacity, width), BF16)] * experts,
        grid_spec=pltpu.PrefetchScalarGridSpec(
            num_scalar_prefetch=1,
            grid=(steps,),
            in_specs=[
                whole((rows, depth)),
                pl.BlockSpec((1, depth, tile), lambda n, part: (0, 0, part[0] * steps + n)),
            ],
            out_specs=[pl.BlockSpec((capacity, tile), lambda n, part: (0, n))] * experts,
        ),
        cost_estimate=cost(2 * rows * depth * width, 2 * depth * width + 2 * rows * width),
        compiler_params=params(53),
        name="down",
    )(part.reshape(1), hidden, down_w)


def combine_kernel(pick_ref, logits_ref, *refs):
    out = refs[-1]
    rows = out.shape[0]
    y = jnp.concatenate([r[...] for r in refs[:-1]], axis=0)
    picked = lax.dot_general(
        pick_ref[...], y, (((0,), (0,)), ((), ())), preferred_element_type=F32
    )
    share = 1.0 / (1.0 + jnp.exp(logits_ref[:, 1:2] - logits_ref[:, 0:1]))
    out[...] = (picked[:rows] * share + picked[rows:] * (1.0 - share)).astype(BF16)


def combine(pick, logits, blocks):
    rows = logits.shape[0]
    width = blocks[0].shape[1]
    return pl.pallas_call(
        combine_kernel,
        out_shape=jax.ShapeDtypeStruct((rows, width), BF16),
        in_specs=[pl.BlockSpec(memory_space=pltpu.VMEM)] * (2 + len(blocks)),
        out_specs=pl.BlockSpec(memory_space=pltpu.VMEM),
        cost_estimate=cost(4 * rows * pick.shape[0] * width, 6 * rows * width),
        compiler_params=params(),
        name="combine",
    )(pick, logits, *blocks)


def swap(value, axis, distance):
    if distance == 0:
        return value
    count = lax.axis_size(axis)
    return lax.ppermute(value, axis, [(i, i ^ distance) for i in range(count)])


def per_device(tokens, expert_ids, route_logits, gate_weight, up_weight, down_weight):
    rows, own_width = tokens.shape
    experts = lax.axis_size("expert")
    shards = lax.axis_size("tensor")
    capacity = rows // 2
    me = lax.axis_index("expert").astype(jnp.int32)
    column = lax.axis_index("tensor").astype(jnp.int32)
    direct = shards <= 8
    distances = list(range(shards)) if direct else [0]
    width = own_width if direct else own_width * shards

    def part_of(distance):
        return lax.bitwise_xor(column, jnp.int32(distance)) if direct else jnp.int32(0)

    if direct:
        blocks = [swap(tokens, "tensor", d) for d in distances]
    else:
        blocks = [lax.all_gather(tokens, "tensor", axis=1, tiled=True)]
    placed, pick = place(me, expert_ids, experts, capacity)

    sums = None
    for d in distances:
        outgoing = dispatch(placed, blocks[d], experts, capacity)
        arrived = [swap(block, "expert", e) for e, block in enumerate(outgoing)]
        sums = gate_up(part_of(d), arrived, gate_weight, up_weight, sums, d == distances[-1])
    hidden = sums

    total = []
    for d in reversed(distances):
        terms = down(part_of(d), hidden, down_weight, width, experts)
        returned = [swap(block, "expert", e) for e, block in enumerate(terms)]
        mixed = combine(pick, route_logits, returned)
        if not direct:
            return lax.psum_scatter(mixed, "tensor", scatter_dimension=1, tiled=True)
        total.append(swap(mixed, "tensor", d))
    out = total[0].astype(F32)
    for term in total[1:]:
        out = out + term.astype(F32)
    return out.astype(BF16)


def solution(mesh):
    in_specs = (
        P(("groups", "expert"), "tensor"),
        P(("groups", "expert"), None),
        P(("groups", "expert"), None),
        P("expert", None, "tensor"),
        P("expert", None, "tensor"),
        P("expert", "tensor", None),
    )
    out_specs = P(("groups", "expert"), "tensor")
    return jax.shard_map(
        per_device, mesh=mesh, in_specs=in_specs, out_specs=out_specs, check_vma=False
    )
```

```python
import functools

import jax
import jax.numpy as jnp
from jax import lax
from jax.experimental import pallas as pl
from jax.experimental.pallas import tpu as pltpu
from jax.sharding import PartitionSpec as P

F32 = jnp.float32
BF16 = jnp.bfloat16
MIB = 1024 * 1024


def params(mib=6):
    return pltpu.CompilerParams(vmem_limit_bytes=mib * MIB)


def cost(flops, moved):
    return pl.CostEstimate(flops=flops, bytes_accessed=moved, transcendentals=0)


def routing_kernel(me_ref, ids_ref, placed_ref, pick_ref, *, experts, capacity):
    rows = ids_ref.shape[1]
    relative = lax.bitwise_xor(ids_ref[...], me_ref[0])
    lane = lax.broadcasted_iota(jnp.int32, (experts, rows), 0)
    names = [lane == relative[k : k + 1] for k in range(2)]
    named = names[0] | names[1]
    earlier = lax.broadcasted_iota(jnp.int32, (rows, rows), 0) < lax.broadcasted_iota(
        jnp.int32, (rows, rows), 1
    )
    before = jnp.dot(
        jnp.where(named, 1.0, 0.0).astype(BF16),
        jnp.where(earlier, 1.0, 0.0).astype(BF16),
        preferred_element_type=F32,
    ).astype(jnp.int32)
    slot = lax.broadcasted_iota(jnp.int32, (capacity, rows), 0)
    for d in range(experts):
        here = slice(d * capacity, (d + 1) * capacity)
        both = None
        for k in range(2):
            position = jnp.where(names[k], before, -1)
            hit = jnp.where(position[d : d + 1] == slot, 1.0, 0.0)
            pick_ref[here, k * rows : (k + 1) * rows] = hit.astype(BF16)
            both = hit if k == 0 else both + hit
        placed_ref[here, :] = both.astype(BF16)


def place(me, expert_ids, experts, capacity):
    rows = expert_ids.shape[0]
    return pl.pallas_call(
        functools.partial(routing_kernel, experts=experts, capacity=capacity),
        out_shape=[
            jax.ShapeDtypeStruct((experts * capacity, rows), BF16),
            jax.ShapeDtypeStruct((experts * capacity, 2 * rows), BF16),
        ],
        in_specs=[
            pl.BlockSpec(memory_space=pltpu.SMEM),
            pl.BlockSpec(memory_space=pltpu.VMEM),
        ],
        out_specs=[pl.BlockSpec(memory_space=pltpu.VMEM)] * 2,
        compiler_params=params(),
        name="routing",
    )(me.reshape(1), expert_ids.T)


def dispatch_kernel(placed_ref, block_ref, *out_refs):
    capacity = out_refs[0].shape[0]
    for d, out in enumerate(out_refs):
        out[...] = jnp.dot(
            placed_ref[d * capacity : (d + 1) * capacity, :],
            block_ref[...],
            preferred_element_type=F32,
        ).astype(BF16)


def dispatch(placed, block, experts, capacity):
    rows, width = block.shape
    return pl.pallas_call(
        dispatch_kernel,
        out_shape=[jax.ShapeDtypeStruct((capacity, width), BF16)] * experts,
        in_specs=[pl.BlockSpec(memory_space=pltpu.VMEM)] * 2,
        out_specs=[pl.BlockSpec(memory_space=pltpu.VMEM)] * experts,
        cost_estimate=cost(2 * experts * capacity * rows * width, 4 * rows * width),
        compiler_params=params(),
        name="dispatch",
    )(placed, block)


def fetch_copies(parts_ref, sources, targets, sems):
    copies = []
    for i, (source, target) in enumerate(zip(sources, targets)):
        count = target.shape[0]
        start = pl.multiple_of(parts_ref[i] * count, count)
        copies.append(
            pltpu.make_async_copy(source.at[0, pl.ds(start, count)], target, sems.at[i])
        )
    return copies


def prefetch_kernel(parts_ref, after_ref, *refs):
    half = len(refs) // 2
    copies = fetch_copies(parts_ref, refs[:half], refs[half:-1], refs[-1])
    for copy in copies:
        copy.start()
    for copy in copies:
        copy.wait()


def fetch_specs(fetches):
    sources = [pltpu.with_memory_space_constraint(w, pltpu.HBM) for w, _, _ in fetches]
    parts = jnp.stack([jnp.asarray(part, jnp.int32) for _, part, _ in fetches] + [jnp.int32(0)])
    shapes = [pltpu.VMEM((count, w.shape[2]), w.dtype) for w, _, count in fetches]
    return parts, sources, shapes


def prefetch(fetches, after):
    parts, sources, shapes = fetch_specs(fetches)
    return pl.pallas_call(
        prefetch_kernel,
        out_shape=shapes,
        in_specs=[pl.BlockSpec(memory_space=pltpu.SMEM)]
        + [pl.BlockSpec(memory_space=pl.ANY)] * (1 + len(sources)),
        out_specs=[pl.BlockSpec(memory_space=pltpu.VMEM)] * len(shapes),
        scratch_shapes=[pltpu.SemaphoreType.DMA((len(shapes),))],
        cost_estimate=cost(0, sum(2 * count * w.shape[2] for w, _, count in fetches)),
        compiler_params=params(),
        name="prefetch",
    )(parts, after, *sources)


def gate_up_kernel(*refs, experts, first, last, fetched):
    parts_ref = refs[0]
    x_refs = refs[1 : 1 + experts]
    gate_w, up_w = refs[1 + experts : 3 + experts]
    rest = list(refs[3 + experts :])
    if not first:
        old_gate, old_up = rest[:2]
        rest = rest[2:]
    copies = []
    if fetched:
        sources, rest = rest[:fetched], rest[fetched:]
        copies = fetch_copies(parts_ref, sources, rest[-1 - fetched : -1], rest[-1])
    for copy in copies:
        copy.start()
    x = jnp.concatenate([r[...] for r in x_refs], axis=0)
    hidden = gate_w.shape[1]
    tile = min(512, hidden)
    for n in range(hidden // tile):
        columns = slice(n * tile, (n + 1) * tile)
        gate = jnp.dot(x, gate_w[:, columns], preferred_element_type=F32)
        up = jnp.dot(x, up_w[:, columns], preferred_element_type=F32)
        if not first:
            gate = gate + old_gate[:, columns]
            up = up + old_up[:, columns]
        if last:
            rest[0][:, columns] = (gate / (1.0 + jnp.exp(-gate)) * up).astype(BF16)
        else:
            rest[0][:, columns] = gate
            rest[1][:, columns] = up
    for copy in copies:
        copy.wait()


def gate_up(x_blocks, gate_w, up_w, sums, last, fetches):
    experts = len(x_blocks)
    capacity, width = x_blocks[0].shape
    rows = experts * capacity
    hidden = gate_w.shape[1]
    first = sums is None
    parts, sources, shapes = fetch_specs(fetches)
    operands = 2 + experts + (0 if first else 2)
    if last:
        out_shape = [pltpu.VMEM((rows, hidden), BF16)]
    else:
        out_shape = [pltpu.VMEM((rows, hidden), F32)] * 2
    results = pl.pallas_call(
        functools.partial(
            gate_up_kernel, experts=experts, first=first, last=last, fetched=len(fetches)
        ),
        out_shape=out_shape + shapes,
        in_specs=[pl.BlockSpec(memory_space=pltpu.SMEM)]
        + [pl.BlockSpec(memory_space=pltpu.VMEM)] * operands
        + [pl.BlockSpec(memory_space=pl.ANY)] * len(sources),
        out_specs=[pl.BlockSpec(memory_space=pltpu.VMEM)] * len(out_shape + shapes),
        scratch_shapes=[pltpu.SemaphoreType.DMA((len(fetches),))] if fetches else [],
        input_output_aliases={} if first or last else {3 + experts: 0, 4 + experts: 1},
        cost_estimate=cost(4 * rows * width * hidden, 4 * width * hidden),
        compiler_params=params(),
        name="gate_up",
    )(parts, *x_blocks, gate_w, up_w, *(() if first else sums), *sources)
    return results[: len(out_shape)], results[len(out_shape) :]


def down_kernel(part_ref, h_ref, w_ref, *out_refs):
    capacity, width = out_refs[0].shape
    tile = min(256, width)
    for n in range(width // tile):
        start = pl.multiple_of(part_ref[0] * width + n * tile, tile)
        y = jnp.dot(h_ref[...], w_ref[:, pl.ds(start, tile)], preferred_element_type=F32)
        for d, out in enumerate(out_refs):
            out[:, n * tile : (n + 1) * tile] = y[d * capacity : (d + 1) * capacity].astype(BF16)


def down(part, hidden, down_w, width, experts):
    rows, depth = hidden.shape
    capacity = rows // experts
    return pl.pallas_call(
        down_kernel,
        out_shape=[jax.ShapeDtypeStruct((capacity, width), BF16)] * experts,
        in_specs=[pl.BlockSpec(memory_space=pltpu.SMEM)]
        + [pl.BlockSpec(memory_space=pltpu.VMEM)] * 2,
        out_specs=[pl.BlockSpec(memory_space=pltpu.VMEM)] * experts,
        cost_estimate=cost(2 * rows * depth * width, 2 * depth * width + 2 * rows * width),
        compiler_params=params(),
        name="down",
    )(part.reshape(1), hidden, down_w)


def combine_kernel(pick_ref, logits_ref, *refs):
    out = refs[-1]
    rows = out.shape[0]
    y = jnp.concatenate([r[...] for r in refs[:-1]], axis=0)
    picked = lax.dot_general(
        pick_ref[...], y, (((0,), (0,)), ((), ())), preferred_element_type=F32
    )
    share = 1.0 / (1.0 + jnp.exp(logits_ref[:, 1:2] - logits_ref[:, 0:1]))
    out[...] = (picked[:rows] * share + picked[rows:] * (1.0 - share)).astype(BF16)


def combine(pick, logits, blocks):
    rows = logits.shape[0]
    width = blocks[0].shape[1]
    return pl.pallas_call(
        combine_kernel,
        out_shape=jax.ShapeDtypeStruct((rows, width), BF16),
        in_specs=[pl.BlockSpec(memory_space=pltpu.VMEM)] * (2 + len(blocks)),
        out_specs=pl.BlockSpec(memory_space=pltpu.VMEM),
        cost_estimate=cost(4 * rows * pick.shape[0] * width, 6 * rows * width),
        compiler_params=params(),
        name="combine",
    )(pick, logits, *blocks)


def swap(value, axis, distance):
    if distance == 0:
        return value
    count = lax.axis_size(axis)
    return lax.ppermute(value, axis, [(i, i ^ distance) for i in range(count)])


def per_device(tokens, expert_ids, route_logits, gate_weight, up_weight, down_weight):
    rows, own_width = tokens.shape
    experts = lax.axis_size("expert")
    shards = lax.axis_size("tensor")
    capacity = rows // 2
    me = lax.axis_index("expert").astype(jnp.int32)
    column = lax.axis_index("tensor").astype(jnp.int32)
    direct = shards <= 8
    distances = list(range(shards)) if direct else [0]
    width = own_width if direct else own_width * shards

    def part_of(distance):
        return lax.bitwise_xor(column, jnp.int32(distance)) if direct else jnp.int32(0)

    if direct:
        blocks = [swap(tokens, "tensor", d) for d in distances]
    else:
        blocks = [lax.all_gather(tokens, "tensor", axis=1, tiled=True)]
    placed, pick = place(me, expert_ids, experts, capacity)

    arrived = []
    for d in distances:
        outgoing = dispatch(placed, blocks[d], experts, capacity)
        arrived.append([swap(block, "expert", e) for e, block in enumerate(outgoing)])
        if d == 0:
            started = outgoing[0]

    def slices(chosen):
        return [(w, part_of(d), width) for d in chosen for w in (gate_weight, up_weight)]

    weights = list(prefetch(slices(distances[:2]), started))
    sums = None
    for d in distances:
        fetches = slices(distances[2:]) if d == 0 else []
        with_down = d == min(1, distances[-1])
        if with_down:
            fetches = fetches + [(down_weight, 0, down_weight.shape[1])]
        sums, fetched = gate_up(
            arrived[d], *weights[2 * d : 2 * d + 2], sums, d == distances[-1], fetches
        )
        if with_down:
            down_w = fetched[-1]
            fetched = fetched[:-1]
        weights.extend(fetched)
    hidden = sums[0]

    total = []
    for d in reversed(distances):
        terms = down(part_of(d), hidden, down_w, width, experts)
        returned = [swap(block, "expert", e) for e, block in enumerate(terms)]
        mixed = combine(pick, route_logits, returned)
        if not direct:
            return lax.psum_scatter(mixed, "tensor", scatter_dimension=1, tiled=True)
        total.append(swap(mixed, "tensor", d))
    out = total[0].astype(F32)
    for term in total[1:]:
        out = out + term.astype(F32)
    return out.astype(BF16)


def solution(mesh):
    in_specs = (
        P(("groups", "expert"), "tensor"),
        P(("groups", "expert"), None),
        P(("groups", "expert"), None),
        P("expert", None, "tensor"),
        P("expert", None, "tensor"),
        P("expert", "tensor", None),
    )
    out_specs = P(("groups", "expert"), "tensor")
    return jax.shard_map(
        per_device, mesh=mesh, in_specs=in_specs, out_specs=out_specs, check_vma=False
    )
```

```python
import functools

import jax
import jax.numpy as jnp
from jax import lax
from jax.experimental import pallas as pl
from jax.experimental.pallas import tpu as pltpu
from jax.sharding import PartitionSpec as P

F32 = jnp.float32
BF16 = jnp.bfloat16
MIB = 1024 * 1024


def params(mib=6):
    return pltpu.CompilerParams(vmem_limit_bytes=mib * MIB)


def cost(flops, moved):
    return pl.CostEstimate(flops=flops, bytes_accessed=moved, transcendentals=0)


def pinned(arrays):
    return [pltpu.with_memory_space_constraint(array, pltpu.VMEM) for array in arrays]


def routing_kernel(me_ref, ids_ref, placed_ref, pick_ref, *, experts, capacity):
    rows = ids_ref.shape[1]
    relative = lax.bitwise_xor(ids_ref[...], me_ref[0])
    lane = lax.broadcasted_iota(jnp.int32, (experts, rows), 0)
    names = [lane == relative[k : k + 1] for k in range(2)]
    named = names[0] | names[1]
    earlier = lax.broadcasted_iota(jnp.int32, (rows, rows), 0) < lax.broadcasted_iota(
        jnp.int32, (rows, rows), 1
    )
    before = jnp.dot(
        jnp.where(named, 1.0, 0.0).astype(BF16),
        jnp.where(earlier, 1.0, 0.0).astype(BF16),
        preferred_element_type=F32,
    ).astype(jnp.int32)
    slot = lax.broadcasted_iota(jnp.int32, (capacity, rows), 0)
    for d in range(experts):
        here = slice(d * capacity, (d + 1) * capacity)
        both = None
        for k in range(2):
            position = jnp.where(names[k], before, -1)
            hit = jnp.where(position[d : d + 1] == slot, 1.0, 0.0)
            pick_ref[here, k * rows : (k + 1) * rows] = hit.astype(BF16)
            both = hit if k == 0 else both + hit
        placed_ref[here, :] = both.astype(BF16)


def place(me, expert_ids, experts, capacity):
    rows = expert_ids.shape[0]
    return pl.pallas_call(
        functools.partial(routing_kernel, experts=experts, capacity=capacity),
        out_shape=[
            jax.ShapeDtypeStruct((experts * capacity, rows), BF16),
            jax.ShapeDtypeStruct((experts * capacity, 2 * rows), BF16),
        ],
        in_specs=[
            pl.BlockSpec(memory_space=pltpu.SMEM),
            pl.BlockSpec(memory_space=pltpu.VMEM),
        ],
        out_specs=[pl.BlockSpec(memory_space=pltpu.VMEM)] * 2,
        compiler_params=params(),
        name="routing",
    )(me.reshape(1), expert_ids.T)


def dispatch_kernel(placed_ref, *refs, count, waits):
    refs = refs[:count] + refs[count + waits :]
    capacity, wide = refs[count].shape
    width = wide // count
    for i in range(count):
        block = refs[i][...]
        for d, out in enumerate(refs[count:]):
            out[:, i * width : (i + 1) * width] = jnp.dot(
                placed_ref[d * capacity : (d + 1) * capacity, :],
                block,
                preferred_element_type=F32,
            ).astype(BF16)


def dispatch(placed, blocks, experts, capacity, after):
    rows, width = blocks[0].shape
    wide = width * len(blocks)
    return pl.pallas_call(
        functools.partial(dispatch_kernel, count=len(blocks), waits=len(after)),
        out_shape=[jax.ShapeDtypeStruct((capacity, wide), BF16)] * experts,
        in_specs=[pl.BlockSpec(memory_space=pltpu.VMEM)] * (1 + len(blocks))
        + [pl.BlockSpec(memory_space=pltpu.VMEM)] * len(after),
        out_specs=[pl.BlockSpec(memory_space=pltpu.VMEM)] * experts,
        cost_estimate=cost(2 * experts * capacity * rows * wide, 6 * rows * wide),
        compiler_params=params(),
        name="dispatch",
    )(placed, *blocks, *pinned(after))


def fetch_copies(parts_ref, sources, targets, sems):
    copies = []
    for i, (source, target) in enumerate(zip(sources, targets)):
        count = target.shape[0]
        start = pl.multiple_of(parts_ref[i] * count, count)
        copies.append(
            pltpu.make_async_copy(source.at[0, pl.ds(start, count)], target, sems.at[i])
        )
    return copies


def prefetch_kernel(parts_ref, after_ref, *refs):
    half = len(refs) // 2
    copies = fetch_copies(parts_ref, refs[:half], refs[half:-1], refs[-1])
    for copy in copies:
        copy.start()
    for copy in copies:
        copy.wait()


def fetch_specs(fetches):
    sources = [pltpu.with_memory_space_constraint(w, pltpu.HBM) for w, _, _ in fetches]
    parts = jnp.stack([jnp.asarray(part, jnp.int32) for _, part, _ in fetches] + [jnp.int32(0)])
    shapes = [pltpu.VMEM((count, w.shape[2]), w.dtype) for w, _, count in fetches]
    return parts, sources, shapes


def prefetch(fetches, after):
    parts, sources, shapes = fetch_specs(fetches)
    return pl.pallas_call(
        prefetch_kernel,
        out_shape=shapes,
        in_specs=[pl.BlockSpec(memory_space=pltpu.SMEM)]
        + [pl.BlockSpec(memory_space=pl.ANY)] * (1 + len(sources)),
        out_specs=[pl.BlockSpec(memory_space=pltpu.VMEM)] * len(shapes),
        scratch_shapes=[pltpu.SemaphoreType.DMA((len(shapes),))],
        cost_estimate=cost(0, sum(2 * count * w.shape[2] for w, _, count in fetches)),
        compiler_params=params(),
        name="prefetch",
    )(parts, after, *sources)


def gate_up_kernel(*refs, experts, slices, first, last, fetched):
    parts_ref = refs[0]
    x_refs = refs[1 : 1 + experts]
    weights = refs[1 + experts : 1 + experts + 2 * slices]
    rest = list(refs[1 + experts + 2 * slices :])
    if not first:
        old_gate, old_up = rest[:2]
        rest = rest[2:]
    copies = []
    if fetched:
        sources, rest = rest[:fetched], rest[fetched:]
        copies = fetch_copies(parts_ref, sources, rest[-1 - fetched : -1], rest[-1])
    for copy in copies:
        copy.start()
    x = jnp.concatenate([r[...] for r in x_refs], axis=0)
    width, hidden = weights[0].shape
    tile = min(512, hidden)
    for n in range(hidden // tile):
        columns = slice(n * tile, (n + 1) * tile)
        sums = []
        for kind in range(2):
            total = None if first else (old_gate, old_up)[kind][:, columns]
            for i in range(slices):
                term = jnp.dot(
                    x[:, i * width : (i + 1) * width],
                    weights[2 * i + kind][:, columns],
                    preferred_element_type=F32,
                )
                total = term if total is None else total + term
            sums.append(total)
        gate, up = sums
        if last:
            rest[0][:, columns] = (gate / (1.0 + jnp.exp(-gate)) * up).astype(BF16)
        else:
            rest[0][:, columns] = gate
            rest[1][:, columns] = up
    for copy in copies:
        copy.wait()


def gate_up(x_blocks, weights, sums, last, fetches):
    experts = len(x_blocks)
    rows = experts * x_blocks[0].shape[0]
    hidden = weights[0].shape[1]
    slices = len(weights) // 2
    first = sums is None
    parts, sources, shapes = fetch_specs(fetches)
    old = [] if first else pinned(sums)
    before = 1 + experts + len(weights)
    if last:
        out_shape = [pltpu.VMEM((rows, hidden), BF16)]
    else:
        out_shape = [pltpu.VMEM((rows, hidden), F32)] * 2
    results = pl.pallas_call(
        functools.partial(
            gate_up_kernel,
            experts=experts,
            slices=slices,
            first=first,
            last=last,
            fetched=len(fetches),
        ),
        out_shape=out_shape + shapes,
        in_specs=[pl.BlockSpec(memory_space=pltpu.SMEM)]
        + [pl.BlockSpec(memory_space=pltpu.VMEM)] * (before - 1 + len(old))
        + [pl.BlockSpec(memory_space=pl.ANY)] * len(sources),
        out_specs=[pl.BlockSpec(memory_space=pltpu.VMEM)] * len(out_shape + shapes),
        scratch_shapes=[pltpu.SemaphoreType.DMA((len(fetches),))] if fetches else [],
        input_output_aliases={} if first or last else {before: 0, before + 1: 1},
        cost_estimate=cost(
            2 * rows * hidden * sum(w.shape[0] for w in weights),
            sum(2 * w.size for w in weights),
        ),
        compiler_params=params(),
        name="gate_up",
    )(parts, *x_blocks, *pinned(weights), *old, *sources)
    return results[: len(out_shape)], results[len(out_shape) :]


def down_kernel(parts_ref, h_ref, w_ref, *refs, slices, waits):
    out_refs = refs[waits:]
    capacity, wide = out_refs[0].shape
    width = wide // slices
    tile = min(256, width)
    for i in range(slices):
        for n in range(width // tile):
            start = pl.multiple_of(parts_ref[i] * width + n * tile, tile)
            y = jnp.dot(h_ref[...], w_ref[:, pl.ds(start, tile)], preferred_element_type=F32)
            columns = pl.ds(i * width + n * tile, tile)
            for d, out in enumerate(out_refs):
                out[:, columns] = y[d * capacity : (d + 1) * capacity].astype(BF16)


def down(parts, hidden, down_w, width, experts, after):
    rows, depth = hidden.shape
    capacity = rows // experts
    wide = width * len(parts)
    return pl.pallas_call(
        functools.partial(down_kernel, slices=len(parts), waits=len(after)),
        out_shape=[jax.ShapeDtypeStruct((capacity, wide), BF16)] * experts,
        in_specs=[pl.BlockSpec(memory_space=pltpu.SMEM)]
        + [pl.BlockSpec(memory_space=pltpu.VMEM)] * 2
        + [pl.BlockSpec(memory_space=pl.ANY)] * len(after),
        out_specs=[pl.BlockSpec(memory_space=pltpu.VMEM)] * experts,
        cost_estimate=cost(2 * rows * depth * wide, 2 * depth * wide + 2 * rows * wide),
        compiler_params=params(),
        name="down",
    )(jnp.stack(parts), *pinned([hidden, down_w]), *after)


def combine_kernel(pick_ref, logits_ref, *refs, experts):
    y_refs, out_refs = refs[:experts], refs[experts:]
    rows, width = out_refs[0].shape
    y = jnp.concatenate([r[...] for r in y_refs], axis=0)
    picked = lax.dot_general(
        pick_ref[...], y, (((0,), (0,)), ((), ())), preferred_element_type=F32
    )
    share = 1.0 / (1.0 + jnp.exp(logits_ref[:, 1:2] - logits_ref[:, 0:1]))
    mixed = (picked[:rows] * share + picked[rows:] * (1.0 - share)).astype(BF16)
    for i, out in enumerate(out_refs):
        out[...] = mixed[:, i * width : (i + 1) * width]


def combine(pick, logits, blocks, slices):
    rows = logits.shape[0]
    wide = blocks[0].shape[1]
    return pl.pallas_call(
        functools.partial(combine_kernel, experts=len(blocks)),
        out_shape=[jax.ShapeDtypeStruct((rows, wide // slices), BF16)] * slices,
        in_specs=[pl.BlockSpec(memory_space=pltpu.VMEM)] * (2 + len(blocks)),
        out_specs=[pl.BlockSpec(memory_space=pltpu.VMEM)] * slices,
        cost_estimate=cost(4 * rows * pick.shape[0] * wide, 6 * rows * wide),
        compiler_params=params(),
        name="combine",
    )(pick, logits, *blocks)


def swap(value, axis, distance):
    if distance == 0:
        return value
    count = lax.axis_size(axis)
    return lax.ppermute(value, axis, [(i, i ^ distance) for i in range(count)])


def per_device(tokens, expert_ids, route_logits, gate_weight, up_weight, down_weight):
    rows, own_width = tokens.shape
    experts = lax.axis_size("expert")
    shards = lax.axis_size("tensor")
    capacity = rows // 2
    me = lax.axis_index("expert").astype(jnp.int32)
    column = lax.axis_index("tensor").astype(jnp.int32)
    direct = shards <= 8
    distances = list(range(shards)) if direct else [0]
    width = own_width if direct else own_width * shards

    def part_of(distance):
        return lax.bitwise_xor(column, jnp.int32(distance)) if direct else jnp.int32(0)

    if direct:
        blocks = [swap(tokens, "tensor", d) for d in distances]
    else:
        blocks = [lax.all_gather(tokens, "tensor", axis=1, tiled=True)]
    placed, pick = place(me, expert_ids, experts, capacity)

    fetches = [(w, part_of(d), width) for d in distances for w in (gate_weight, up_weight)]
    fetches.append((down_weight, 0, down_weight.shape[1]))
    early = min(6, len(fetches) - 1)
    groups = [distances[i : i + 2] for i in range(0, len(distances), 2)]
    arrived, weights = [], []
    for group in groups:
        block = [blocks[d] for d in group]
        outgoing = dispatch(placed, block, experts, capacity, weights[:1])
        arrived.append([swap(block, "expert", e) for e, block in enumerate(outgoing)])
        if not weights:
            weights = list(prefetch(fetches[:early], outgoing[0]))
    sums = None
    for group, x_blocks in zip(groups, arrived):
        chosen = weights[2 * group[0] : 2 * group[-1] + 2]
        later = fetches[early:] if group is groups[0] else []
        sums, fetched = gate_up(x_blocks, chosen, sums, group is groups[-1], later)
        weights.extend(fetched)
    hidden, down_w = sums[0], weights[-1]

    groups = [[d] for d in reversed(distances)]
    total = []
    for group in groups:
        after = total[:1] if group is groups[-1] else []
        terms = down([part_of(d) for d in group], hidden, down_w, width, experts, after)
        returned = [swap(block, "expert", e) for e, block in enumerate(terms)]
        mixtures = combine(pick, route_logits, returned, len(group))
        if not direct:
            return lax.psum_scatter(mixtures[0], "tensor", scatter_dimension=1, tiled=True)
        total.extend(swap(mixed, "tensor", d) for d, mixed in zip(group, mixtures))
    out = total[0].astype(F32)
    for term in total[1:]:
        out = out + term.astype(F32)
    return out.astype(BF16)


def solution(mesh):
    in_specs = (
        P(("groups", "expert"), "tensor"),
        P(("groups", "expert"), None),
        P(("groups", "expert"), None),
        P("expert", None, "tensor"),
        P("expert", None, "tensor"),
        P("expert", "tensor", None),
    )
    out_specs = P(("groups", "expert"), "tensor")
    return jax.shard_map(
        per_device, mesh=mesh, in_specs=in_specs, out_specs=out_specs, check_vma=False
    )
```

```python
import functools

import jax
import jax.numpy as jnp
from jax import lax
from jax.experimental import pallas as pl
from jax.experimental.pallas import tpu as pltpu
from jax.sharding import PartitionSpec as P

F32 = jnp.float32
BF16 = jnp.bfloat16
MIB = 1024 * 1024


def params(mib=6):
    return pltpu.CompilerParams(vmem_limit_bytes=mib * MIB)


def cost(flops, moved):
    return pl.CostEstimate(flops=flops, bytes_accessed=moved, transcendentals=0)


def pinned(arrays):
    return [pltpu.with_memory_space_constraint(array, pltpu.VMEM) for array in arrays]


def routing_kernel(me_ref, ids_ref, placed_ref, pick_ref, *, experts, capacity):
    rows = ids_ref.shape[1]
    relative = lax.bitwise_xor(ids_ref[...], me_ref[0])
    lane = lax.broadcasted_iota(jnp.int32, (experts, rows), 0)
    names = [lane == relative[k : k + 1] for k in range(2)]
    named = names[0] | names[1]
    earlier = lax.broadcasted_iota(jnp.int32, (rows, rows), 0) < lax.broadcasted_iota(
        jnp.int32, (rows, rows), 1
    )
    before = jnp.dot(
        jnp.where(named, 1.0, 0.0).astype(BF16),
        jnp.where(earlier, 1.0, 0.0).astype(BF16),
        preferred_element_type=F32,
    ).astype(jnp.int32)
    slot = lax.broadcasted_iota(jnp.int32, (capacity, rows), 0)
    for d in range(experts):
        here = slice(d * capacity, (d + 1) * capacity)
        both = None
        for k in range(2):
            position = jnp.where(names[k], before, -1)
            hit = jnp.where(position[d : d + 1] == slot, 1.0, 0.0)
            pick_ref[here, k * rows : (k + 1) * rows] = hit.astype(BF16)
            both = hit if k == 0 else both + hit
        placed_ref[here, :] = both.astype(BF16)


def place(me, expert_ids, experts, capacity):
    rows = expert_ids.shape[0]
    return pl.pallas_call(
        functools.partial(routing_kernel, experts=experts, capacity=capacity),
        out_shape=[
            jax.ShapeDtypeStruct((experts * capacity, rows), BF16),
            jax.ShapeDtypeStruct((experts * capacity, 2 * rows), BF16),
        ],
        in_specs=[
            pl.BlockSpec(memory_space=pltpu.SMEM),
            pl.BlockSpec(memory_space=pltpu.VMEM),
        ],
        out_specs=[pl.BlockSpec(memory_space=pltpu.VMEM)] * 2,
        compiler_params=params(),
        name="routing",
    )(me.reshape(1), expert_ids.T)


def dispatch_kernel(placed_ref, *refs, count, waits):
    refs = refs[:count] + refs[count + waits :]
    capacity, wide = refs[count].shape
    width = wide // count
    for i in range(count):
        block = refs[i][...]
        for d, out in enumerate(refs[count:]):
            out[:, i * width : (i + 1) * width] = jnp.dot(
                placed_ref[d * capacity : (d + 1) * capacity, :],
                block,
                preferred_element_type=F32,
            ).astype(BF16)


def dispatch(placed, blocks, experts, capacity, after):
    rows, width = blocks[0].shape
    wide = width * len(blocks)
    return pl.pallas_call(
        functools.partial(dispatch_kernel, count=len(blocks), waits=len(after)),
        out_shape=[jax.ShapeDtypeStruct((capacity, wide), BF16)] * experts,
        in_specs=[pl.BlockSpec(memory_space=pltpu.VMEM)] * (1 + len(blocks))
        + [pl.BlockSpec(memory_space=pltpu.VMEM)] * len(after),
        out_specs=[pl.BlockSpec(memory_space=pltpu.VMEM)] * experts,
        cost_estimate=cost(2 * experts * capacity * rows * wide, 6 * rows * wide),
        compiler_params=params(),
        name="dispatch",
    )(placed, *blocks, *pinned(after))


def fetch_copies(parts_ref, sources, targets, sems):
    copies = []
    for i, (source, target) in enumerate(zip(sources, targets)):
        count = target.shape[0]
        start = pl.multiple_of(parts_ref[i] * count, count)
        copies.append(
            pltpu.make_async_copy(source.at[0, pl.ds(start, count)], target, sems.at[i])
        )
    return copies


def prefetch_kernel(parts_ref, after_ref, *refs):
    half = len(refs) // 2
    copies = fetch_copies(parts_ref, refs[:half], refs[half:-1], refs[-1])
    for copy in copies:
        copy.start()
    for copy in copies:
        copy.wait()


def fetch_specs(fetches):
    sources = [pltpu.with_memory_space_constraint(w, pltpu.HBM) for w, _, _ in fetches]
    parts = jnp.stack([jnp.asarray(part, jnp.int32) for _, part, _ in fetches] + [jnp.int32(0)])
    shapes = [pltpu.VMEM((count, w.shape[2]), w.dtype) for w, _, count in fetches]
    return parts, sources, shapes


def prefetch(fetches, after):
    parts, sources, shapes = fetch_specs(fetches)
    return pl.pallas_call(
        prefetch_kernel,
        out_shape=shapes,
        in_specs=[pl.BlockSpec(memory_space=pltpu.SMEM)]
        + [pl.BlockSpec(memory_space=pl.ANY)] * (1 + len(sources)),
        out_specs=[pl.BlockSpec(memory_space=pltpu.VMEM)] * len(shapes),
        scratch_shapes=[pltpu.SemaphoreType.DMA((len(shapes),))],
        cost_estimate=cost(0, sum(2 * count * w.shape[2] for w, _, count in fetches)),
        compiler_params=params(),
        name="prefetch",
    )(parts, after, *sources)


def gate_up_kernel(*refs, experts, slices, first, last, fetched):
    parts_ref = refs[0]
    x_refs = refs[1 : 1 + experts]
    weights = refs[1 + experts : 1 + experts + 2 * slices]
    rest = list(refs[1 + experts + 2 * slices :])
    if not first:
        old_gate, old_up = rest[:2]
        rest = rest[2:]
    copies = []
    if fetched:
        sources, rest = rest[:fetched], rest[fetched:]
        copies = fetch_copies(parts_ref, sources, rest[-1 - fetched : -1], rest[-1])
    for copy in copies:
        copy.start()
    x = jnp.concatenate([r[...] for r in x_refs], axis=0)
    width, hidden = weights[0].shape
    tile = min(512, hidden)

    @pl.loop(0, hidden // tile)
    def _(n):
        columns = pl.ds(pl.multiple_of(n * tile, tile), tile)
        sums = []
        for kind in range(2):
            total = None if first else (old_gate, old_up)[kind][:, columns]
            for i in range(slices):
                term = jnp.dot(
                    x[:, i * width : (i + 1) * width],
                    weights[2 * i + kind][:, columns],
                    preferred_element_type=F32,
                )
                total = term if total is None else total + term
            sums.append(total)
        gate, up = sums
        if last:
            rest[0][:, columns] = (gate / (1.0 + jnp.exp(-gate)) * up).astype(BF16)
        else:
            rest[0][:, columns] = gate
            rest[1][:, columns] = up

    for copy in copies:
        copy.wait()


def gate_up(x_blocks, weights, sums, last, fetches):
    experts = len(x_blocks)
    rows = experts * x_blocks[0].shape[0]
    hidden = weights[0].shape[1]
    slices = len(weights) // 2
    first = sums is None
    parts, sources, shapes = fetch_specs(fetches)
    old = [] if first else pinned(sums)
    before = 1 + experts + len(weights)
    if last:
        out_shape = [pltpu.VMEM((rows, hidden), BF16)]
    else:
        out_shape = [pltpu.VMEM((rows, hidden), F32)] * 2
    results = pl.pallas_call(
        functools.partial(
            gate_up_kernel,
            experts=experts,
            slices=slices,
            first=first,
            last=last,
            fetched=len(fetches),
        ),
        out_shape=out_shape + shapes,
        in_specs=[pl.BlockSpec(memory_space=pltpu.SMEM)]
        + [pl.BlockSpec(memory_space=pltpu.VMEM)] * (before - 1 + len(old))
        + [pl.BlockSpec(memory_space=pl.ANY)] * len(sources),
        out_specs=[pl.BlockSpec(memory_space=pltpu.VMEM)] * len(out_shape + shapes),
        scratch_shapes=[pltpu.SemaphoreType.DMA((len(fetches),))] if fetches else [],
        input_output_aliases={} if first or last else {before: 0, before + 1: 1},
        cost_estimate=cost(
            2 * rows * hidden * sum(w.shape[0] for w in weights),
            sum(2 * w.size for w in weights),
        ),
        compiler_params=params(),
        name="gate_up",
    )(parts, *x_blocks, *pinned(weights), *old, *sources)
    return results[: len(out_shape)], results[len(out_shape) :]


def down_kernel(parts_ref, h_ref, w_ref, *refs, width, experts, waits):
    out_refs = refs[waits:]
    capacity = out_refs[0].shape[0]
    tile = min(256, width)
    part = 0
    for g in range(len(out_refs) // experts):
        outs = out_refs[g * experts : (g + 1) * experts]
        for i in range(outs[0].shape[1] // width):
            for n in range(width // tile):
                start = pl.multiple_of(parts_ref[part] * width + n * tile, tile)
                y = jnp.dot(h_ref[...], w_ref[:, pl.ds(start, tile)], preferred_element_type=F32)
                columns = pl.ds(i * width + n * tile, tile)
                for d, out in enumerate(outs):
                    out[:, columns] = y[d * capacity : (d + 1) * capacity].astype(BF16)
            part += 1


def down(groups, hidden, down_w, width, experts, after):
    rows, depth = hidden.shape
    capacity = rows // experts
    parts = [part for group in groups for part in group]
    wide = width * len(parts)
    blocks = pl.pallas_call(
        functools.partial(down_kernel, width=width, experts=experts, waits=len(after)),
        out_shape=[
            jax.ShapeDtypeStruct((capacity, width * len(group)), BF16)
            for group in groups
            for _ in range(experts)
        ],
        in_specs=[pl.BlockSpec(memory_space=pltpu.SMEM)]
        + [pl.BlockSpec(memory_space=pltpu.VMEM)] * 2
        + [pl.BlockSpec(memory_space=pl.ANY)] * len(after),
        out_specs=[pl.BlockSpec(memory_space=pltpu.VMEM)] * (experts * len(groups)),
        cost_estimate=cost(2 * rows * depth * wide, 2 * depth * wide + 2 * rows * wide),
        compiler_params=params(),
        name="down",
    )(jnp.stack(parts), *pinned([hidden, down_w]), *after)
    return [blocks[i * experts : (i + 1) * experts] for i in range(len(groups))]


def hold_kernel(*refs):
    count = len(refs) // 2
    for i in range(count):
        refs[count + 1 + i][...] = refs[i][...]


def hold(blocks, after):
    return pl.pallas_call(
        hold_kernel,
        out_shape=[jax.ShapeDtypeStruct(block.shape, block.dtype) for block in blocks],
        in_specs=[pl.BlockSpec(memory_space=pltpu.VMEM)] * len(blocks)
        + [pl.BlockSpec(memory_space=pl.ANY)],
        out_specs=[pl.BlockSpec(memory_space=pltpu.VMEM)] * len(blocks),
        cost_estimate=cost(0, sum(4 * block.size for block in blocks)),
        compiler_params=params(),
        name="hold",
    )(*blocks, after)


def combine_kernel(pick_ref, logits_ref, *refs, experts, sums, index):
    y_refs, added, out = refs[:experts], refs[experts : experts + sums], refs[-1]
    rows, width = out.shape
    columns = pl.ds(index * width, width)
    y = jnp.concatenate([r[:, columns] for r in y_refs], axis=0)
    picked = lax.dot_general(
        pick_ref[...], y, (((0,), (0,)), ((), ())), preferred_element_type=F32
    )
    share = 1.0 / (1.0 + jnp.exp(logits_ref[:, 1:2] - logits_ref[:, 0:1]))
    mixed = picked[:rows] * share + picked[rows:] * (1.0 - share)
    for other in added:
        mixed = mixed + other[...].astype(F32)
    out[...] = mixed.astype(BF16)


def combine(pick, logits, blocks, width, index, added):
    rows = logits.shape[0]
    operands = 2 + len(blocks) + len(added)
    return pl.pallas_call(
        functools.partial(
            combine_kernel, experts=len(blocks), sums=len(added), index=index
        ),
        out_shape=jax.ShapeDtypeStruct((rows, width), BF16),
        in_specs=[pl.BlockSpec(memory_space=pltpu.VMEM)] * operands,
        out_specs=pl.BlockSpec(memory_space=pltpu.VMEM),
        cost_estimate=cost(4 * rows * pick.shape[0] * width, 6 * rows * width),
        compiler_params=params(),
        name="combine",
    )(pick, logits, *blocks, *added)


def swap(value, axis, distance):
    if distance == 0:
        return value
    count = lax.axis_size(axis)
    return lax.ppermute(value, axis, [(i, i ^ distance) for i in range(count)])


def per_device(tokens, expert_ids, route_logits, gate_weight, up_weight, down_weight):
    rows, own_width = tokens.shape
    experts = lax.axis_size("expert")
    shards = lax.axis_size("tensor")
    capacity = rows // 2
    me = lax.axis_index("expert").astype(jnp.int32)
    column = lax.axis_index("tensor").astype(jnp.int32)
    direct = shards <= 8
    distances = list(range(shards)) if direct else [0]
    width = own_width if direct else own_width * shards

    def part_of(distance):
        return lax.bitwise_xor(column, jnp.int32(distance)) if direct else jnp.int32(0)

    if direct:
        blocks = [swap(tokens, "tensor", d) for d in distances]
    else:
        blocks = [lax.all_gather(tokens, "tensor", axis=1, tiled=True)]
    placed, pick = place(me, expert_ids, experts, capacity)

    groups = [distances[i : i + 2] for i in range(0, len(distances), 2)]
    ready, arrived, weights = placed, [], []
    for group in groups:
        fetches = [(w, part_of(d), width) for d in group for w in (gate_weight, up_weight)]
        weights.append(list(prefetch(fetches, ready)))
        block = [blocks[d] for d in group]
        outgoing = dispatch(placed, block, experts, capacity, weights[-1][:1])
        arrived.append([swap(block, "expert", e) for e, block in enumerate(outgoing)])
        ready = outgoing[0]

    sums, fetched = None, []
    for group, x_blocks, chosen in zip(groups, arrived, weights):
        later = [(down_weight, 0, down_weight.shape[1])] if sums is None else []
        sums, brought = gate_up(x_blocks, chosen, sums, group is groups[-1], later)
        fetched.extend(brought)
    hidden, down_w = sums[0], fetched[0]

    groups = [[d] for d in reversed(distances)]
    parts = [[part_of(d) for d in group] for group in groups]
    terms = down(parts[:1], hidden, down_w, width, experts, [])
    sums = []
    for group in groups:
        blocks = terms[groups.index(group)]
        if group is groups[-1] and sums:
            blocks = hold(blocks, sums[0])
        returned = [swap(block, "expert", e) for e, block in enumerate(blocks)]
        if group is groups[0] and len(parts) > 1:
            terms += down(parts[1:], hidden, down_w, width, experts, returned[1:2])
        for index, d in enumerate(group):
            last = d == distances[0]
            added = sums if last else []
            mixed = combine(pick, route_logits, returned, width, index, added)
            if not last:
                sums.append(swap(mixed, "tensor", d))
    if direct:
        return mixed
    return lax.psum_scatter(mixed, "tensor", scatter_dimension=1, tiled=True)


def solution(mesh):
    in_specs = (
        P(("groups", "expert"), "tensor"),
        P(("groups", "expert"), None),
        P(("groups", "expert"), None),
        P("expert", None, "tensor"),
        P("expert", None, "tensor"),
        P("expert", "tensor", None),
    )
    out_specs = P(("groups", "expert"), "tensor")
    return jax.shard_map(
        per_device, mesh=mesh, in_specs=in_specs, out_specs=out_specs, check_vma=False
    )
```

```python
import functools

import jax
import jax.numpy as jnp
from jax import lax
from jax.experimental import pallas as pl
from jax.experimental.pallas import tpu as pltpu
from jax.sharding import PartitionSpec as P

F32 = jnp.float32
BF16 = jnp.bfloat16
MIB = 1024 * 1024


def params(mib=6):
    return pltpu.CompilerParams(vmem_limit_bytes=mib * MIB)


def cost(flops, moved):
    return pl.CostEstimate(flops=flops, bytes_accessed=moved, transcendentals=0)


def pinned(arrays):
    return [pltpu.with_memory_space_constraint(array, pltpu.VMEM) for array in arrays]


def routing_kernel(where_ref, ids_ref, logits_ref, placed_ref, pick_ref, mix_ref, *, experts):
    rows = ids_ref.shape[1]
    capacity = placed_ref.shape[0] // experts
    relative = lax.bitwise_xor(ids_ref[...], where_ref[0])
    lane = lax.broadcasted_iota(jnp.int32, (experts, rows), 0)
    names = [lane == relative[k : k + 1] for k in range(2)]
    named = names[0] | names[1]
    row = lax.broadcasted_iota(jnp.int32, (rows, rows), 0)
    column = lax.broadcasted_iota(jnp.int32, (rows, rows), 1)
    before = jnp.dot(
        jnp.where(named, 1.0, 0.0).astype(BF16),
        jnp.where(row < column, 1.0, 0.0).astype(BF16),
        preferred_element_type=F32,
    ).astype(jnp.int32)
    slot = lax.broadcasted_iota(jnp.int32, (capacity, rows), 0)
    for d in range(experts):
        here = slice(d * capacity, (d + 1) * capacity)
        both = None
        for k in range(2):
            position = jnp.where(names[k], before, -1)
            hit = jnp.where(position[d : d + 1] == slot, 1.0, 0.0)
            pick_ref[here, k * rows : (k + 1) * rows] = hit.astype(BF16)
            both = hit if k == 0 else both + hit
        placed_ref[here, :] = both.astype(BF16)
    share = 1.0 / (1.0 + jnp.exp(logits_ref[1:2] - logits_ref[0:1]))
    share = jnp.sum(jnp.where(row == column, share, 0.0), axis=1, keepdims=True)
    mix_ref[:, 0:1] = share
    mix_ref[:, 1:2] = 1.0 - share


def place(where, expert_ids, route_logits, experts, capacity):
    rows = expert_ids.shape[0]
    return pl.pallas_call(
        functools.partial(routing_kernel, experts=experts),
        out_shape=[
            jax.ShapeDtypeStruct((experts * capacity, rows), BF16),
            jax.ShapeDtypeStruct((experts * capacity, 2 * rows), BF16),
            jax.ShapeDtypeStruct((rows, 2), F32),
        ],
        in_specs=[pl.BlockSpec(memory_space=pltpu.SMEM)]
        + [pl.BlockSpec(memory_space=pltpu.VMEM)] * 2,
        out_specs=[pl.BlockSpec(memory_space=pltpu.VMEM)] * 3,
        compiler_params=params(),
        name="routing",
    )(where, expert_ids.T, route_logits.T)


def dispatch_kernel(placed_ref, *refs, count, waits):
    refs = refs[:count] + refs[count + waits :]
    capacity, wide = refs[count].shape
    width = wide // count
    for i in range(count):
        block = refs[i][...]
        for d, out in enumerate(refs[count:]):
            out[:, i * width : (i + 1) * width] = jnp.dot(
                placed_ref[d * capacity : (d + 1) * capacity, :],
                block,
                preferred_element_type=F32,
            ).astype(BF16)


def dispatch(placed, blocks, experts, capacity, after):
    rows, width = blocks[0].shape
    wide = width * len(blocks)
    return pl.pallas_call(
        functools.partial(dispatch_kernel, count=len(blocks), waits=len(after)),
        out_shape=[jax.ShapeDtypeStruct((capacity, wide), BF16)] * experts,
        in_specs=[pl.BlockSpec(memory_space=pltpu.VMEM)] * (1 + len(blocks))
        + [pl.BlockSpec(memory_space=pl.ANY)] * len(after),
        out_specs=[pl.BlockSpec(memory_space=pltpu.VMEM)] * experts,
        cost_estimate=cost(2 * experts * capacity * rows * wide, 6 * rows * wide),
        compiler_params=params(),
        name="dispatch",
    )(placed, *blocks, *pinned(after))


def part_of(where_ref, distance):
    return 0 if distance is None else lax.bitwise_xor(where_ref[1], distance)


def prefetch_kernel(where_ref, after_ref, *refs, distances):
    half = len(refs) // 2
    copies = []
    for i, distance in enumerate(distances):
        source, target, sem = refs[i], refs[half + i], refs[-1].at[i]
        count = target.shape[0]
        start = pl.multiple_of(part_of(where_ref, distance) * count, count)
        copies.append(pltpu.make_async_copy(source.at[0, pl.ds(start, count)], target, sem))
    for copy in copies:
        copy.start()
    for copy in copies:
        copy.wait()


def prefetch(where, fetches, after):
    sources = [pltpu.with_memory_space_constraint(w, pltpu.HBM) for w, _, _ in fetches]
    shapes = [pltpu.VMEM((count, w.shape[2]), w.dtype) for w, _, count in fetches]
    return pl.pallas_call(
        functools.partial(prefetch_kernel, distances=[d for _, d, _ in fetches]),
        out_shape=shapes,
        in_specs=[pl.BlockSpec(memory_space=pltpu.SMEM)]
        + [pl.BlockSpec(memory_space=pl.ANY)] * (1 + len(sources)),
        out_specs=[pl.BlockSpec(memory_space=pltpu.VMEM)] * len(shapes),
        scratch_shapes=[pltpu.SemaphoreType.DMA((len(shapes),))],
        cost_estimate=cost(0, sum(2 * count * w.shape[2] for w, _, count in fetches)),
        compiler_params=params(),
        name="prefetch",
    )(where, after, *sources)


def gate_up_kernel(*refs, experts, slices, first, last):
    x_refs = refs[:experts]
    weights = refs[experts : experts + 2 * slices]
    rest = refs[experts + 2 * slices :]
    if not first:
        old_gate, old_up = rest[:2]
        rest = rest[2:]
    x = jnp.concatenate([r[...] for r in x_refs], axis=0)
    width, hidden = weights[0].shape
    tile = min(512, hidden)
    for n in range(hidden // tile):
        columns = slice(n * tile, (n + 1) * tile)
        sums = []
        for kind in range(2):
            total = None if first else (old_gate, old_up)[kind][:, columns]
            for i in range(slices):
                term = jnp.dot(
                    x[:, i * width : (i + 1) * width],
                    weights[2 * i + kind][:, columns],
                    preferred_element_type=F32,
                )
                total = term if total is None else total + term
            sums.append(total)
        gate, up = sums
        if last:
            rest[0][:, columns] = (gate / (1.0 + jnp.exp(-gate)) * up).astype(BF16)
        else:
            rest[0][:, columns] = gate
            rest[1][:, columns] = up


def gate_up(x_blocks, weights, sums, last):
    experts = len(x_blocks)
    rows = experts * x_blocks[0].shape[0]
    hidden = weights[0].shape[1]
    first = sums is None
    old = [] if first else pinned(sums)
    before = experts + len(weights)
    if last:
        out_shape = [pltpu.VMEM((rows, hidden), BF16)]
    else:
        out_shape = [pltpu.VMEM((rows, hidden), F32)] * 2
    return pl.pallas_call(
        functools.partial(
            gate_up_kernel, experts=experts, slices=len(weights) // 2, first=first, last=last
        ),
        out_shape=out_shape,
        in_specs=[pl.BlockSpec(memory_space=pltpu.VMEM)] * (before + len(old)),
        out_specs=[pl.BlockSpec(memory_space=pltpu.VMEM)] * len(out_shape),
        input_output_aliases={} if first or last else {before: 0, before + 1: 1},
        cost_estimate=cost(
            2 * rows * hidden * sum(w.shape[0] for w in weights),
            sum(2 * w.size for w in weights),
        ),
        compiler_params=params(),
        name="gate_up",
    )(*x_blocks, *pinned(weights), *old)


def down_kernel(where_ref, h_ref, w_ref, *refs, distance, waits):
    out_refs = refs[waits:]
    capacity, width = out_refs[0].shape
    tile = min(256, width)
    for n in range(width // tile):
        start = pl.multiple_of(part_of(where_ref, distance) * width + n * tile, tile)
        y = jnp.dot(h_ref[...], w_ref[:, pl.ds(start, tile)], preferred_element_type=F32)
        columns = slice(n * tile, (n + 1) * tile)
        for d, out in enumerate(out_refs):
            out[:, columns] = y[d * capacity : (d + 1) * capacity].astype(BF16)


def down(where, distance, hidden, down_w, width, experts, after):
    rows, depth = hidden.shape
    capacity = rows // experts
    return pl.pallas_call(
        functools.partial(down_kernel, distance=distance, waits=len(after)),
        out_shape=[jax.ShapeDtypeStruct((capacity, width), BF16)] * experts,
        in_specs=[pl.BlockSpec(memory_space=pltpu.SMEM)]
        + [pl.BlockSpec(memory_space=pltpu.VMEM)] * 2
        + [pl.BlockSpec(memory_space=pl.ANY)] * len(after),
        out_specs=[pl.BlockSpec(memory_space=pltpu.VMEM)] * experts,
        cost_estimate=cost(2 * rows * depth * width, 2 * depth * width + 2 * rows * width),
        compiler_params=params(),
        name="down",
    )(where, *pinned([hidden, down_w]), *after)


def combine_kernel(pick_ref, mix_ref, *refs, experts):
    y_refs, added, out = refs[:experts], refs[experts:-1], refs[-1]
    rows = out.shape[0]
    y = jnp.concatenate([r[...] for r in y_refs], axis=0)
    picked = lax.dot_general(
        pick_ref[...], y, (((0,), (0,)), ((), ())), preferred_element_type=F32
    )
    mixed = picked[:rows] * mix_ref[:, 0:1] + picked[rows:] * mix_ref[:, 1:2]
    for other in added:
        mixed = mixed + other[...].astype(F32)
    out[...] = mixed.astype(BF16)


def combine(pick, mix, blocks, added):
    rows = mix.shape[0]
    width = blocks[0].shape[1]
    operands = 2 + len(blocks) + len(added)
    return pl.pallas_call(
        functools.partial(combine_kernel, experts=len(blocks)),
        out_shape=jax.ShapeDtypeStruct((rows, width), BF16),
        in_specs=[pl.BlockSpec(memory_space=pltpu.VMEM)] * operands,
        out_specs=pl.BlockSpec(memory_space=pltpu.VMEM),
        cost_estimate=cost(4 * rows * pick.shape[0] * width, 6 * rows * width),
        compiler_params=params(),
        name="combine",
    )(pick, mix, *blocks, *added)


def swap(value, axis, distance):
    if not distance:
        return value
    count = lax.axis_size(axis)
    return lax.ppermute(value, axis, [(i, i ^ distance) for i in range(count)])


def per_device(tokens, expert_ids, route_logits, gate_weight, up_weight, down_weight):
    rows, own_width = tokens.shape
    experts = lax.axis_size("expert")
    shards = lax.axis_size("tensor")
    capacity = rows // 2
    where = jnp.stack([lax.axis_index("expert"), lax.axis_index("tensor")]).astype(jnp.int32)
    direct = shards <= 8
    distances = list(range(shards)) if direct else [None]
    width = own_width if direct else own_width * shards

    if direct:
        blocks = [swap(tokens, "tensor", d) for d in distances]
    else:
        blocks = [lax.all_gather(tokens, "tensor", axis=1, tiled=True)]
    placed, pick, mix = place(where, expert_ids, route_logits, experts, capacity)

    def rows_of(chosen):
        return [(w, d, width) for d in chosen for w in (gate_weight, up_weight)]

    whole = [(down_weight, None, down_weight.shape[1])]
    weights = list(prefetch(where, rows_of(distances[:2]), placed))
    groups = [list(range(len(distances)))[:2]] + [[i] for i in range(2, len(distances))]
    arrived = []
    for group in groups:
        after = weights[:1] if group is groups[0] else weights[-1:]
        outgoing = dispatch(placed, [blocks[i] for i in group], experts, capacity, after)
        arrived.append([swap(block, "expert", e) for e, block in enumerate(outgoing)])
        if group is groups[0]:
            weights += prefetch(where, rows_of(distances[2:]) + whole, outgoing[0])
    sums = None
    for group, x_blocks in zip(groups, arrived):
        chosen = weights[2 * group[0] : 2 * group[-1] + 2]
        sums = gate_up(x_blocks, chosen, sums, group is groups[-1])
    hidden, down_w = sums[0], weights[-1]

    sums, mixtures = [], []
    for d in reversed(distances):
        last = d == distances[0]
        after = sums[:1] if last else mixtures[-2:-1]
        terms = down(where, d, hidden, down_w, width, experts, after)
        returned = [swap(block, "expert", e) for e, block in enumerate(terms)]
        mixed = combine(pick, mix, returned, sums[::-1] if last else [])
        if not last:
            mixtures.append(mixed)
            sums.append(swap(mixed, "tensor", d))
    if direct:
        return mixed
    return lax.psum_scatter(mixed, "tensor", scatter_dimension=1, tiled=True)


def solution(mesh):
    in_specs = (
        P(("groups", "expert"), "tensor"),
        P(("groups", "expert"), None),
        P(("groups", "expert"), None),
        P("expert", None, "tensor"),
        P("expert", None, "tensor"),
        P("expert", "tensor", None),
    )
    out_specs = P(("groups", "expert"), "tensor")
    return jax.shard_map(
        per_device, mesh=mesh, in_specs=in_specs, out_specs=out_specs, check_vma=False
    )
```

```python
import functools

import jax
import jax.numpy as jnp
from jax import lax
from jax.experimental import pallas as pl
from jax.experimental.pallas import tpu as pltpu
from jax.sharding import PartitionSpec as P

F32 = jnp.float32
BF16 = jnp.bfloat16
MIB = 1024 * 1024


def params(mib=6):
    return pltpu.CompilerParams(vmem_limit_bytes=mib * MIB)


def cost(flops, moved):
    return pl.CostEstimate(flops=flops, bytes_accessed=moved, transcendentals=0)


def pinned(arrays):
    return [pltpu.with_memory_space_constraint(array, pltpu.VMEM) for array in arrays]


def routing_kernel(me_ref, ids_ref, logits_ref, placed_ref, pick_ref, mix_ref, *, experts):
    rows = ids_ref.shape[1]
    capacity = placed_ref.shape[0] // experts
    relative = lax.bitwise_xor(ids_ref[...], me_ref[0])
    lane = lax.broadcasted_iota(jnp.int32, (experts, rows), 0)
    names = [lane == relative[k : k + 1] for k in range(2)]
    named = names[0] | names[1]
    row = lax.broadcasted_iota(jnp.int32, (rows, rows), 0)
    column = lax.broadcasted_iota(jnp.int32, (rows, rows), 1)
    before = jnp.dot(
        jnp.where(named, 1.0, 0.0).astype(BF16),
        jnp.where(row < column, 1.0, 0.0).astype(BF16),
        preferred_element_type=F32,
    ).astype(jnp.int32)
    slot = lax.broadcasted_iota(jnp.int32, (capacity, rows), 0)
    for d in range(experts):
        here = slice(d * capacity, (d + 1) * capacity)
        both = None
        for k in range(2):
            position = jnp.where(names[k], before, -1)
            hit = jnp.where(position[d : d + 1] == slot, 1.0, 0.0)
            pick_ref[here, k * rows : (k + 1) * rows] = hit.astype(BF16)
            both = hit if k == 0 else both + hit
        placed_ref[here, :] = both.astype(BF16)
    share = 1.0 / (1.0 + jnp.exp(logits_ref[1:2] - logits_ref[0:1]))
    share = jnp.sum(jnp.where(row == column, share, 0.0), axis=1, keepdims=True)
    mix_ref[:, 0:1] = share
    mix_ref[:, 1:2] = 1.0 - share


def place(me, expert_ids, route_logits, experts, capacity):
    rows = expert_ids.shape[0]
    return pl.pallas_call(
        functools.partial(routing_kernel, experts=experts),
        out_shape=[
            jax.ShapeDtypeStruct((experts * capacity, rows), BF16),
            jax.ShapeDtypeStruct((experts * capacity, 2 * rows), BF16),
            jax.ShapeDtypeStruct((rows, 2), F32),
        ],
        in_specs=[pl.BlockSpec(memory_space=pltpu.SMEM)]
        + [pl.BlockSpec(memory_space=pltpu.VMEM)] * 2,
        out_specs=[pl.BlockSpec(memory_space=pltpu.VMEM)] * 3,
        compiler_params=params(),
        name="routing",
    )(me.reshape(1), expert_ids.T, route_logits.T)


def dispatch_kernel(placed_ref, *refs, counts, waits):
    inputs, outputs = refs[: sum(counts)], refs[sum(counts) + waits :]
    capacity, wide = outputs[0].shape
    width = wide // len(counts)
    for i, count in enumerate(counts):
        block = inputs[sum(counts[:i])][...]
        for j in range(1, count):
            block = block + inputs[sum(counts[:i]) + j][...]
        for d, out in enumerate(outputs):
            out[:, i * width : (i + 1) * width] = jnp.dot(
                placed_ref[d * capacity : (d + 1) * capacity, :],
                block,
                preferred_element_type=F32,
            ).astype(BF16)


def dispatch(placed, slices, experts, capacity, after):
    rows, width = slices[0][0].shape
    wide = width * len(slices)
    arrays = [array for arrays in slices for array in arrays]
    return pl.pallas_call(
        functools.partial(
            dispatch_kernel, counts=[len(arrays) for arrays in slices], waits=len(after)
        ),
        out_shape=[jax.ShapeDtypeStruct((capacity, wide), BF16)] * experts,
        in_specs=[pl.BlockSpec(memory_space=pltpu.VMEM)] * (1 + len(arrays))
        + [pl.BlockSpec(memory_space=pl.ANY)] * len(after),
        out_specs=[pl.BlockSpec(memory_space=pltpu.VMEM)] * experts,
        cost_estimate=cost(2 * experts * capacity * rows * wide, 6 * rows * wide),
        compiler_params=params(),
        name="dispatch",
    )(placed, *arrays, *pinned(after))


def across(distance):
    return lambda column: lax.bitwise_xor(column, distance)


def second(column):
    return jnp.where(column < 2, 2, 1)


def third(column):
    return jnp.where(column < 2, 3, 0)


def everything(column):
    return 0


def prefetch_kernel(column_ref, after_ref, *refs, parts):
    half = len(refs) // 2
    copies = []
    for i, part in enumerate(parts):
        source, target, sem = refs[i], refs[half + i], refs[-1].at[i]
        count = target.shape[0]
        start = pl.multiple_of(part(column_ref[0]) * count, count)
        copies.append(pltpu.make_async_copy(source.at[0, pl.ds(start, count)], target, sem))
    for copy in copies:
        copy.start()
    for copy in copies:
        copy.wait()


def prefetch(column, fetches, after):
    sources = [pltpu.with_memory_space_constraint(w, pltpu.HBM) for w, _, _ in fetches]
    shapes = [pltpu.VMEM((count, w.shape[2]), w.dtype) for w, _, count in fetches]
    return pl.pallas_call(
        functools.partial(prefetch_kernel, parts=[part for _, part, _ in fetches]),
        out_shape=shapes,
        in_specs=[pl.BlockSpec(memory_space=pltpu.SMEM)]
        + [pl.BlockSpec(memory_space=pl.ANY)] * (1 + len(sources)),
        out_specs=[pl.BlockSpec(memory_space=pltpu.VMEM)] * len(shapes),
        scratch_shapes=[pltpu.SemaphoreType.DMA((len(shapes),))],
        cost_estimate=cost(0, sum(2 * count * w.shape[2] for w, _, count in fetches)),
        compiler_params=params(),
        name="prefetch",
    )(column.reshape(1), after, *sources)


def gate_up_kernel(*refs, experts, slices, first, last):
    x_refs = refs[:experts]
    weights = refs[experts : experts + 2 * slices]
    rest = refs[experts + 2 * slices :]
    if not first:
        old_gate, old_up = rest[:2]
        rest = rest[2:]
    x = jnp.concatenate([r[...] for r in x_refs], axis=0)
    width, hidden = weights[0].shape
    tile = min(512, hidden)
    for n in range(hidden // tile):
        columns = slice(n * tile, (n + 1) * tile)
        sums = []
        for kind in range(2):
            total = None if first else (old_gate, old_up)[kind][:, columns]
            for i in range(slices):
                term = jnp.dot(
                    x[:, i * width : (i + 1) * width],
                    weights[2 * i + kind][:, columns],
                    preferred_element_type=F32,
                )
                total = term if total is None else total + term
            sums.append(total)
        gate, up = sums
        if last:
            rest[0][:, columns] = (gate / (1.0 + jnp.exp(-gate)) * up).astype(BF16)
        else:
            rest[0][:, columns] = gate
            rest[1][:, columns] = up


def gate_up(x_blocks, weights, sums, last):
    experts = len(x_blocks)
    rows = experts * x_blocks[0].shape[0]
    hidden = weights[0].shape[1]
    first = sums is None
    old = [] if first else pinned(sums)
    before = experts + len(weights)
    if last:
        out_shape = [pltpu.VMEM((rows, hidden), BF16)]
    else:
        out_shape = [pltpu.VMEM((rows, hidden), F32)] * 2
    return pl.pallas_call(
        functools.partial(
            gate_up_kernel, experts=experts, slices=len(weights) // 2, first=first, last=last
        ),
        out_shape=out_shape,
        in_specs=[pl.BlockSpec(memory_space=pltpu.VMEM)] * (before + len(old)),
        out_specs=[pl.BlockSpec(memory_space=pltpu.VMEM)] * len(out_shape),
        input_output_aliases={} if first or last else {before: 0, before + 1: 1},
        cost_estimate=cost(
            2 * rows * hidden * sum(w.shape[0] for w in weights),
            sum(2 * w.size for w in weights),
        ),
        compiler_params=params(),
        name="gate_up",
    )(*x_blocks, *pinned(weights), *old)


def down_kernel(column_ref, h_ref, w_ref, *out_refs, part):
    capacity, width = out_refs[0].shape
    tile = min(256, width)
    for n in range(width // tile):
        start = pl.multiple_of(part(column_ref[0]) * width + n * tile, tile)
        y = jnp.dot(h_ref[...], w_ref[0, :, pl.ds(start, tile)], preferred_element_type=F32)
        columns = slice(n * tile, (n + 1) * tile)
        for d, out in enumerate(out_refs):
            out[:, columns] = y[d * capacity : (d + 1) * capacity].astype(BF16)


def down(column, part, hidden, down_w, width, experts):
    rows, depth = hidden.shape
    capacity = rows // experts
    return pl.pallas_call(
        functools.partial(down_kernel, part=part),
        out_shape=[jax.ShapeDtypeStruct((capacity, width), BF16)] * experts,
        in_specs=[pl.BlockSpec(memory_space=pltpu.SMEM)]
        + [pl.BlockSpec(memory_space=pltpu.VMEM)] * 2,
        out_specs=[pl.BlockSpec(memory_space=pltpu.VMEM)] * experts,
        cost_estimate=cost(2 * rows * depth * width, 2 * depth * width + 2 * rows * width),
        compiler_params=params(),
        name="down",
    )(column.reshape(1), *pinned([hidden, down_w]))


def combine_kernel(pick_ref, mix_ref, *refs, experts, sums, plain):
    outs = refs[len(refs) - 1 - plain :]
    y_refs, added = refs[:experts], refs[experts : experts + sums]
    rows = outs[0].shape[0]
    y = jnp.concatenate([r[...] for r in y_refs], axis=0)
    picked = lax.dot_general(
        pick_ref[...], y, (((0,), (0,)), ((), ())), preferred_element_type=F32
    )
    mixed = picked[:rows] * mix_ref[:, 0:1] + picked[rows:] * mix_ref[:, 1:2]
    if plain:
        outs[1][...] = mixed.astype(BF16)
    for other in added:
        mixed = mixed + other[...].astype(F32)
    outs[0][...] = mixed.astype(BF16)


def combine(pick, mix, blocks, added, after=(), plain=False):
    rows = mix.shape[0]
    width = blocks[0].shape[1]
    operands = 2 + len(blocks) + len(added)
    return pl.pallas_call(
        functools.partial(
            combine_kernel, experts=len(blocks), sums=len(added), plain=plain
        ),
        out_shape=[jax.ShapeDtypeStruct((rows, width), BF16)] * (1 + plain),
        in_specs=[pl.BlockSpec(memory_space=pltpu.VMEM)] * operands
        + [pl.BlockSpec(memory_space=pl.ANY)] * len(after),
        out_specs=[pl.BlockSpec(memory_space=pltpu.VMEM)] * (1 + plain),
        cost_estimate=cost(4 * rows * pick.shape[0] * width, 6 * rows * width),
        compiler_params=params(),
        name="combine",
    )(pick, mix, *blocks, *added, *after)


def add_kernel(a_ref, b_ref, out_ref):
    out_ref[...] = (a_ref[...].astype(F32) + b_ref[...].astype(F32)).astype(BF16)


def add(a, b):
    return pl.pallas_call(
        add_kernel,
        out_shape=jax.ShapeDtypeStruct(a.shape, BF16),
        in_specs=[pl.BlockSpec(memory_space=pltpu.VMEM)] * 2,
        out_specs=pl.BlockSpec(memory_space=pltpu.VMEM),
        cost_estimate=cost(a.size, 6 * a.size),
        compiler_params=params(),
        name="add",
    )(a, b)


def swap(value, axis, distance):
    if not distance:
        return value
    count = lax.axis_size(axis)
    return lax.ppermute(value, axis, [(i, i ^ distance) for i in range(count)])


def middle(value):
    return lax.ppermute(value, "tensor", [(1, 2), (2, 1)])


def outwards(value):
    return lax.ppermute(value, "tensor", [(1, 0), (2, 3)])


def inwards(value):
    return lax.ppermute(value, "tensor", [(0, 1), (3, 2)])


def per_device(tokens, expert_ids, route_logits, gate_weight, up_weight, down_weight):
    rows, own_width = tokens.shape
    experts = lax.axis_size("expert")
    shards = lax.axis_size("tensor")
    capacity = rows // 2
    me = lax.axis_index("expert").astype(jnp.int32)
    column = lax.axis_index("tensor").astype(jnp.int32)
    line = shards == 4
    width = own_width if line else own_width * shards

    if line:
        beside = swap(tokens, "tensor", 1)
        near = middle(tokens)
        far = middle(beside)
        parts = [across(0), across(1), second, third]
        slices = [[tokens], [beside], [near, outwards(near)], [far, outwards(far)]]
        groups = [[0, 1], [2], [3]]
    else:
        parts = [everything]
        slices = [[lax.all_gather(tokens, "tensor", axis=1, tiled=True)]]
        groups = [[0]]
    placed, pick, mix = place(me, expert_ids, route_logits, experts, capacity)

    weights, arrived, ready = [], [], placed
    for i, part in enumerate(parts):
        fetches = [(w, part, width) for w in (gate_weight, up_weight)]
        weights.append(list(prefetch(column, fetches, ready)))
        if i < len(groups):
            chosen = [slices[j] for j in groups[i]]
            outgoing = dispatch(placed, chosen, experts, capacity, weights[-1][:1])
            arrived.append([swap(block, "expert", e) for e, block in enumerate(outgoing)])
            ready = outgoing[0]

    sums = None
    for group, x_blocks in zip(groups, arrived):
        chosen = [w for j in group for w in weights[j]]
        sums = gate_up(x_blocks, chosen, sums, group is groups[-1])
    hidden = sums[0]

    def returned(part):
        terms = down(column, part, hidden, down_weight, width, experts)
        return [swap(block, "expert", e) for e, block in enumerate(terms)]

    if not line:
        mixed = combine(pick, mix, returned(everything), [])[0]
        return lax.psum_scatter(mixed, "tensor", scatter_dimension=1, tiled=True)
    blocks = [returned(across(distance)) for distance in range(4)]
    last = combine(pick, mix, blocks[3], [], after=blocks[2][2:3])[0]
    from_end = inwards(last)
    onwards, alone = combine(pick, mix, blocks[2], [from_end], after=blocks[1][2:3], plain=True)
    over = middle(onwards)
    crossing = middle(add(last, inwards(alone)))
    next_to = combine(pick, mix, blocks[1], [over], after=blocks[0][2:3])[0]
    beside = swap(next_to, "tensor", 1)
    return combine(pick, mix, blocks[0], [beside, crossing])[0]


def solution(mesh):
    in_specs = (
        P(("groups", "expert"), "tensor"),
        P(("groups", "expert"), None),
        P(("groups", "expert"), None),
        P("expert", None, "tensor"),
        P("expert", None, "tensor"),
        P("expert", "tensor", None),
    )
    out_specs = P(("groups", "expert"), "tensor")
    return jax.shard_map(
        per_device, mesh=mesh, in_specs=in_specs, out_specs=out_specs, check_vma=False
    )
```

```python
import functools

import jax
import jax.numpy as jnp
from jax import lax
from jax.experimental import pallas as pl
from jax.experimental.pallas import tpu as pltpu
from jax.sharding import PartitionSpec as P

F32 = jnp.float32
BF16 = jnp.bfloat16
MIB = 1024 * 1024


def params(mib=6):
    return pltpu.CompilerParams(vmem_limit_bytes=mib * MIB)


def cost(flops, moved):
    return pl.CostEstimate(flops=flops, bytes_accessed=moved, transcendentals=0)


def pinned(arrays):
    return [pltpu.with_memory_space_constraint(array, pltpu.VMEM) for array in arrays]


def routing_kernel(me_ref, ids_ref, logits_ref, placed_ref, pick_ref, mix_ref, *, experts):
    rows = ids_ref.shape[1]
    capacity = placed_ref.shape[0] // experts
    relative = lax.bitwise_xor(ids_ref[...], me_ref[0])
    lane = lax.broadcasted_iota(jnp.int32, (experts, rows), 0)
    names = [lane == relative[k : k + 1] for k in range(2)]
    named = names[0] | names[1]
    row = lax.broadcasted_iota(jnp.int32, (rows, rows), 0)
    column = lax.broadcasted_iota(jnp.int32, (rows, rows), 1)
    before = jnp.dot(
        jnp.where(named, 1.0, 0.0).astype(BF16),
        jnp.where(row < column, 1.0, 0.0).astype(BF16),
        preferred_element_type=F32,
    ).astype(jnp.int32)
    slot = lax.broadcasted_iota(jnp.int32, (capacity, rows), 0)
    for d in range(experts):
        here = slice(d * capacity, (d + 1) * capacity)
        both = None
        for k in range(2):
            position = jnp.where(names[k], before, -1)
            hit = jnp.where(position[d : d + 1] == slot, 1.0, 0.0)
            pick_ref[here, k * rows : (k + 1) * rows] = hit.astype(BF16)
            both = hit if k == 0 else both + hit
        placed_ref[here, :] = both.astype(BF16)
    share = 1.0 / (1.0 + jnp.exp(logits_ref[1:2] - logits_ref[0:1]))
    share = jnp.sum(jnp.where(row == column, share, 0.0), axis=1, keepdims=True)
    mix_ref[:, 0:1] = share
    mix_ref[:, 1:2] = 1.0 - share


def place(me, expert_ids, route_logits, experts, capacity):
    rows = expert_ids.shape[0]
    return pl.pallas_call(
        functools.partial(routing_kernel, experts=experts),
        out_shape=[
            jax.ShapeDtypeStruct((experts * capacity, rows), BF16),
            jax.ShapeDtypeStruct((experts * capacity, 2 * rows), BF16),
            jax.ShapeDtypeStruct((rows, 2), F32),
        ],
        in_specs=[pl.BlockSpec(memory_space=pltpu.SMEM)]
        + [pl.BlockSpec(memory_space=pltpu.VMEM)] * 2,
        out_specs=[pl.BlockSpec(memory_space=pltpu.VMEM)] * 3,
        compiler_params=params(),
        name="routing",
    )(me.reshape(1), expert_ids.T, route_logits.T)


def dispatch_kernel(placed_ref, *refs, count, waits):
    inputs, outputs = refs[:count], refs[count + waits :]
    capacity, wide = outputs[0].shape
    width = wide // count
    for i, block in enumerate(inputs):
        for d, out in enumerate(outputs):
            out[:, i * width : (i + 1) * width] = jnp.dot(
                placed_ref[d * capacity : (d + 1) * capacity, :],
                block[...],
                preferred_element_type=F32,
            ).astype(BF16)


def dispatch(placed, slices, experts, capacity, after):
    rows, width = slices[0].shape
    wide = width * len(slices)
    return pl.pallas_call(
        functools.partial(dispatch_kernel, count=len(slices), waits=len(after)),
        out_shape=[jax.ShapeDtypeStruct((capacity, wide), BF16)] * experts,
        in_specs=[pl.BlockSpec(memory_space=pltpu.VMEM)] * (1 + len(slices))
        + [pl.BlockSpec(memory_space=pl.ANY)] * len(after),
        out_specs=[pl.BlockSpec(memory_space=pltpu.VMEM)] * experts,
        cost_estimate=cost(2 * experts * capacity * rows * wide, 6 * rows * wide),
        compiler_params=params(),
        name="dispatch",
    )(placed, *slices, *pinned(after))


def across(distance):
    return lambda column: lax.bitwise_xor(column, distance)


def everything(column):
    return 0


def prefetch_kernel(column_ref, after_ref, *refs, parts):
    half = len(refs) // 2
    copies = []
    for i, part in enumerate(parts):
        source, target, sem = refs[i], refs[half + i], refs[-1].at[i]
        count = target.shape[0]
        start = pl.multiple_of(part(column_ref[0]) * count, count)
        copies.append(pltpu.make_async_copy(source.at[0, pl.ds(start, count)], target, sem))
    for copy in copies:
        copy.start()
    for copy in copies:
        copy.wait()


def prefetch(column, fetches, after):
    sources = [pltpu.with_memory_space_constraint(w, pltpu.HBM) for w, _, _ in fetches]
    shapes = [pltpu.VMEM((count, w.shape[2]), w.dtype) for w, _, count in fetches]
    return pl.pallas_call(
        functools.partial(prefetch_kernel, parts=[part for _, part, _ in fetches]),
        out_shape=shapes,
        in_specs=[pl.BlockSpec(memory_space=pltpu.SMEM)]
        + [pl.BlockSpec(memory_space=pl.ANY)] * (1 + len(sources)),
        out_specs=[pl.BlockSpec(memory_space=pltpu.VMEM)] * len(shapes),
        scratch_shapes=[pltpu.SemaphoreType.DMA((len(shapes),))],
        cost_estimate=cost(0, sum(2 * count * w.shape[2] for w, _, count in fetches)),
        compiler_params=params(),
        name="prefetch",
    )(column.reshape(1), after, *sources)


def gate_up_kernel(*refs, experts, slices, first, last, waits):
    x_refs = refs[:experts]
    weights = refs[experts : experts + 2 * slices]
    rest = refs[experts + 2 * slices :]
    if not first:
        old_gate, old_up = rest[:2]
        rest = rest[2:]
    rest = rest[waits:]
    x = jnp.concatenate([r[...] for r in x_refs], axis=0)
    width, hidden = weights[0].shape
    tile = min(512, hidden)
    for n in range(hidden // tile):
        columns = slice(n * tile, (n + 1) * tile)
        sums = []
        for kind in range(2):
            total = None if first else (old_gate, old_up)[kind][:, columns]
            for i in range(slices):
                term = jnp.dot(
                    x[:, i * width : (i + 1) * width],
                    weights[2 * i + kind][:, columns],
                    preferred_element_type=F32,
                )
                total = term if total is None else total + term
            sums.append(total)
        gate, up = sums
        if last:
            rest[0][:, columns] = (gate / (1.0 + jnp.exp(-gate)) * up).astype(BF16)
        else:
            rest[0][:, columns] = gate
            rest[1][:, columns] = up


def gate_up(x_blocks, weights, sums, last, after):
    experts = len(x_blocks)
    rows = experts * x_blocks[0].shape[0]
    hidden = weights[0].shape[1]
    first = sums is None
    old = [] if first else pinned(sums)
    before = experts + len(weights)
    if last:
        out_shape = [pltpu.VMEM((rows, hidden), BF16)]
    else:
        out_shape = [pltpu.VMEM((rows, hidden), F32)] * 2
    return pl.pallas_call(
        functools.partial(
            gate_up_kernel,
            experts=experts,
            slices=len(weights) // 2,
            first=first,
            last=last,
            waits=len(after),
        ),
        out_shape=out_shape,
        in_specs=[pl.BlockSpec(memory_space=pltpu.VMEM)] * (before + len(old))
        + [pl.BlockSpec(memory_space=pl.ANY)] * len(after),
        out_specs=[pl.BlockSpec(memory_space=pltpu.VMEM)] * len(out_shape),
        input_output_aliases={} if first or last else {before: 0, before + 1: 1},
        cost_estimate=cost(
            2 * rows * hidden * sum(w.shape[0] for w in weights),
            sum(2 * w.size for w in weights),
        ),
        compiler_params=params(),
        name="gate_up",
    )(*x_blocks, *pinned(weights), *old, *after)


def down_kernel(column_ref, h_ref, w_ref, *refs, part, waits):
    out_refs = refs[waits:]
    capacity, width = out_refs[0].shape
    tile = min(256, width)
    for n in range(width // tile):
        start = pl.multiple_of(part(column_ref[0]) * width + n * tile, tile)
        y = jnp.dot(h_ref[...], w_ref[0, :, pl.ds(start, tile)], preferred_element_type=F32)
        columns = slice(n * tile, (n + 1) * tile)
        for d, out in enumerate(out_refs):
            out[:, columns] = y[d * capacity : (d + 1) * capacity].astype(BF16)


def down(column, part, hidden, down_w, width, experts, after):
    rows, depth = hidden.shape
    capacity = rows // experts
    return pl.pallas_call(
        functools.partial(down_kernel, part=part, waits=len(after)),
        out_shape=[jax.ShapeDtypeStruct((capacity, width), BF16)] * experts,
        in_specs=[pl.BlockSpec(memory_space=pltpu.SMEM)]
        + [pl.BlockSpec(memory_space=pltpu.VMEM)] * 2
        + [pl.BlockSpec(memory_space=pl.ANY)] * len(after),
        out_specs=[pl.BlockSpec(memory_space=pltpu.VMEM)] * experts,
        cost_estimate=cost(2 * rows * depth * width, 2 * depth * width + 2 * rows * width),
        compiler_params=params(),
        name="down",
    )(column.reshape(1), *pinned([hidden, down_w]), *after)


def combine_kernel(pick_ref, mix_ref, *refs, experts, sums):
    y_refs, added, out = refs[:experts], refs[experts : experts + sums], refs[-1]
    rows = out.shape[0]
    y = jnp.concatenate([r[...] for r in y_refs], axis=0)
    picked = lax.dot_general(
        pick_ref[...], y, (((0,), (0,)), ((), ())), preferred_element_type=F32
    )
    mixed = picked[:rows] * mix_ref[:, 0:1] + picked[rows:] * mix_ref[:, 1:2]
    for other in added:
        mixed = mixed + other[...].astype(F32)
    out[...] = mixed.astype(BF16)


def combine(pick, mix, blocks, added, after=()):
    rows = mix.shape[0]
    width = blocks[0].shape[1]
    operands = 2 + len(blocks) + len(added)
    return pl.pallas_call(
        functools.partial(combine_kernel, experts=len(blocks), sums=len(added)),
        out_shape=jax.ShapeDtypeStruct((rows, width), BF16),
        in_specs=[pl.BlockSpec(memory_space=pltpu.VMEM)] * operands
        + [pl.BlockSpec(memory_space=pl.ANY)] * len(after),
        out_specs=pl.BlockSpec(memory_space=pltpu.VMEM),
        cost_estimate=cost(4 * rows * pick.shape[0] * width, 6 * rows * width),
        compiler_params=params(),
        name="combine",
    )(pick, mix, *blocks, *added, *after)


def swap(value, axis, distance):
    if not distance:
        return value
    count = lax.axis_size(axis)
    return lax.ppermute(value, axis, [(i, i ^ distance) for i in range(count)])


def per_device(tokens, expert_ids, route_logits, gate_weight, up_weight, down_weight):
    rows, own_width = tokens.shape
    experts = lax.axis_size("expert")
    shards = lax.axis_size("tensor")
    capacity = rows // 2
    me = lax.axis_index("expert").astype(jnp.int32)
    column = lax.axis_index("tensor").astype(jnp.int32)
    doubling = shards == 4
    width = own_width if doubling else own_width * shards

    if doubling:
        across_two = swap(tokens, "tensor", 2)
        slices = [tokens, swap(tokens, "tensor", 1), across_two, swap(across_two, "tensor", 1)]
        parts = [across(distance) for distance in range(4)]
        groups = [[0, 1], [2], [3]]
    else:
        slices = [lax.all_gather(tokens, "tensor", axis=1, tiled=True)]
        parts = [everything]
        groups = [[0]]
    placed, pick, mix = place(me, expert_ids, route_logits, experts, capacity)

    def fetch(chosen, after):
        fetches = [(w, parts[i], width) for i in chosen for w in (gate_weight, up_weight)]
        return list(prefetch(column, fetches, after))

    weights, arrived = fetch(groups[0], placed), []
    for group in groups:
        after = weights[-1:] if len(arrived) < 2 else []
        outgoing = dispatch(placed, [slices[i] for i in group], experts, capacity, after)
        arrived.append([swap(block, "expert", e) for e, block in enumerate(outgoing)])
        if len(arrived) == 1 and len(groups) > 1:
            weights += fetch([2, 3], outgoing[0])
    sums = None
    for group, x_blocks in zip(groups, arrived):
        chosen = weights[2 * group[0] : 2 * group[-1] + 2]
        after = arrived[1][1:2] if sums is None and len(groups) > 1 else []
        sums = gate_up(x_blocks, chosen, sums, group is groups[-1], after)
    hidden = sums[0]

    def returned(part, after=()):
        terms = down(column, part, hidden, down_weight, width, experts, after)
        return [swap(block, "expert", e) for e, block in enumerate(terms)]

    if not doubling:
        mixed = combine(pick, mix, returned(everything), [])
        return lax.psum_scatter(mixed, "tensor", scatter_dimension=1, tiled=True)
    blocks = [returned(across(3)), returned(across(2))]
    passed = swap(combine(pick, mix, blocks[0], [], blocks[1][2:3]), "tensor", 1)
    onwards = combine(pick, mix, blocks[1], [passed])
    over = swap(onwards, "tensor", 2)
    beside = swap(combine(pick, mix, returned(across(1), [onwards]), []), "tensor", 1)
    return combine(pick, mix, returned(across(0), [onwards]), [beside, over])


def solution(mesh):
    in_specs = (
        P(("groups", "expert"), "tensor"),
        P(("groups", "expert"), None),
        P(("groups", "expert"), None),
        P("expert", None, "tensor"),
        P("expert", None, "tensor"),
        P("expert", "tensor", None),
    )
    out_specs = P(("groups", "expert"), "tensor")
    return jax.shard_map(
        per_device, mesh=mesh, in_specs=in_specs, out_specs=out_specs, check_vma=False
    )
```

```python
import functools

import jax
import jax.numpy as jnp
from jax import lax
from jax.experimental import pallas as pl
from jax.experimental.pallas import tpu as pltpu
from jax.sharding import PartitionSpec as P

F32 = jnp.float32
BF16 = jnp.bfloat16
MIB = 1024 * 1024


def params(mib=6):
    return pltpu.CompilerParams(vmem_limit_bytes=mib * MIB)


def cost(flops, moved):
    return pl.CostEstimate(flops=flops, bytes_accessed=moved, transcendentals=0)


def pinned(arrays):
    return [pltpu.with_memory_space_constraint(array, pltpu.VMEM) for array in arrays]


def routing_kernel(me_ref, ids_ref, logits_ref, placed_ref, pick_ref, mix_ref, *, experts):
    rows = ids_ref.shape[1]
    capacity = placed_ref.shape[0] // experts
    relative = lax.bitwise_xor(ids_ref[...], me_ref[0])
    lane = lax.broadcasted_iota(jnp.int32, (experts, rows), 0)
    names = [lane == relative[k : k + 1] for k in range(2)]
    named = names[0] | names[1]
    row = lax.broadcasted_iota(jnp.int32, (rows, rows), 0)
    column = lax.broadcasted_iota(jnp.int32, (rows, rows), 1)
    before = jnp.dot(
        jnp.where(named, 1.0, 0.0).astype(BF16),
        jnp.where(row < column, 1.0, 0.0).astype(BF16),
        preferred_element_type=F32,
    ).astype(jnp.int32)
    slot = lax.broadcasted_iota(jnp.int32, (capacity, rows), 0)
    for d in range(experts):
        here = slice(d * capacity, (d + 1) * capacity)
        both = None
        for k in range(2):
            position = jnp.where(names[k], before, -1)
            hit = jnp.where(position[d : d + 1] == slot, 1.0, 0.0)
            pick_ref[here, k * rows : (k + 1) * rows] = hit.astype(BF16)
            both = hit if k == 0 else both + hit
        placed_ref[here, :] = both.astype(BF16)
    share = 1.0 / (1.0 + jnp.exp(logits_ref[1:2] - logits_ref[0:1]))
    share = jnp.sum(jnp.where(row == column, share, 0.0), axis=1, keepdims=True)
    mix_ref[:, 0:1] = share
    mix_ref[:, 1:2] = 1.0 - share


def place(me, expert_ids, route_logits, experts, capacity):
    rows = expert_ids.shape[0]
    return pl.pallas_call(
        functools.partial(routing_kernel, experts=experts),
        out_shape=[
            jax.ShapeDtypeStruct((experts * capacity, rows), BF16),
            jax.ShapeDtypeStruct((experts * capacity, 2 * rows), BF16),
            jax.ShapeDtypeStruct((rows, 2), F32),
        ],
        in_specs=[pl.BlockSpec(memory_space=pltpu.SMEM)]
        + [pl.BlockSpec(memory_space=pltpu.VMEM)] * 2,
        out_specs=[pl.BlockSpec(memory_space=pltpu.VMEM)] * 3,
        compiler_params=params(),
        name="routing",
    )(me.reshape(1), expert_ids.T, route_logits.T)


def dispatch_kernel(placed_ref, *refs, count, waits):
    inputs, outputs = refs[:count], refs[count + waits :]
    capacity, wide = outputs[0].shape
    width = wide // count
    for i, block in enumerate(inputs):
        for d, out in enumerate(outputs):
            out[:, i * width : (i + 1) * width] = jnp.dot(
                placed_ref[d * capacity : (d + 1) * capacity, :],
                block[...],
                preferred_element_type=F32,
            ).astype(BF16)


def dispatch(placed, slices, experts, capacity, after):
    rows, width = slices[0].shape
    wide = width * len(slices)
    return pl.pallas_call(
        functools.partial(dispatch_kernel, count=len(slices), waits=len(after)),
        out_shape=[jax.ShapeDtypeStruct((capacity, wide), BF16)] * experts,
        in_specs=[pl.BlockSpec(memory_space=pltpu.VMEM)] * (1 + len(slices))
        + [pl.BlockSpec(memory_space=pl.ANY)] * len(after),
        out_specs=[pl.BlockSpec(memory_space=pltpu.VMEM)] * experts,
        cost_estimate=cost(2 * experts * capacity * rows * wide, 6 * rows * wide),
        compiler_params=params(),
        name="dispatch",
    )(placed, *slices, *pinned(after))


def across(distance):
    return lambda column: lax.bitwise_xor(column, distance)


def everything(column):
    return 0


def prefetch_kernel(column_ref, after_ref, *refs, parts):
    half = len(refs) // 2
    copies = []
    for i, part in enumerate(parts):
        source, target, sem = refs[i], refs[half + i], refs[-1].at[i]
        count = target.shape[0]
        start = pl.multiple_of(part(column_ref[0]) * count, count)
        copies.append(pltpu.make_async_copy(source.at[0, pl.ds(start, count)], target, sem))
    for copy in copies:
        copy.start()
    for copy in copies:
        copy.wait()


def prefetch(column, fetches, after):
    sources = [pltpu.with_memory_space_constraint(w, pltpu.HBM) for w, _, _ in fetches]
    shapes = [pltpu.VMEM((count, w.shape[2]), w.dtype) for w, _, count in fetches]
    return pl.pallas_call(
        functools.partial(prefetch_kernel, parts=[part for _, part, _ in fetches]),
        out_shape=shapes,
        in_specs=[pl.BlockSpec(memory_space=pltpu.SMEM)]
        + [pl.BlockSpec(memory_space=pl.ANY)] * (1 + len(sources)),
        out_specs=[pl.BlockSpec(memory_space=pltpu.VMEM)] * len(shapes),
        scratch_shapes=[pltpu.SemaphoreType.DMA((len(shapes),))],
        cost_estimate=cost(0, sum(2 * count * w.shape[2] for w, _, count in fetches)),
        compiler_params=params(),
        name="prefetch",
    )(column.reshape(1), after, *sources)


def gate_up_kernel(*refs, experts, slices, first, last, waits):
    x_refs = refs[:experts]
    weights = refs[experts : experts + 2 * slices]
    rest = refs[experts + 2 * slices :]
    if not first:
        old_gate, old_up = rest[:2]
        rest = rest[2:]
    rest = rest[waits:]
    x = jnp.concatenate([r[...] for r in x_refs], axis=0)
    width, hidden = weights[0].shape
    tile = min(512, hidden)
    for n in range(hidden // tile):
        columns = slice(n * tile, (n + 1) * tile)
        sums = []
        for kind in range(2):
            total = None if first else (old_gate, old_up)[kind][:, columns]
            for i in range(slices):
                term = jnp.dot(
                    x[:, i * width : (i + 1) * width],
                    weights[2 * i + kind][:, columns],
                    preferred_element_type=F32,
                )
                total = term if total is None else total + term
            sums.append(total)
        gate, up = sums
        if last:
            rest[0][:, columns] = (gate / (1.0 + jnp.exp(-gate)) * up).astype(BF16)
        else:
            rest[0][:, columns] = gate
            rest[1][:, columns] = up


def gate_up(x_blocks, weights, sums, last, after):
    experts = len(x_blocks)
    rows = experts * x_blocks[0].shape[0]
    hidden = weights[0].shape[1]
    first = sums is None
    old = [] if first else pinned(sums)
    before = experts + len(weights)
    if last:
        out_shape = [pltpu.VMEM((rows, hidden), BF16)]
    else:
        out_shape = [pltpu.VMEM((rows, hidden), F32)] * 2
    return pl.pallas_call(
        functools.partial(
            gate_up_kernel,
            experts=experts,
            slices=len(weights) // 2,
            first=first,
            last=last,
            waits=len(after),
        ),
        out_shape=out_shape,
        in_specs=[pl.BlockSpec(memory_space=pltpu.VMEM)] * (before + len(old))
        + [pl.BlockSpec(memory_space=pl.ANY)] * len(after),
        out_specs=[pl.BlockSpec(memory_space=pltpu.VMEM)] * len(out_shape),
        input_output_aliases={} if first or last else {before: 0, before + 1: 1},
        cost_estimate=cost(
            2 * rows * hidden * sum(w.shape[0] for w in weights),
            sum(2 * w.size for w in weights),
        ),
        compiler_params=params(),
        name="gate_up",
    )(*x_blocks, *pinned(weights), *old, *after)


def down_kernel(column_ref, h_ref, w_ref, *refs, part, waits):
    out_refs = refs[waits:]
    capacity, width = out_refs[0].shape
    tile = min(256, width)
    for n in range(width // tile):
        start = pl.multiple_of(part(column_ref[0]) * width + n * tile, tile)
        y = jnp.dot(h_ref[...], w_ref[0, :, pl.ds(start, tile)], preferred_element_type=F32)
        columns = slice(n * tile, (n + 1) * tile)
        for d, out in enumerate(out_refs):
            out[:, columns] = y[d * capacity : (d + 1) * capacity].astype(BF16)


def down(column, part, hidden, down_w, width, experts, after):
    rows, depth = hidden.shape
    capacity = rows // experts
    return pl.pallas_call(
        functools.partial(down_kernel, part=part, waits=len(after)),
        out_shape=[jax.ShapeDtypeStruct((capacity, width), BF16)] * experts,
        in_specs=[pl.BlockSpec(memory_space=pltpu.SMEM)]
        + [pl.BlockSpec(memory_space=pltpu.VMEM)] * 2
        + [pl.BlockSpec(memory_space=pl.ANY)] * len(after),
        out_specs=[pl.BlockSpec(memory_space=pltpu.VMEM)] * experts,
        cost_estimate=cost(2 * rows * depth * width, 2 * depth * width + 2 * rows * width),
        compiler_params=params(),
        name="down",
    )(column.reshape(1), *pinned([hidden, down_w]), *after)


def combine_kernel(pick_ref, mix_ref, *refs, experts):
    y_refs, added, out = refs[:experts], refs[experts:-1], refs[-1]
    rows = out.shape[0]
    y = jnp.concatenate([r[...] for r in y_refs], axis=0)
    picked = lax.dot_general(
        pick_ref[...], y, (((0,), (0,)), ((), ())), preferred_element_type=F32
    )
    mixed = picked[:rows] * mix_ref[:, 0:1] + picked[rows:] * mix_ref[:, 1:2]
    for other in added:
        mixed = mixed + other[...].astype(F32)
    out[...] = mixed.astype(BF16)


def combine(pick, mix, blocks, added):
    rows = mix.shape[0]
    width = blocks[0].shape[1]
    operands = 2 + len(blocks) + len(added)
    return pl.pallas_call(
        functools.partial(combine_kernel, experts=len(blocks)),
        out_shape=jax.ShapeDtypeStruct((rows, width), BF16),
        in_specs=[pl.BlockSpec(memory_space=pltpu.VMEM)] * operands,
        out_specs=pl.BlockSpec(memory_space=pltpu.VMEM),
        cost_estimate=cost(4 * rows * pick.shape[0] * width, 6 * rows * width),
        compiler_params=params(),
        name="combine",
    )(pick, mix, *blocks, *added)


def swap(value, axis, distance):
    if not distance:
        return value
    count = lax.axis_size(axis)
    return lax.ppermute(value, axis, [(i, i ^ distance) for i in range(count)])


def per_device(tokens, expert_ids, route_logits, gate_weight, up_weight, down_weight):
    rows, own_width = tokens.shape
    experts = lax.axis_size("expert")
    shards = lax.axis_size("tensor")
    capacity = rows // 2
    me = lax.axis_index("expert").astype(jnp.int32)
    column = lax.axis_index("tensor").astype(jnp.int32)
    doubling = shards == 4
    width = own_width if doubling else own_width * shards

    if doubling:
        across_two = swap(tokens, "tensor", 2)
        slices = [tokens, swap(tokens, "tensor", 1), across_two, swap(across_two, "tensor", 1)]
        parts = [across(distance) for distance in range(4)]
        groups = [[0, 1], [2], [3]]
    else:
        slices = [lax.all_gather(tokens, "tensor", axis=1, tiled=True)]
        parts = [everything]
        groups = [[0]]
    placed, pick, mix = place(me, expert_ids, route_logits, experts, capacity)

    def fetch(chosen, after):
        fetches = [(w, parts[i], width) for i in chosen for w in (gate_weight, up_weight)]
        return list(prefetch(column, fetches, after))

    weights, arrived = fetch(groups[0], placed), []
    for group in groups:
        after = weights[-1:] if len(arrived) < 2 else []
        outgoing = dispatch(placed, [slices[i] for i in group], experts, capacity, after)
        arrived.append([swap(block, "expert", e) for e, block in enumerate(outgoing)])
        if len(arrived) == 1 and len(groups) > 1:
            weights += fetch([2, 3], outgoing[0])
    sums = None
    for group, x_blocks in zip(groups, arrived):
        chosen = weights[2 * group[0] : 2 * group[-1] + 2]
        after = arrived[1][1:2] if sums is None and len(groups) > 1 else []
        sums = gate_up(x_blocks, chosen, sums, group is groups[-1], after)
    hidden = sums[0]

    def returned(part, after=()):
        terms = down(column, part, hidden, down_weight, width, experts, after)
        return [swap(block, "expert", e) for e, block in enumerate(terms)]

    if not doubling:
        mixed = combine(pick, mix, returned(everything), [])
        return lax.psum_scatter(mixed, "tensor", scatter_dimension=1, tiled=True)
    sums, mixtures = [], []
    for distance in (3, 2, 1):
        blocks = returned(across(distance), mixtures[-2:-1])
        mixtures.append(combine(pick, mix, blocks, []))
        sums.append(swap(mixtures[-1], "tensor", distance))
    return combine(pick, mix, returned(across(0), sums[:1]), sums[::-1])


def solution(mesh):
    in_specs = (
        P(("groups", "expert"), "tensor"),
        P(("groups", "expert"), None),
        P(("groups", "expert"), None),
        P("expert", None, "tensor"),
        P("expert", None, "tensor"),
        P("expert", "tensor", None),
    )
    out_specs = P(("groups", "expert"), "tensor")
    return jax.shard_map(
        per_device, mesh=mesh, in_specs=in_specs, out_specs=out_specs, check_vma=False
    )
```

```python
import functools

import jax
import jax.numpy as jnp
from jax import lax
from jax.experimental import pallas as pl
from jax.experimental.pallas import tpu as pltpu
from jax.sharding import PartitionSpec as P

F32 = jnp.float32
BF16 = jnp.bfloat16
MIB = 1024 * 1024


def params(mib=6):
    return pltpu.CompilerParams(vmem_limit_bytes=mib * MIB)


def cost(flops, moved):
    return pl.CostEstimate(flops=flops, bytes_accessed=moved, transcendentals=0)


def pinned(arrays):
    return [pltpu.with_memory_space_constraint(array, pltpu.VMEM) for array in arrays]


def routing_kernel(
    me_ref, ids_ref, logits_ref, after_ref, placed_ref, pick_ref, mix_ref, *, experts
):
    rows = ids_ref.shape[1]
    capacity = placed_ref.shape[0] // experts
    relative = lax.bitwise_xor(ids_ref[...], me_ref[0])
    lane = lax.broadcasted_iota(jnp.int32, (experts, rows), 0)
    names = [lane == relative[k : k + 1] for k in range(2)]
    named = names[0] | names[1]
    row = lax.broadcasted_iota(jnp.int32, (rows, rows), 0)
    column = lax.broadcasted_iota(jnp.int32, (rows, rows), 1)
    before = jnp.dot(
        jnp.where(named, 1.0, 0.0).astype(BF16),
        jnp.where(row < column, 1.0, 0.0).astype(BF16),
        preferred_element_type=F32,
    ).astype(jnp.int32)
    slot = lax.broadcasted_iota(jnp.int32, (capacity, rows), 0)
    for d in range(experts):
        here = slice(d * capacity, (d + 1) * capacity)
        both = None
        for k in range(2):
            position = jnp.where(names[k], before, -1)
            hit = jnp.where(position[d : d + 1] == slot, 1.0, 0.0)
            pick_ref[here, k * rows : (k + 1) * rows] = hit.astype(BF16)
            both = hit if k == 0 else both + hit
        placed_ref[here, :] = both.astype(BF16)
    share = 1.0 / (1.0 + jnp.exp(logits_ref[1:2] - logits_ref[0:1]))
    share = jnp.sum(jnp.where(row == column, share, 0.0), axis=1, keepdims=True)
    mix_ref[:, 0:1] = share
    mix_ref[:, 1:2] = 1.0 - share


def place(me, expert_ids, route_logits, experts, capacity, after):
    rows = expert_ids.shape[0]
    return pl.pallas_call(
        functools.partial(routing_kernel, experts=experts),
        out_shape=[
            jax.ShapeDtypeStruct((experts * capacity, rows), BF16),
            jax.ShapeDtypeStruct((experts * capacity, 2 * rows), BF16),
            jax.ShapeDtypeStruct((rows, 2), F32),
        ],
        in_specs=[pl.BlockSpec(memory_space=pltpu.SMEM)]
        + [pl.BlockSpec(memory_space=pltpu.VMEM)] * 2
        + [pl.BlockSpec(memory_space=pl.ANY)],
        out_specs=[pl.BlockSpec(memory_space=pltpu.VMEM)] * 3,
        compiler_params=params(),
        name="routing",
    )(me.reshape(1), expert_ids.T, route_logits.T, *pinned([after]))


def dispatch_kernel(placed_ref, *refs, count, waits):
    inputs, outputs = refs[:count], refs[count + waits :]
    capacity, wide = outputs[0].shape
    width = wide // count
    for i, block in enumerate(inputs):
        for d, out in enumerate(outputs):
            out[:, i * width : (i + 1) * width] = jnp.dot(
                placed_ref[d * capacity : (d + 1) * capacity, :],
                block[...],
                preferred_element_type=F32,
            ).astype(BF16)


def dispatch(placed, slices, experts, capacity, after):
    rows, width = slices[0].shape
    wide = width * len(slices)
    return pl.pallas_call(
        functools.partial(dispatch_kernel, count=len(slices), waits=len(after)),
        out_shape=[jax.ShapeDtypeStruct((capacity, wide), BF16)] * experts,
        in_specs=[pl.BlockSpec(memory_space=pltpu.VMEM)] * (1 + len(slices))
        + [pl.BlockSpec(memory_space=pl.ANY)] * len(after),
        out_specs=[pl.BlockSpec(memory_space=pltpu.VMEM)] * experts,
        cost_estimate=cost(2 * experts * capacity * rows * wide, 6 * rows * wide),
        compiler_params=params(),
        name="dispatch",
    )(placed, *slices, *pinned(after))


def across(distance):
    return lambda column: lax.bitwise_xor(column, distance)


def everything(column):
    return 0


def prefetch_kernel(column_ref, after_ref, *refs, parts):
    half = len(refs) // 2
    copies = []
    for i, part in enumerate(parts):
        source, target, sem = refs[i], refs[half + i], refs[-1].at[i]
        count = target.shape[0]
        start = pl.multiple_of(part(column_ref[0]) * count, count)
        copies.append(pltpu.make_async_copy(source.at[0, pl.ds(start, count)], target, sem))
    for copy in copies:
        copy.start()
    for copy in copies:
        copy.wait()


def prefetch(column, fetches, after):
    sources = [pltpu.with_memory_space_constraint(w, pltpu.HBM) for w, _, _ in fetches]
    shapes = [pltpu.VMEM((count, w.shape[2]), w.dtype) for w, _, count in fetches]
    return pl.pallas_call(
        functools.partial(prefetch_kernel, parts=[part for _, part, _ in fetches]),
        out_shape=shapes,
        in_specs=[pl.BlockSpec(memory_space=pltpu.SMEM)]
        + [pl.BlockSpec(memory_space=pl.ANY)] * (1 + len(sources)),
        out_specs=[pl.BlockSpec(memory_space=pltpu.VMEM)] * len(shapes),
        scratch_shapes=[pltpu.SemaphoreType.DMA((len(shapes),))],
        cost_estimate=cost(0, sum(2 * count * w.shape[2] for w, _, count in fetches)),
        compiler_params=params(),
        name="prefetch",
    )(column.reshape(1), after, *sources)


def gate_up_kernel(*refs, experts, slices, first, last, waits):
    x_refs = refs[:experts]
    weights = refs[experts : experts + 2 * slices]
    rest = refs[experts + 2 * slices :]
    if not first:
        old_gate, old_up = rest[:2]
        rest = rest[2:]
    rest = rest[waits:]
    x = jnp.concatenate([r[...] for r in x_refs], axis=0)
    width, hidden = weights[0].shape
    tile = min(512, hidden)
    for n in range(hidden // tile):
        columns = slice(n * tile, (n + 1) * tile)
        sums = []
        for kind in range(2):
            total = None if first else (old_gate, old_up)[kind][:, columns]
            for i in range(slices):
                term = jnp.dot(
                    x[:, i * width : (i + 1) * width],
                    weights[2 * i + kind][:, columns],
                    preferred_element_type=F32,
                )
                total = term if total is None else total + term
            sums.append(total)
        gate, up = sums
        if last:
            rest[0][:, columns] = (gate / (1.0 + jnp.exp(-gate)) * up).astype(BF16)
        else:
            rest[0][:, columns] = gate
            rest[1][:, columns] = up


def gate_up(x_blocks, weights, sums, last, after):
    experts = len(x_blocks)
    rows = experts * x_blocks[0].shape[0]
    hidden = weights[0].shape[1]
    first = sums is None
    old = [] if first else pinned(sums)
    before = experts + len(weights)
    if last:
        out_shape = [pltpu.VMEM((rows, hidden), BF16)]
    else:
        out_shape = [pltpu.VMEM((rows, hidden), F32)] * 2
    return pl.pallas_call(
        functools.partial(
            gate_up_kernel,
            experts=experts,
            slices=len(weights) // 2,
            first=first,
            last=last,
            waits=len(after),
        ),
        out_shape=out_shape,
        in_specs=[pl.BlockSpec(memory_space=pltpu.VMEM)] * (before + len(old))
        + [pl.BlockSpec(memory_space=pl.ANY)] * len(after),
        out_specs=[pl.BlockSpec(memory_space=pltpu.VMEM)] * len(out_shape),
        input_output_aliases={} if first or last else {before: 0, before + 1: 1},
        cost_estimate=cost(
            2 * rows * hidden * sum(w.shape[0] for w in weights),
            sum(2 * w.size for w in weights),
        ),
        compiler_params=params(),
        name="gate_up",
    )(*x_blocks, *pinned(weights), *old, *after)


def down_kernel(column_ref, h_ref, w_ref, *refs, part, waits):
    out_refs = refs[waits:]
    capacity, width = out_refs[0].shape
    tile = min(256, width)
    for n in range(width // tile):
        start = pl.multiple_of(part(column_ref[0]) * width + n * tile, tile)
        y = jnp.dot(h_ref[...], w_ref[0, :, pl.ds(start, tile)], preferred_element_type=F32)
        columns = slice(n * tile, (n + 1) * tile)
        for d, out in enumerate(out_refs):
            out[:, columns] = y[d * capacity : (d + 1) * capacity].astype(BF16)


def down(column, part, hidden, down_w, width, experts, after):
    rows, depth = hidden.shape
    capacity = rows // experts
    return pl.pallas_call(
        functools.partial(down_kernel, part=part, waits=len(after)),
        out_shape=[jax.ShapeDtypeStruct((capacity, width), BF16)] * experts,
        in_specs=[pl.BlockSpec(memory_space=pltpu.SMEM)]
        + [pl.BlockSpec(memory_space=pltpu.VMEM)] * 2
        + [pl.BlockSpec(memory_space=pl.ANY)] * len(after),
        out_specs=[pl.BlockSpec(memory_space=pltpu.VMEM)] * experts,
        cost_estimate=cost(2 * rows * depth * width, 2 * depth * width + 2 * rows * width),
        compiler_params=params(),
        name="down",
    )(column.reshape(1), *pinned([hidden, down_w]), *after)


def combine_kernel(pick_ref, mix_ref, *refs, experts, sums):
    y_refs, added, out = refs[:experts], refs[experts : experts + sums], refs[-1]
    rows = out.shape[0]
    y = jnp.concatenate([r[...] for r in y_refs], axis=0)
    picked = lax.dot_general(
        pick_ref[...], y, (((0,), (0,)), ((), ())), preferred_element_type=F32
    )
    mixed = picked[:rows] * mix_ref[:, 0:1] + picked[rows:] * mix_ref[:, 1:2]
    for other in added:
        mixed = mixed + other[...].astype(F32)
    out[...] = mixed.astype(BF16)


def combine(pick, mix, blocks, added, after=()):
    rows = mix.shape[0]
    width = blocks[0].shape[1]
    operands = 2 + len(blocks) + len(added)
    return pl.pallas_call(
        functools.partial(combine_kernel, experts=len(blocks), sums=len(added)),
        out_shape=jax.ShapeDtypeStruct((rows, width), BF16),
        in_specs=[pl.BlockSpec(memory_space=pltpu.VMEM)] * operands
        + [pl.BlockSpec(memory_space=pl.ANY)] * len(after),
        out_specs=pl.BlockSpec(memory_space=pltpu.VMEM),
        cost_estimate=cost(4 * rows * pick.shape[0] * width, 6 * rows * width),
        compiler_params=params(),
        name="combine",
    )(pick, mix, *blocks, *added, *after)


def swap(value, axis, distance):
    if not distance:
        return value
    count = lax.axis_size(axis)
    return lax.ppermute(value, axis, [(i, i ^ distance) for i in range(count)])


def per_device(tokens, expert_ids, route_logits, gate_weight, up_weight, down_weight):
    rows, own_width = tokens.shape
    experts = lax.axis_size("expert")
    shards = lax.axis_size("tensor")
    capacity = rows // 2
    me = lax.axis_index("expert").astype(jnp.int32)
    column = lax.axis_index("tensor").astype(jnp.int32)
    doubling = shards == 4
    width = own_width if doubling else own_width * shards

    if doubling:
        across_two = swap(tokens, "tensor", 2)
        slices = [tokens, swap(tokens, "tensor", 1), across_two, swap(across_two, "tensor", 1)]
        parts = [across(distance) for distance in range(4)]
        groups = [[0, 1], [2], [3]]
    else:
        slices = [lax.all_gather(tokens, "tensor", axis=1, tiled=True)]
        parts = [everything]
        groups = [[0]]

    def fetch(chosen, after):
        fetches = [(w, parts[i], width) for i in chosen for w in (gate_weight, up_weight)]
        return list(prefetch(column, fetches, after))

    weights, arrived = fetch(range(len(parts))[:3], tokens), []
    placed, pick, mix = place(me, expert_ids, route_logits, experts, capacity, weights[0])
    for group in groups:
        after = weights[-1:] if len(arrived) < 2 else []
        outgoing = dispatch(placed, [slices[i] for i in group], experts, capacity, after)
        arrived.append([swap(block, "expert", e) for e, block in enumerate(outgoing)])
        if len(arrived) == 1 and len(groups) > 1:
            weights += fetch([3], outgoing[0])
    sums = None
    for group, x_blocks in zip(groups, arrived):
        chosen = weights[2 * group[0] : 2 * group[-1] + 2]
        after = arrived[1][1:2] if sums is None and len(groups) > 1 else []
        sums = gate_up(x_blocks, chosen, sums, group is groups[-1], after)
    hidden = sums[0]

    def returned(part, after=()):
        terms = down(column, part, hidden, down_weight, width, experts, after)
        return [swap(block, "expert", e) for e, block in enumerate(terms)]

    if not doubling:
        mixed = combine(pick, mix, returned(everything), [])
        return lax.psum_scatter(mixed, "tensor", scatter_dimension=1, tiled=True)
    passed = swap(combine(pick, mix, returned(across(3)), []), "tensor", 1)
    over = swap(combine(pick, mix, returned(across(2)), [passed]), "tensor", 2)
    near = returned(across(1), [passed])
    own = returned(across(0), [passed])
    beside = swap(combine(pick, mix, near, [], own[1:2]), "tensor", 1)
    return combine(pick, mix, own, [beside, over])


def solution(mesh):
    in_specs = (
        P(("groups", "expert"), "tensor"),
        P(("groups", "expert"), None),
        P(("groups", "expert"), None),
        P("expert", None, "tensor"),
        P("expert", None, "tensor"),
        P("expert", "tensor", None),
    )
    out_specs = P(("groups", "expert"), "tensor")
    return jax.shard_map(
        per_device, mesh=mesh, in_specs=in_specs, out_specs=out_specs, check_vma=False
    )
```

```python
import functools

import jax
import jax.numpy as jnp
from jax import lax
from jax.experimental import pallas as pl
from jax.experimental.pallas import tpu as pltpu
from jax.sharding import PartitionSpec as P

F32 = jnp.float32
BF16 = jnp.bfloat16
MIB = 1024 * 1024


def params(mib=6):
    return pltpu.CompilerParams(vmem_limit_bytes=mib * MIB)


def cost(flops, moved):
    return pl.CostEstimate(flops=flops, bytes_accessed=moved, transcendentals=0)


def pinned(arrays):
    return [pltpu.with_memory_space_constraint(array, pltpu.VMEM) for array in arrays]


def routing_kernel(me_ref, ids_ref, logits_ref, placed_ref, pick_ref, mix_ref, *, experts):
    rows = ids_ref.shape[1]
    capacity = placed_ref.shape[0] // experts
    relative = lax.bitwise_xor(ids_ref[...], me_ref[0])
    lane = lax.broadcasted_iota(jnp.int32, (experts, rows), 0)
    names = [lane == relative[k : k + 1] for k in range(2)]
    named = names[0] | names[1]
    row = lax.broadcasted_iota(jnp.int32, (rows, rows), 0)
    column = lax.broadcasted_iota(jnp.int32, (rows, rows), 1)
    before = jnp.dot(
        jnp.where(named, 1.0, 0.0).astype(BF16),
        jnp.where(row < column, 1.0, 0.0).astype(BF16),
        preferred_element_type=F32,
    ).astype(jnp.int32)
    slot = lax.broadcasted_iota(jnp.int32, (capacity, rows), 0)
    for d in range(experts):
        here = slice(d * capacity, (d + 1) * capacity)
        both = None
        for k in range(2):
            position = jnp.where(names[k], before, -1)
            hit = jnp.where(position[d : d + 1] == slot, 1.0, 0.0)
            pick_ref[here, k * rows : (k + 1) * rows] = hit.astype(BF16)
            both = hit if k == 0 else both + hit
        placed_ref[here, :] = both.astype(BF16)
    share = 1.0 / (1.0 + jnp.exp(logits_ref[1:2] - logits_ref[0:1]))
    share = jnp.sum(jnp.where(row == column, share, 0.0), axis=1, keepdims=True)
    mix_ref[:, 0:1] = share
    mix_ref[:, 1:2] = 1.0 - share


def place(me, expert_ids, route_logits, experts, capacity):
    rows = expert_ids.shape[0]
    return pl.pallas_call(
        functools.partial(routing_kernel, experts=experts),
        out_shape=[
            jax.ShapeDtypeStruct((experts * capacity, rows), BF16),
            jax.ShapeDtypeStruct((experts * capacity, 2 * rows), BF16),
            jax.ShapeDtypeStruct((rows, 2), F32),
        ],
        in_specs=[pl.BlockSpec(memory_space=pltpu.SMEM)]
        + [pl.BlockSpec(memory_space=pltpu.VMEM)] * 2,
        out_specs=[pl.BlockSpec(memory_space=pltpu.VMEM)] * 3,
        compiler_params=params(),
        name="routing",
    )(me.reshape(1), expert_ids.T, route_logits.T)


def dispatch_kernel(placed_ref, *refs, count, waits):
    inputs, outputs = refs[:count], refs[count + waits :]
    capacity, wide = outputs[0].shape
    width = wide // count
    for i, block in enumerate(inputs):
        for d, out in enumerate(outputs):
            out[:, i * width : (i + 1) * width] = jnp.dot(
                placed_ref[d * capacity : (d + 1) * capacity, :],
                block[...],
                preferred_element_type=F32,
            ).astype(BF16)


def dispatch(placed, slices, experts, capacity, after):
    rows, width = slices[0].shape
    wide = width * len(slices)
    return pl.pallas_call(
        functools.partial(dispatch_kernel, count=len(slices), waits=len(after)),
        out_shape=[jax.ShapeDtypeStruct((capacity, wide), BF16)] * experts,
        in_specs=[pl.BlockSpec(memory_space=pltpu.VMEM)] * (1 + len(slices))
        + [pl.BlockSpec(memory_space=pl.ANY)] * len(after),
        out_specs=[pl.BlockSpec(memory_space=pltpu.VMEM)] * experts,
        cost_estimate=cost(2 * experts * capacity * rows * wide, 6 * rows * wide),
        compiler_params=params(),
        name="dispatch",
    )(placed, *slices, *pinned(after))


def across(distance):
    return lambda column: lax.bitwise_xor(column, distance)


def everything(column):
    return 0


def prefetch_kernel(column_ref, after_ref, *refs, parts):
    half = len(refs) // 2
    copies = []
    for i, part in enumerate(parts):
        source, target, sem = refs[i], refs[half + i], refs[-1].at[i]
        count = target.shape[0]
        start = pl.multiple_of(part(column_ref[0]) * count, count)
        copies.append(pltpu.make_async_copy(source.at[0, pl.ds(start, count)], target, sem))
    for copy in copies:
        copy.start()
    for copy in copies:
        copy.wait()


def prefetch(column, fetches, after):
    sources = [pltpu.with_memory_space_constraint(w, pltpu.HBM) for w, _, _ in fetches]
    shapes = [pltpu.VMEM((count, w.shape[2]), w.dtype) for w, _, count in fetches]
    return pl.pallas_call(
        functools.partial(prefetch_kernel, parts=[part for _, part, _ in fetches]),
        out_shape=shapes,
        in_specs=[pl.BlockSpec(memory_space=pltpu.SMEM)]
        + [pl.BlockSpec(memory_space=pl.ANY)] * (1 + len(sources)),
        out_specs=[pl.BlockSpec(memory_space=pltpu.VMEM)] * len(shapes),
        scratch_shapes=[pltpu.SemaphoreType.DMA((len(shapes),))],
        cost_estimate=cost(0, sum(2 * count * w.shape[2] for w, _, count in fetches)),
        compiler_params=params(),
        name="prefetch",
    )(column.reshape(1), after, *sources)


def gate_up_kernel(*refs, experts, slices, first, last, waits):
    x_refs = refs[:experts]
    weights = refs[experts : experts + 2 * slices]
    rest = refs[experts + 2 * slices :]
    if not first:
        old_gate, old_up = rest[:2]
        rest = rest[2:]
    rest = rest[waits:]
    x = jnp.concatenate([r[...] for r in x_refs], axis=0)
    width, hidden = weights[0].shape
    tile = min(512, hidden)
    for n in range(hidden // tile):
        columns = slice(n * tile, (n + 1) * tile)
        sums = []
        for kind in range(2):
            total = None if first else (old_gate, old_up)[kind][:, columns]
            for i in range(slices):
                term = jnp.dot(
                    x[:, i * width : (i + 1) * width],
                    weights[2 * i + kind][:, columns],
                    preferred_element_type=F32,
                )
                total = term if total is None else total + term
            sums.append(total)
        gate, up = sums
        if last:
            rest[0][:, columns] = (gate / (1.0 + jnp.exp(-gate)) * up).astype(BF16)
        else:
            rest[0][:, columns] = gate
            rest[1][:, columns] = up


def gate_up(x_blocks, weights, sums, last, after):
    experts = len(x_blocks)
    rows = experts * x_blocks[0].shape[0]
    hidden = weights[0].shape[1]
    first = sums is None
    old = [] if first else pinned(sums)
    before = experts + len(weights)
    if last:
        out_shape = [pltpu.VMEM((rows, hidden), BF16)]
    else:
        out_shape = [pltpu.VMEM((rows, hidden), F32)] * 2
    return pl.pallas_call(
        functools.partial(
            gate_up_kernel,
            experts=experts,
            slices=len(weights) // 2,
            first=first,
            last=last,
            waits=len(after),
        ),
        out_shape=out_shape,
        in_specs=[pl.BlockSpec(memory_space=pltpu.VMEM)] * (before + len(old))
        + [pl.BlockSpec(memory_space=pl.ANY)] * len(after),
        out_specs=[pl.BlockSpec(memory_space=pltpu.VMEM)] * len(out_shape),
        input_output_aliases={} if first or last else {before: 0, before + 1: 1},
        cost_estimate=cost(
            2 * rows * hidden * sum(w.shape[0] for w in weights),
            sum(2 * w.size for w in weights),
        ),
        compiler_params=params(),
        name="gate_up",
    )(*x_blocks, *pinned(weights), *old, *after)


def down_kernel(column_ref, h_ref, w_ref, *refs, part, waits):
    out_refs = refs[waits:]
    capacity, width = out_refs[0].shape
    tile = min(256, width)
    for n in range(width // tile):
        start = pl.multiple_of(part(column_ref[0]) * width + n * tile, tile)
        y = jnp.dot(h_ref[...], w_ref[0, :, pl.ds(start, tile)], preferred_element_type=F32)
        columns = slice(n * tile, (n + 1) * tile)
        for d, out in enumerate(out_refs):
            out[:, columns] = y[d * capacity : (d + 1) * capacity].astype(BF16)


def down(column, part, hidden, down_w, width, experts, after):
    rows, depth = hidden.shape
    capacity = rows // experts
    return pl.pallas_call(
        functools.partial(down_kernel, part=part, waits=len(after)),
        out_shape=[jax.ShapeDtypeStruct((capacity, width), BF16)] * experts,
        in_specs=[pl.BlockSpec(memory_space=pltpu.SMEM)]
        + [pl.BlockSpec(memory_space=pltpu.VMEM)] * 2
        + [pl.BlockSpec(memory_space=pl.ANY)] * len(after),
        out_specs=[pl.BlockSpec(memory_space=pltpu.VMEM)] * experts,
        cost_estimate=cost(2 * rows * depth * width, 2 * depth * width + 2 * rows * width),
        compiler_params=params(),
        name="down",
    )(column.reshape(1), *pinned([hidden, down_w]), *after)


def combine_kernel(pick_ref, mix_ref, *refs, experts, starts):
    y_refs, added = refs[:experts], refs[experts : experts + len(starts)]
    outs = refs[experts + len(starts) :]
    width = y_refs[0].shape[1]
    rows, part = outs[0].shape
    y = jnp.concatenate([r[...] for r in y_refs], axis=0)
    picked = lax.dot_general(
        pick_ref[...], y, (((0,), (0,)), ((), ())), preferred_element_type=F32
    )
    mixed = picked[:rows] * mix_ref[:, 0:1] + picked[rows:] * mix_ref[:, 1:2]
    for other, start in zip(added, starts):
        value = other[...].astype(F32)
        stop = start + value.shape[1]
        pieces = [mixed[:, :start]] * (start > 0) + [mixed[:, start:stop] + value]
        pieces += [mixed[:, stop:]] * (stop < width)
        mixed = jnp.concatenate(pieces, axis=1) if len(pieces) > 1 else pieces[0]
    for i, out in enumerate(outs):
        out[...] = mixed[:, i * part : (i + 1) * part].astype(BF16)


def combine(pick, mix, blocks, added, cuts=1):
    rows = mix.shape[0]
    width = blocks[0].shape[1]
    operands = 2 + len(blocks) + len(added)
    return pl.pallas_call(
        functools.partial(
            combine_kernel, experts=len(blocks), starts=[start for _, start in added]
        ),
        out_shape=[jax.ShapeDtypeStruct((rows, width // cuts), BF16)] * cuts,
        in_specs=[pl.BlockSpec(memory_space=pltpu.VMEM)] * operands,
        out_specs=[pl.BlockSpec(memory_space=pltpu.VMEM)] * cuts,
        cost_estimate=cost(4 * rows * pick.shape[0] * width, 6 * rows * width),
        compiler_params=params(),
        name="combine",
    )(pick, mix, *blocks, *[array for array, _ in added])


def swap(value, axis, distance):
    if not distance:
        return value
    count = lax.axis_size(axis)
    return lax.ppermute(value, axis, [(i, i ^ distance) for i in range(count)])


def per_device(tokens, expert_ids, route_logits, gate_weight, up_weight, down_weight):
    rows, own_width = tokens.shape
    experts = lax.axis_size("expert")
    shards = lax.axis_size("tensor")
    capacity = rows // 2
    me = lax.axis_index("expert").astype(jnp.int32)
    column = lax.axis_index("tensor").astype(jnp.int32)
    doubling = shards == 4
    width = own_width if doubling else own_width * shards

    if doubling:
        across_two = swap(tokens, "tensor", 2)
        slices = [tokens, swap(tokens, "tensor", 1), across_two, swap(across_two, "tensor", 1)]
        parts = [across(distance) for distance in range(4)]
        groups = [[0, 1], [2], [3]]
    else:
        slices = [lax.all_gather(tokens, "tensor", axis=1, tiled=True)]
        parts = [everything]
        groups = [[0]]
    placed, pick, mix = place(me, expert_ids, route_logits, experts, capacity)

    def fetch(chosen, after):
        fetches = [(w, parts[i], width) for i in chosen for w in (gate_weight, up_weight)]
        return list(prefetch(column, fetches, after))

    weights, arrived = fetch(groups[0], placed), []
    for group in groups:
        after = weights[-1:] if len(arrived) < 2 else []
        outgoing = dispatch(placed, [slices[i] for i in group], experts, capacity, after)
        arrived.append([swap(block, "expert", e) for e, block in enumerate(outgoing)])
        if len(arrived) == 1 and len(groups) > 1:
            weights += fetch([2, 3], outgoing[0])
    sums = None
    for group, x_blocks in zip(groups, arrived):
        chosen = weights[2 * group[0] : 2 * group[-1] + 2]
        after = arrived[1][1:2] if sums is None and len(groups) > 1 else []
        sums = gate_up(x_blocks, chosen, sums, group is groups[-1], after)
    hidden = sums[0]

    def returned(part, after=()):
        terms = down(column, part, hidden, down_weight, width, experts, after)
        return [swap(block, "expert", e) for e, block in enumerate(terms)]

    if not doubling:
        mixed = combine(pick, mix, returned(everything), [])[0]
        return lax.psum_scatter(mixed, "tensor", scatter_dimension=1, tiled=True)
    low, high = combine(pick, mix, returned(across(3)), [], cuts=2)
    passed = swap(low, "tensor", 1)
    far = (swap(high, "tensor", 3), width // 2)
    over = (swap(combine(pick, mix, returned(across(2)), [(passed, 0)])[0], "tensor", 2), 0)
    beside = (swap(combine(pick, mix, returned(across(1), [low]), [])[0], "tensor", 1), 0)
    return combine(pick, mix, returned(across(0), [far[0]]), [beside, over, far])[0]


def solution(mesh):
    in_specs = (
        P(("groups", "expert"), "tensor"),
        P(("groups", "expert"), None),
        P(("groups", "expert"), None),
        P("expert", None, "tensor"),
        P("expert", None, "tensor"),
        P("expert", "tensor", None),
    )
    out_specs = P(("groups", "expert"), "tensor")
    return jax.shard_map(
        per_device, mesh=mesh, in_specs=in_specs, out_specs=out_specs, check_vma=False
    )
```

```python
import functools

import jax
import jax.numpy as jnp
from jax import lax
from jax.experimental import pallas as pl
from jax.experimental.pallas import tpu as pltpu
from jax.sharding import PartitionSpec as P

F32 = jnp.float32
BF16 = jnp.bfloat16
MIB = 1024 * 1024


def params(mib=6):
    return pltpu.CompilerParams(vmem_limit_bytes=mib * MIB)


def cost(flops, moved):
    return pl.CostEstimate(flops=flops, bytes_accessed=moved, transcendentals=0)


def pinned(arrays):
    return [pltpu.with_memory_space_constraint(array, pltpu.VMEM) for array in arrays]


def routing_kernel(me_ref, ids_ref, logits_ref, placed_ref, pick_ref, mix_ref, *, experts):
    rows = ids_ref.shape[1]
    capacity = placed_ref.shape[0] // experts
    relative = lax.bitwise_xor(ids_ref[...], me_ref[0])
    lane = lax.broadcasted_iota(jnp.int32, (experts, rows), 0)
    names = [lane == relative[k : k + 1] for k in range(2)]
    named = names[0] | names[1]
    row = lax.broadcasted_iota(jnp.int32, (rows, rows), 0)
    column = lax.broadcasted_iota(jnp.int32, (rows, rows), 1)
    before = jnp.dot(
        jnp.where(named, 1.0, 0.0).astype(BF16),
        jnp.where(row < column, 1.0, 0.0).astype(BF16),
        preferred_element_type=F32,
    ).astype(jnp.int32)
    slot = lax.broadcasted_iota(jnp.int32, (capacity, rows), 0)
    for d in range(experts):
        here = slice(d * capacity, (d + 1) * capacity)
        both = None
        for k in range(2):
            position = jnp.where(names[k], before, -1)
            hit = jnp.where(position[d : d + 1] == slot, 1.0, 0.0)
            pick_ref[here, k * rows : (k + 1) * rows] = hit.astype(BF16)
            both = hit if k == 0 else both + hit
        placed_ref[here, :] = both.astype(BF16)
    share = 1.0 / (1.0 + jnp.exp(logits_ref[1:2] - logits_ref[0:1]))
    share = jnp.sum(jnp.where(row == column, share, 0.0), axis=1, keepdims=True)
    mix_ref[:, 0:1] = share
    mix_ref[:, 1:2] = 1.0 - share


def place(me, expert_ids, route_logits, experts, capacity):
    rows = expert_ids.shape[0]
    return pl.pallas_call(
        functools.partial(routing_kernel, experts=experts),
        out_shape=[
            jax.ShapeDtypeStruct((experts * capacity, rows), BF16),
            jax.ShapeDtypeStruct((experts * capacity, 2 * rows), BF16),
            jax.ShapeDtypeStruct((rows, 2), F32),
        ],
        in_specs=[pl.BlockSpec(memory_space=pltpu.SMEM)]
        + [pl.BlockSpec(memory_space=pltpu.VMEM)] * 2,
        out_specs=[pl.BlockSpec(memory_space=pltpu.VMEM)] * 3,
        compiler_params=params(),
        name="routing",
    )(me.reshape(1), expert_ids.T, route_logits.T)


def dispatch_kernel(placed_ref, *refs, count, waits):
    inputs, outputs = refs[:count], refs[count + waits :]
    capacity, wide = outputs[0].shape
    width = wide // count
    for i, block in enumerate(inputs):
        for d, out in enumerate(outputs):
            out[:, i * width : (i + 1) * width] = jnp.dot(
                placed_ref[d * capacity : (d + 1) * capacity, :],
                block[...],
                preferred_element_type=F32,
            ).astype(BF16)


def dispatch(placed, slices, experts, capacity, after):
    rows, width = slices[0].shape
    wide = width * len(slices)
    return pl.pallas_call(
        functools.partial(dispatch_kernel, count=len(slices), waits=len(after)),
        out_shape=[jax.ShapeDtypeStruct((capacity, wide), BF16)] * experts,
        in_specs=[pl.BlockSpec(memory_space=pltpu.VMEM)] * (1 + len(slices))
        + [pl.BlockSpec(memory_space=pl.ANY)] * len(after),
        out_specs=[pl.BlockSpec(memory_space=pltpu.VMEM)] * experts,
        cost_estimate=cost(2 * experts * capacity * rows * wide, 6 * rows * wide),
        compiler_params=params(),
        name="dispatch",
    )(placed, *slices, *pinned(after))


def across(distance):
    return lambda column: lax.bitwise_xor(column, distance)


def everything(column):
    return 0


def prefetch_kernel(column_ref, after_ref, *refs, parts):
    half = len(refs) // 2
    copies = []
    for i, part in enumerate(parts):
        source, target, sem = refs[i], refs[half + i], refs[-1].at[i]
        count = target.shape[0]
        start = pl.multiple_of(part(column_ref[0]) * count, count)
        copies.append(pltpu.make_async_copy(source.at[0, pl.ds(start, count)], target, sem))
    for copy in copies:
        copy.start()
    for copy in copies:
        copy.wait()


def prefetch(column, fetches, after):
    sources = [pltpu.with_memory_space_constraint(w, pltpu.HBM) for w, _, _ in fetches]
    shapes = [pltpu.VMEM((count, w.shape[2]), w.dtype) for w, _, count in fetches]
    return pl.pallas_call(
        functools.partial(prefetch_kernel, parts=[part for _, part, _ in fetches]),
        out_shape=shapes,
        in_specs=[pl.BlockSpec(memory_space=pltpu.SMEM)]
        + [pl.BlockSpec(memory_space=pl.ANY)] * (1 + len(sources)),
        out_specs=[pl.BlockSpec(memory_space=pltpu.VMEM)] * len(shapes),
        scratch_shapes=[pltpu.SemaphoreType.DMA((len(shapes),))],
        cost_estimate=cost(0, sum(2 * count * w.shape[2] for w, _, count in fetches)),
        compiler_params=params(),
        name="prefetch",
    )(column.reshape(1), after, *sources)


def gate_up_kernel(*refs, experts, slices, first, last, waits):
    x_refs = refs[:experts]
    weights = refs[experts : experts + 2 * slices]
    rest = refs[experts + 2 * slices :]
    if not first:
        old_gate, old_up = rest[:2]
        rest = rest[2:]
    rest = rest[waits:]
    x = jnp.concatenate([r[...] for r in x_refs], axis=0)
    width, hidden = weights[0].shape
    tile = min(512, hidden)
    for n in range(hidden // tile):
        columns = slice(n * tile, (n + 1) * tile)
        sums = []
        for kind in range(2):
            total = None if first else (old_gate, old_up)[kind][:, columns]
            for i in range(slices):
                term = jnp.dot(
                    x[:, i * width : (i + 1) * width],
                    weights[2 * i + kind][:, columns],
                    preferred_element_type=F32,
                )
                total = term if total is None else total + term
            sums.append(total)
        gate, up = sums
        if last:
            rest[0][:, columns] = (gate / (1.0 + jnp.exp(-gate)) * up).astype(BF16)
        else:
            rest[0][:, columns] = gate
            rest[1][:, columns] = up


def gate_up(x_blocks, weights, sums, last, after):
    experts = len(x_blocks)
    rows = experts * x_blocks[0].shape[0]
    hidden = weights[0].shape[1]
    first = sums is None
    old = [] if first else pinned(sums)
    before = experts + len(weights)
    if last:
        out_shape = [pltpu.VMEM((rows, hidden), BF16)]
    else:
        out_shape = [pltpu.VMEM((rows, hidden), F32)] * 2
    return pl.pallas_call(
        functools.partial(
            gate_up_kernel,
            experts=experts,
            slices=len(weights) // 2,
            first=first,
            last=last,
            waits=len(after),
        ),
        out_shape=out_shape,
        in_specs=[pl.BlockSpec(memory_space=pltpu.VMEM)] * (before + len(old))
        + [pl.BlockSpec(memory_space=pl.ANY)] * len(after),
        out_specs=[pl.BlockSpec(memory_space=pltpu.VMEM)] * len(out_shape),
        input_output_aliases={} if first or last else {before: 0, before + 1: 1},
        cost_estimate=cost(
            2 * rows * hidden * sum(w.shape[0] for w in weights),
            sum(2 * w.size for w in weights),
        ),
        compiler_params=params(),
        name="gate_up",
    )(*x_blocks, *pinned(weights), *old, *after)


def down_kernel(column_ref, h_ref, w_ref, *refs, part, waits):
    out_refs = refs[waits:]
    capacity, width = out_refs[0].shape
    tile = min(256, width)
    for n in range(width // tile):
        start = pl.multiple_of(part(column_ref[0]) * width + n * tile, tile)
        y = jnp.dot(h_ref[...], w_ref[0, :, pl.ds(start, tile)], preferred_element_type=F32)
        columns = slice(n * tile, (n + 1) * tile)
        for d, out in enumerate(out_refs):
            out[:, columns] = y[d * capacity : (d + 1) * capacity].astype(BF16)


def down(column, part, hidden, down_w, width, experts, after):
    rows, depth = hidden.shape
    capacity = rows // experts
    return pl.pallas_call(
        functools.partial(down_kernel, part=part, waits=len(after)),
        out_shape=[jax.ShapeDtypeStruct((capacity, width), BF16)] * experts,
        in_specs=[pl.BlockSpec(memory_space=pltpu.SMEM)]
        + [pl.BlockSpec(memory_space=pltpu.VMEM)] * 2
        + [pl.BlockSpec(memory_space=pl.ANY)] * len(after),
        out_specs=[pl.BlockSpec(memory_space=pltpu.VMEM)] * experts,
        cost_estimate=cost(2 * rows * depth * width, 2 * depth * width + 2 * rows * width),
        compiler_params=params(),
        name="down",
    )(column.reshape(1), *pinned([hidden, down_w]), *after)


def combine_kernel(pick_ref, mix_ref, *refs, experts, starts):
    y_refs, added = refs[:experts], refs[experts : experts + len(starts)]
    outs = refs[experts + len(starts) :]
    width = y_refs[0].shape[1]
    rows, part = outs[0].shape
    y = jnp.concatenate([r[...] for r in y_refs], axis=0)
    picked = lax.dot_general(
        pick_ref[...], y, (((0,), (0,)), ((), ())), preferred_element_type=F32
    )
    mixed = picked[:rows] * mix_ref[:, 0:1] + picked[rows:] * mix_ref[:, 1:2]
    for other, start in zip(added, starts):
        value = other[...].astype(F32)
        stop = start + value.shape[1]
        pieces = [mixed[:, :start]] * (start > 0) + [mixed[:, start:stop] + value]
        pieces += [mixed[:, stop:]] * (stop < width)
        mixed = jnp.concatenate(pieces, axis=1) if len(pieces) > 1 else pieces[0]
    for i, out in enumerate(outs):
        out[...] = mixed[:, i * part : (i + 1) * part].astype(BF16)


def combine(pick, mix, blocks, added, cuts=1):
    rows = mix.shape[0]
    width = blocks[0].shape[1]
    operands = 2 + len(blocks) + len(added)
    return pl.pallas_call(
        functools.partial(
            combine_kernel, experts=len(blocks), starts=[start for _, start in added]
        ),
        out_shape=[jax.ShapeDtypeStruct((rows, width // cuts), BF16)] * cuts,
        in_specs=[pl.BlockSpec(memory_space=pltpu.VMEM)] * operands,
        out_specs=[pl.BlockSpec(memory_space=pltpu.VMEM)] * cuts,
        cost_estimate=cost(4 * rows * pick.shape[0] * width, 6 * rows * width),
        compiler_params=params(),
        name="combine",
    )(pick, mix, *blocks, *[array for array, _ in added])


def swap(value, axis, distance):
    if not distance:
        return value
    count = lax.axis_size(axis)
    return lax.ppermute(value, axis, [(i, i ^ distance) for i in range(count)])


def per_device(tokens, expert_ids, route_logits, gate_weight, up_weight, down_weight):
    rows, own_width = tokens.shape
    experts = lax.axis_size("expert")
    shards = lax.axis_size("tensor")
    capacity = rows // 2
    me = lax.axis_index("expert").astype(jnp.int32)
    column = lax.axis_index("tensor").astype(jnp.int32)
    doubling = shards == 4
    width = own_width if doubling else own_width * shards

    if doubling:
        across_two = swap(tokens, "tensor", 2)
        slices = [tokens, swap(tokens, "tensor", 1), across_two, swap(across_two, "tensor", 1)]
        parts = [across(distance) for distance in range(4)]
        groups = [[0, 1], [2], [3]]
    else:
        slices = [lax.all_gather(tokens, "tensor", axis=1, tiled=True)]
        parts = [everything]
        groups = [[0]]
    placed, pick, mix = place(me, expert_ids, route_logits, experts, capacity)

    def fetch(chosen, after):
        fetches = [(w, parts[i], width) for i in chosen for w in (gate_weight, up_weight)]
        return list(prefetch(column, fetches, after))

    weights, arrived = fetch(groups[0], placed), []
    for group in groups:
        after = weights[-1:] if len(arrived) < 2 else []
        outgoing = dispatch(placed, [slices[i] for i in group], experts, capacity, after)
        arrived.append([swap(block, "expert", e) for e, block in enumerate(outgoing)])
        if len(arrived) == 1 and len(groups) > 1:
            weights += fetch([2, 3], outgoing[0])
    sums = None
    for group, x_blocks in zip(groups, arrived):
        chosen = weights[2 * group[0] : 2 * group[-1] + 2]
        after = arrived[1][1:2] if sums is None and len(groups) > 1 else []
        sums = gate_up(x_blocks, chosen, sums, group is groups[-1], after)
    hidden = sums[0]

    def returned(part, after=()):
        terms = down(column, part, hidden, down_weight, width, experts, after)
        return [swap(block, "expert", e) for e, block in enumerate(terms)]

    if not doubling:
        mixed = combine(pick, mix, returned(everything), [])[0]
        return lax.psum_scatter(mixed, "tensor", scatter_dimension=1, tiled=True)
    low, high = combine(pick, mix, returned(across(3)), [], cuts=2)
    passed = swap(low, "tensor", 1)
    far = (swap(high, "tensor", 3), width // 2)
    onwards = combine(pick, mix, returned(across(2)), [(passed, 0)])[0]
    over = (swap(onwards, "tensor", 2), 0)
    near = combine(pick, mix, returned(across(1), [low]), [])[0]
    beside = (swap(near, "tensor", 1), 0)
    return combine(pick, mix, returned(across(0), [passed]), [beside, over, far])[0]


def solution(mesh):
    in_specs = (
        P(("groups", "expert"), "tensor"),
        P(("groups", "expert"), None),
        P(("groups", "expert"), None),
        P("expert", None, "tensor"),
        P("expert", None, "tensor"),
        P("expert", "tensor", None),
    )
    out_specs = P(("groups", "expert"), "tensor")
    return jax.shard_map(
        per_device, mesh=mesh, in_specs=in_specs, out_specs=out_specs, check_vma=False
    )
```

```python
import functools

import jax
import jax.numpy as jnp
from jax import lax
from jax.experimental import pallas as pl
from jax.experimental.pallas import tpu as pltpu
from jax.sharding import PartitionSpec as P

F32 = jnp.float32
BF16 = jnp.bfloat16
MIB = 1024 * 1024


def params(mib=6):
    return pltpu.CompilerParams(vmem_limit_bytes=mib * MIB)


def cost(flops, moved):
    return pl.CostEstimate(flops=flops, bytes_accessed=moved, transcendentals=0)


def pinned(arrays):
    return [pltpu.with_memory_space_constraint(array, pltpu.VMEM) for array in arrays]


def routing_kernel(me_ref, ids_ref, logits_ref, placed_ref, pick_ref, mix_ref, *, experts):
    rows = ids_ref.shape[1]
    capacity = placed_ref.shape[0] // experts
    relative = lax.bitwise_xor(ids_ref[...], me_ref[0])
    lane = lax.broadcasted_iota(jnp.int32, (experts, rows), 0)
    names = [lane == relative[k : k + 1] for k in range(2)]
    named = names[0] | names[1]
    row = lax.broadcasted_iota(jnp.int32, (rows, rows), 0)
    column = lax.broadcasted_iota(jnp.int32, (rows, rows), 1)
    before = jnp.dot(
        jnp.where(named, 1.0, 0.0).astype(BF16),
        jnp.where(row < column, 1.0, 0.0).astype(BF16),
        preferred_element_type=F32,
    ).astype(jnp.int32)
    slot = lax.broadcasted_iota(jnp.int32, (capacity, rows), 0)
    for d in range(experts):
        here = slice(d * capacity, (d + 1) * capacity)
        both = None
        for k in range(2):
            position = jnp.where(names[k], before, -1)
            hit = jnp.where(position[d : d + 1] == slot, 1.0, 0.0)
            pick_ref[here, k * rows : (k + 1) * rows] = hit.astype(BF16)
            both = hit if k == 0 else both + hit
        placed_ref[here, :] = both.astype(BF16)
    share = 1.0 / (1.0 + jnp.exp(logits_ref[1:2] - logits_ref[0:1]))
    share = jnp.sum(jnp.where(row == column, share, 0.0), axis=1, keepdims=True)
    mix_ref[:, 0:1] = share
    mix_ref[:, 1:2] = 1.0 - share


def place(me, expert_ids, route_logits, experts, capacity):
    rows = expert_ids.shape[0]
    return pl.pallas_call(
        functools.partial(routing_kernel, experts=experts),
        out_shape=[
            jax.ShapeDtypeStruct((experts * capacity, rows), BF16),
            jax.ShapeDtypeStruct((experts * capacity, 2 * rows), BF16),
            jax.ShapeDtypeStruct((rows, 2), F32),
        ],
        in_specs=[pl.BlockSpec(memory_space=pltpu.SMEM)]
        + [pl.BlockSpec(memory_space=pltpu.VMEM)] * 2,
        out_specs=[pl.BlockSpec(memory_space=pltpu.VMEM)] * 3,
        compiler_params=params(),
        name="routing",
    )(me.reshape(1), expert_ids.T, route_logits.T)


def dispatch_kernel(placed_ref, *refs, count, waits):
    inputs, outputs = refs[:count], refs[count + waits :]
    capacity, wide = outputs[0].shape
    width = wide // count
    for i, block in enumerate(inputs):
        for d, out in enumerate(outputs):
            out[:, i * width : (i + 1) * width] = jnp.dot(
                placed_ref[d * capacity : (d + 1) * capacity, :],
                block[...],
                preferred_element_type=F32,
            ).astype(BF16)


def dispatch(placed, slices, experts, capacity, after):
    rows, width = slices[0].shape
    wide = width * len(slices)
    return pl.pallas_call(
        functools.partial(dispatch_kernel, count=len(slices), waits=len(after)),
        out_shape=[jax.ShapeDtypeStruct((capacity, wide), BF16)] * experts,
        in_specs=[pl.BlockSpec(memory_space=pltpu.VMEM)] * (1 + len(slices))
        + [pl.BlockSpec(memory_space=pl.ANY)] * len(after),
        out_specs=[pl.BlockSpec(memory_space=pltpu.VMEM)] * experts,
        cost_estimate=cost(2 * experts * capacity * rows * wide, 6 * rows * wide),
        compiler_params=params(),
        name="dispatch",
    )(placed, *slices, *pinned(after))


def across(distance):
    return lambda column: lax.bitwise_xor(column, distance)


def everything(column):
    return 0


def prefetch_kernel(column_ref, after_ref, *refs, parts):
    half = len(refs) // 2
    copies = []
    for i, part in enumerate(parts):
        source, target, sem = refs[i], refs[half + i], refs[-1].at[i]
        count = target.shape[0]
        start = pl.multiple_of(part(column_ref[0]) * count, count)
        copies.append(pltpu.make_async_copy(source.at[0, pl.ds(start, count)], target, sem))
    for copy in copies:
        copy.start()
    for copy in copies:
        copy.wait()


def prefetch(column, fetches, after):
    sources = [pltpu.with_memory_space_constraint(w, pltpu.HBM) for w, _, _ in fetches]
    shapes = [pltpu.VMEM((count, w.shape[2]), w.dtype) for w, _, count in fetches]
    return pl.pallas_call(
        functools.partial(prefetch_kernel, parts=[part for _, part, _ in fetches]),
        out_shape=shapes,
        in_specs=[pl.BlockSpec(memory_space=pltpu.SMEM)]
        + [pl.BlockSpec(memory_space=pl.ANY)] * (1 + len(sources)),
        out_specs=[pl.BlockSpec(memory_space=pltpu.VMEM)] * len(shapes),
        scratch_shapes=[pltpu.SemaphoreType.DMA((len(shapes),))],
        cost_estimate=cost(0, sum(2 * count * w.shape[2] for w, _, count in fetches)),
        compiler_params=params(),
        name="prefetch",
    )(column.reshape(1), after, *sources)


def gate_up_kernel(*refs, experts, slices, first, last, waits):
    x_refs = refs[:experts]
    weights = refs[experts : experts + 2 * slices]
    rest = refs[experts + 2 * slices :]
    if not first:
        old_gate, old_up = rest[:2]
        rest = rest[2:]
    rest = rest[waits:]
    x = jnp.concatenate([r[...] for r in x_refs], axis=0)
    width, hidden = weights[0].shape
    tile = min(512, hidden)
    for n in range(hidden // tile):
        columns = slice(n * tile, (n + 1) * tile)
        sums = []
        for kind in range(2):
            total = None if first else (old_gate, old_up)[kind][:, columns]
            for i in range(slices):
                term = jnp.dot(
                    x[:, i * width : (i + 1) * width],
                    weights[2 * i + kind][:, columns],
                    preferred_element_type=F32,
                )
                total = term if total is None else total + term
            sums.append(total)
        gate, up = sums
        if last:
            rest[0][:, columns] = (gate / (1.0 + jnp.exp(-gate)) * up).astype(BF16)
        else:
            rest[0][:, columns] = gate
            rest[1][:, columns] = up


def gate_up(x_blocks, weights, sums, last, after):
    experts = len(x_blocks)
    rows = experts * x_blocks[0].shape[0]
    hidden = weights[0].shape[1]
    first = sums is None
    old = [] if first else pinned(sums)
    before = experts + len(weights)
    if last:
        out_shape = [pltpu.VMEM((rows, hidden), BF16)]
    else:
        out_shape = [pltpu.VMEM((rows, hidden), F32)] * 2
    return pl.pallas_call(
        functools.partial(
            gate_up_kernel,
            experts=experts,
            slices=len(weights) // 2,
            first=first,
            last=last,
            waits=len(after),
        ),
        out_shape=out_shape,
        in_specs=[pl.BlockSpec(memory_space=pltpu.VMEM)] * (before + len(old))
        + [pl.BlockSpec(memory_space=pl.ANY)] * len(after),
        out_specs=[pl.BlockSpec(memory_space=pltpu.VMEM)] * len(out_shape),
        input_output_aliases={} if first or last else {before: 0, before + 1: 1},
        cost_estimate=cost(
            2 * rows * hidden * sum(w.shape[0] for w in weights),
            sum(2 * w.size for w in weights),
        ),
        compiler_params=params(),
        name="gate_up",
    )(*x_blocks, *pinned(weights), *old, *after)


def down_kernel(column_ref, h_ref, w_ref, *refs, part, waits):
    out_refs = refs[waits:]
    capacity, width = out_refs[0].shape
    tile = min(256, width)
    for n in range(width // tile):
        start = pl.multiple_of(part(column_ref[0]) * width + n * tile, tile)
        y = jnp.dot(h_ref[...], w_ref[0, :, pl.ds(start, tile)], preferred_element_type=F32)
        columns = slice(n * tile, (n + 1) * tile)
        for d, out in enumerate(out_refs):
            out[:, columns] = y[d * capacity : (d + 1) * capacity].astype(BF16)


def down(column, part, hidden, down_w, width, experts, after):
    rows, depth = hidden.shape
    capacity = rows // experts
    return pl.pallas_call(
        functools.partial(down_kernel, part=part, waits=len(after)),
        out_shape=[jax.ShapeDtypeStruct((capacity, width), BF16)] * experts,
        in_specs=[pl.BlockSpec(memory_space=pltpu.SMEM)]
        + [pl.BlockSpec(memory_space=pltpu.VMEM)] * 2
        + [pl.BlockSpec(memory_space=pl.ANY)] * len(after),
        out_specs=[pl.BlockSpec(memory_space=pltpu.VMEM)] * experts,
        cost_estimate=cost(2 * rows * depth * width, 2 * depth * width + 2 * rows * width),
        compiler_params=params(),
        name="down",
    )(column.reshape(1), *pinned([hidden, down_w]), *after)


def combine_kernel(pick_ref, mix_ref, *refs, experts, starts):
    y_refs, added = refs[:experts], refs[experts : experts + len(starts)]
    outs = refs[experts + len(starts) :]
    width = y_refs[0].shape[1]
    rows, part = outs[0].shape
    y = jnp.concatenate([r[...] for r in y_refs], axis=0)
    picked = lax.dot_general(
        pick_ref[...], y, (((0,), (0,)), ((), ())), preferred_element_type=F32
    )
    mixed = picked[:rows] * mix_ref[:, 0:1] + picked[rows:] * mix_ref[:, 1:2]
    for other, start in zip(added, starts):
        value = other[...].astype(F32)
        stop = start + value.shape[1]
        pieces = [mixed[:, :start]] * (start > 0) + [mixed[:, start:stop] + value]
        pieces += [mixed[:, stop:]] * (stop < width)
        mixed = jnp.concatenate(pieces, axis=1) if len(pieces) > 1 else pieces[0]
    for i, out in enumerate(outs):
        out[...] = mixed[:, i * part : (i + 1) * part].astype(BF16)


def combine(pick, mix, blocks, added, cuts=1):
    rows = mix.shape[0]
    width = blocks[0].shape[1]
    operands = 2 + len(blocks) + len(added)
    return pl.pallas_call(
        functools.partial(
            combine_kernel, experts=len(blocks), starts=[start for _, start in added]
        ),
        out_shape=[jax.ShapeDtypeStruct((rows, width // cuts), BF16)] * cuts,
        in_specs=[pl.BlockSpec(memory_space=pltpu.VMEM)] * operands,
        out_specs=[pl.BlockSpec(memory_space=pltpu.VMEM)] * cuts,
        cost_estimate=cost(4 * rows * pick.shape[0] * width, 6 * rows * width),
        compiler_params=params(),
        name="combine",
    )(pick, mix, *blocks, *[array for array, _ in added])


def hold_kernel(array_ref, after_ref, out_ref):
    out_ref[...] = array_ref[...]


def hold(array, after):
    return pl.pallas_call(
        hold_kernel,
        out_shape=jax.ShapeDtypeStruct(array.shape, array.dtype),
        in_specs=[pl.BlockSpec(memory_space=pltpu.VMEM), pl.BlockSpec(memory_space=pl.ANY)],
        out_specs=pl.BlockSpec(memory_space=pltpu.VMEM),
        cost_estimate=cost(0, 4 * array.size),
        compiler_params=params(),
        name="hold",
    )(array, after)


def swap(value, axis, distance):
    if not distance:
        return value
    count = lax.axis_size(axis)
    return lax.ppermute(value, axis, [(i, i ^ distance) for i in range(count)])


def per_device(tokens, expert_ids, route_logits, gate_weight, up_weight, down_weight):
    rows, own_width = tokens.shape
    experts = lax.axis_size("expert")
    shards = lax.axis_size("tensor")
    capacity = rows // 2
    me = lax.axis_index("expert").astype(jnp.int32)
    column = lax.axis_index("tensor").astype(jnp.int32)
    doubling = shards == 4
    width = own_width if doubling else own_width * shards

    if doubling:
        across_two = swap(tokens, "tensor", 2)
        slices = [tokens, swap(tokens, "tensor", 1), across_two, swap(across_two, "tensor", 1)]
        parts = [across(distance) for distance in range(4)]
        groups = [[0, 1], [2], [3]]
    else:
        slices = [lax.all_gather(tokens, "tensor", axis=1, tiled=True)]
        parts = [everything]
        groups = [[0]]
    placed, pick, mix = place(me, expert_ids, route_logits, experts, capacity)

    def fetch(chosen, after):
        fetches = [(w, parts[i], width) for i in chosen for w in (gate_weight, up_weight)]
        return list(prefetch(column, fetches, after))

    weights, arrived = fetch(groups[0], placed), []
    for group in groups:
        after = weights[-1:] if len(arrived) < 2 else []
        outgoing = dispatch(placed, [slices[i] for i in group], experts, capacity, after)
        arrived.append([swap(block, "expert", e) for e, block in enumerate(outgoing)])
        if len(arrived) == 1 and len(groups) > 1:
            weights += fetch([2, 3], outgoing[0])
    sums = None
    for group, x_blocks in zip(groups, arrived):
        chosen = weights[2 * group[0] : 2 * group[-1] + 2]
        after = arrived[1][1:2] if sums is None and len(groups) > 1 else []
        sums = gate_up(x_blocks, chosen, sums, group is groups[-1], after)
    hidden = sums[0]

    def returned(part, after=()):
        terms = down(column, part, hidden, down_weight, width, experts, after)
        return [swap(block, "expert", e) for e, block in enumerate(terms)]

    if not doubling:
        mixed = combine(pick, mix, returned(everything), [])[0]
        return lax.psum_scatter(mixed, "tensor", scatter_dimension=1, tiled=True)
    low, high = combine(pick, mix, returned(across(3)), [], cuts=2)
    passed = swap(low, "tensor", 1)
    onwards = combine(pick, mix, returned(across(2)), [(passed, 0)])[0]
    over = (swap(onwards, "tensor", 2), 0)
    far = (swap(hold(high, onwards), "tensor", 3), width // 2)
    near = combine(pick, mix, returned(across(1), [low]), [])[0]
    beside = (swap(near, "tensor", 1), 0)
    return combine(pick, mix, returned(across(0), [passed]), [beside, over, far])[0]


def solution(mesh):
    in_specs = (
        P(("groups", "expert"), "tensor"),
        P(("groups", "expert"), None),
        P(("groups", "expert"), None),
        P("expert", None, "tensor"),
        P("expert", None, "tensor"),
        P("expert", "tensor", None),
    )
    out_specs = P(("groups", "expert"), "tensor")
    return jax.shard_map(
        per_device, mesh=mesh, in_specs=in_specs, out_specs=out_specs, check_vma=False
    )
```

```python
import functools

import jax
import jax.numpy as jnp
from jax import lax
from jax.experimental import pallas as pl
from jax.experimental.pallas import tpu as pltpu
from jax.sharding import PartitionSpec as P

F32 = jnp.float32
BF16 = jnp.bfloat16
MIB = 1024 * 1024


def params(mib=6):
    return pltpu.CompilerParams(vmem_limit_bytes=mib * MIB)


def cost(flops, moved):
    return pl.CostEstimate(flops=flops, bytes_accessed=moved, transcendentals=0)


def pinned(arrays):
    return [pltpu.with_memory_space_constraint(array, pltpu.VMEM) for array in arrays]


def routing_kernel(me_ref, ids_ref, logits_ref, placed_ref, pick_ref, mix_ref, *, experts):
    rows = ids_ref.shape[1]
    capacity = placed_ref.shape[0] // experts
    relative = lax.bitwise_xor(ids_ref[...], me_ref[0])
    lane = lax.broadcasted_iota(jnp.int32, (experts, rows), 0)
    names = [lane == relative[k : k + 1] for k in range(2)]
    named = names[0] | names[1]
    row = lax.broadcasted_iota(jnp.int32, (rows, rows), 0)
    column = lax.broadcasted_iota(jnp.int32, (rows, rows), 1)
    before = jnp.dot(
        jnp.where(named, 1.0, 0.0).astype(BF16),
        jnp.where(row < column, 1.0, 0.0).astype(BF16),
        preferred_element_type=F32,
    ).astype(jnp.int32)
    slot = lax.broadcasted_iota(jnp.int32, (capacity, rows), 0)
    for d in range(experts):
        here = slice(d * capacity, (d + 1) * capacity)
        both = None
        for k in range(2):
            position = jnp.where(names[k], before, -1)
            hit = jnp.where(position[d : d + 1] == slot, 1.0, 0.0)
            pick_ref[here, k * rows : (k + 1) * rows] = hit.astype(BF16)
            both = hit if k == 0 else both + hit
        placed_ref[here, :] = both.astype(BF16)
    share = 1.0 / (1.0 + jnp.exp(logits_ref[1:2] - logits_ref[0:1]))
    share = jnp.sum(jnp.where(row == column, share, 0.0), axis=1, keepdims=True)
    mix_ref[:, 0:1] = share
    mix_ref[:, 1:2] = 1.0 - share


def place(me, expert_ids, route_logits, experts, capacity):
    rows = expert_ids.shape[0]
    return pl.pallas_call(
        functools.partial(routing_kernel, experts=experts),
        out_shape=[
            jax.ShapeDtypeStruct((experts * capacity, rows), BF16),
            jax.ShapeDtypeStruct((experts * capacity, 2 * rows), BF16),
            jax.ShapeDtypeStruct((rows, 2), F32),
        ],
        in_specs=[pl.BlockSpec(memory_space=pltpu.SMEM)]
        + [pl.BlockSpec(memory_space=pltpu.VMEM)] * 2,
        out_specs=[pl.BlockSpec(memory_space=pltpu.VMEM)] * 3,
        compiler_params=params(),
        name="routing",
    )(me.reshape(1), expert_ids.T, route_logits.T)


def dispatch_kernel(placed_ref, *refs, count, waits):
    inputs, outputs = refs[:count], refs[count + waits :]
    capacity, wide = outputs[0].shape
    width = wide // count
    for i, block in enumerate(inputs):
        for d, out in enumerate(outputs):
            out[:, i * width : (i + 1) * width] = jnp.dot(
                placed_ref[d * capacity : (d + 1) * capacity, :],
                block[...],
                preferred_element_type=F32,
            ).astype(BF16)


def dispatch(placed, slices, experts, capacity, after):
    rows, width = slices[0].shape
    wide = width * len(slices)
    return pl.pallas_call(
        functools.partial(dispatch_kernel, count=len(slices), waits=len(after)),
        out_shape=[jax.ShapeDtypeStruct((capacity, wide), BF16)] * experts,
        in_specs=[pl.BlockSpec(memory_space=pltpu.VMEM)] * (1 + len(slices))
        + [pl.BlockSpec(memory_space=pl.ANY)] * len(after),
        out_specs=[pl.BlockSpec(memory_space=pltpu.VMEM)] * experts,
        cost_estimate=cost(2 * experts * capacity * rows * wide, 6 * rows * wide),
        compiler_params=params(),
        name="dispatch",
    )(placed, *slices, *pinned(after))


def across(distance):
    return lambda column: lax.bitwise_xor(column, distance)


def everything(column):
    return 0


def prefetch_kernel(column_ref, after_ref, *refs, parts):
    half = len(refs) // 2
    copies = []
    for i, part in enumerate(parts):
        source, target, sem = refs[i], refs[half + i], refs[-1].at[i]
        count = target.shape[0]
        start = pl.multiple_of(part(column_ref[0]) * count, count)
        copies.append(pltpu.make_async_copy(source.at[0, pl.ds(start, count)], target, sem))
    for copy in copies:
        copy.start()
    for copy in copies:
        copy.wait()


def prefetch(column, fetches, after):
    sources = [pltpu.with_memory_space_constraint(w, pltpu.HBM) for w, _, _ in fetches]
    shapes = [pltpu.VMEM((count, w.shape[2]), w.dtype) for w, _, count in fetches]
    return pl.pallas_call(
        functools.partial(prefetch_kernel, parts=[part for _, part, _ in fetches]),
        out_shape=shapes,
        in_specs=[pl.BlockSpec(memory_space=pltpu.SMEM)]
        + [pl.BlockSpec(memory_space=pl.ANY)] * (1 + len(sources)),
        out_specs=[pl.BlockSpec(memory_space=pltpu.VMEM)] * len(shapes),
        scratch_shapes=[pltpu.SemaphoreType.DMA((len(shapes),))],
        cost_estimate=cost(0, sum(2 * count * w.shape[2] for w, _, count in fetches)),
        compiler_params=params(),
        name="prefetch",
    )(column.reshape(1), after, *sources)


def gate_up_kernel(*refs, experts, slices, first, last, waits):
    x_refs = refs[:experts]
    weights = refs[experts : experts + 2 * slices]
    rest = refs[experts + 2 * slices :]
    if not first:
        old_gate, old_up = rest[:2]
        rest = rest[2:]
    rest = rest[waits:]
    x = jnp.concatenate([r[...] for r in x_refs], axis=0)
    width, hidden = weights[0].shape
    tile = min(512, hidden)
    for n in range(hidden // tile):
        columns = slice(n * tile, (n + 1) * tile)
        sums = []
        for kind in range(2):
            total = None if first else (old_gate, old_up)[kind][:, columns]
            for i in range(slices):
                term = jnp.dot(
                    x[:, i * width : (i + 1) * width],
                    weights[2 * i + kind][:, columns],
                    preferred_element_type=F32,
                )
                total = term if total is None else total + term
            sums.append(total)
        gate, up = sums
        if last:
            rest[0][:, columns] = (gate / (1.0 + jnp.exp(-gate)) * up).astype(BF16)
        else:
            rest[0][:, columns] = gate
            rest[1][:, columns] = up


def gate_up(x_blocks, weights, sums, last, after):
    experts = len(x_blocks)
    rows = experts * x_blocks[0].shape[0]
    hidden = weights[0].shape[1]
    first = sums is None
    old = [] if first else pinned(sums)
    before = experts + len(weights)
    if last:
        out_shape = [pltpu.VMEM((rows, hidden), BF16)]
    else:
        out_shape = [pltpu.VMEM((rows, hidden), F32)] * 2
    return pl.pallas_call(
        functools.partial(
            gate_up_kernel,
            experts=experts,
            slices=len(weights) // 2,
            first=first,
            last=last,
            waits=len(after),
        ),
        out_shape=out_shape,
        in_specs=[pl.BlockSpec(memory_space=pltpu.VMEM)] * (before + len(old))
        + [pl.BlockSpec(memory_space=pl.ANY)] * len(after),
        out_specs=[pl.BlockSpec(memory_space=pltpu.VMEM)] * len(out_shape),
        input_output_aliases={} if first or last else {before: 0, before + 1: 1},
        cost_estimate=cost(
            2 * rows * hidden * sum(w.shape[0] for w in weights),
            sum(2 * w.size for w in weights),
        ),
        compiler_params=params(),
        name="gate_up",
    )(*x_blocks, *pinned(weights), *old, *after)


def down_kernel(column_ref, h_ref, w_ref, *refs, parts, waits):
    out_refs = refs[waits:]
    capacity, wide = out_refs[0].shape
    width = wide // len(parts)
    tile = min(256, width)
    for i, part in enumerate(parts):
        for n in range(width // tile):
            start = pl.multiple_of(part(column_ref[0]) * width + n * tile, tile)
            y = jnp.dot(h_ref[...], w_ref[0, :, pl.ds(start, tile)], preferred_element_type=F32)
            columns = slice(i * width + n * tile, i * width + (n + 1) * tile)
            for d, out in enumerate(out_refs):
                out[:, columns] = y[d * capacity : (d + 1) * capacity].astype(BF16)


def down(column, parts, hidden, down_w, width, experts, after):
    rows, depth = hidden.shape
    capacity = rows // experts
    wide = width * len(parts)
    return pl.pallas_call(
        functools.partial(down_kernel, parts=parts, waits=len(after)),
        out_shape=[jax.ShapeDtypeStruct((capacity, wide), BF16)] * experts,
        in_specs=[pl.BlockSpec(memory_space=pltpu.SMEM)]
        + [pl.BlockSpec(memory_space=pltpu.VMEM)] * 2
        + [pl.BlockSpec(memory_space=pl.ANY)] * len(after),
        out_specs=[pl.BlockSpec(memory_space=pltpu.VMEM)] * experts,
        cost_estimate=cost(2 * rows * depth * wide, 2 * depth * wide + 2 * rows * wide),
        compiler_params=params(),
        name="down",
    )(column.reshape(1), *pinned([hidden, down_w]), *after)


def combine_kernel(pick_ref, mix_ref, *refs, experts, starts, index):
    y_refs, added = refs[:experts], refs[experts : experts + len(starts)]
    outs = refs[experts + len(starts) :]
    rows, part = outs[0].shape
    width = part * len(outs)
    columns = slice(index * width, (index + 1) * width)
    y = jnp.concatenate([r[:, columns] for r in y_refs], axis=0)
    picked = lax.dot_general(
        pick_ref[...], y, (((0,), (0,)), ((), ())), preferred_element_type=F32
    )
    mixed = picked[:rows] * mix_ref[:, 0:1] + picked[rows:] * mix_ref[:, 1:2]
    for other, start in zip(added, starts):
        value = other[...].astype(F32)
        stop = start + value.shape[1]
        pieces = [mixed[:, :start]] * (start > 0) + [mixed[:, start:stop] + value]
        pieces += [mixed[:, stop:]] * (stop < width)
        mixed = jnp.concatenate(pieces, axis=1) if len(pieces) > 1 else pieces[0]
    for i, out in enumerate(outs):
        out[...] = mixed[:, i * part : (i + 1) * part].astype(BF16)


def combine(pick, mix, blocks, added, cuts=1, slices=1, index=0):
    rows = mix.shape[0]
    width = blocks[0].shape[1] // slices
    operands = 2 + len(blocks) + len(added)
    return pl.pallas_call(
        functools.partial(
            combine_kernel,
            experts=len(blocks),
            starts=[start for _, start in added],
            index=index,
        ),
        out_shape=[jax.ShapeDtypeStruct((rows, width // cuts), BF16)] * cuts,
        in_specs=[pl.BlockSpec(memory_space=pltpu.VMEM)] * operands,
        out_specs=[pl.BlockSpec(memory_space=pltpu.VMEM)] * cuts,
        cost_estimate=cost(4 * rows * pick.shape[0] * width, 6 * rows * width),
        compiler_params=params(),
        name="combine",
    )(pick, mix, *blocks, *[array for array, _ in added])


def swap(value, axis, distance):
    if not distance:
        return value
    count = lax.axis_size(axis)
    return lax.ppermute(value, axis, [(i, i ^ distance) for i in range(count)])


def per_device(tokens, expert_ids, route_logits, gate_weight, up_weight, down_weight):
    rows, own_width = tokens.shape
    experts = lax.axis_size("expert")
    shards = lax.axis_size("tensor")
    capacity = rows // 2
    me = lax.axis_index("expert").astype(jnp.int32)
    column = lax.axis_index("tensor").astype(jnp.int32)
    doubling = shards == 4
    width = own_width if doubling else own_width * shards

    if doubling:
        across_two = swap(tokens, "tensor", 2)
        slices = [tokens, swap(tokens, "tensor", 1), across_two, swap(across_two, "tensor", 1)]
        parts = [across(distance) for distance in range(4)]
        groups = [[0, 1], [2], [3]]
    else:
        slices = [lax.all_gather(tokens, "tensor", axis=1, tiled=True)]
        parts = [everything]
        groups = [[0]]
    placed, pick, mix = place(me, expert_ids, route_logits, experts, capacity)

    def fetch(chosen, after):
        fetches = [(w, parts[i], width) for i in chosen for w in (gate_weight, up_weight)]
        return list(prefetch(column, fetches, after))

    weights, arrived = fetch(groups[0], placed), []
    for group in groups:
        after = weights[-1:] if len(arrived) < 2 else []
        outgoing = dispatch(placed, [slices[i] for i in group], experts, capacity, after)
        arrived.append([swap(block, "expert", e) for e, block in enumerate(outgoing)])
        if len(arrived) == 1 and len(groups) > 1:
            weights += fetch([2, 3], outgoing[0])
    sums = None
    for group, x_blocks in zip(groups, arrived):
        chosen = weights[2 * group[0] : 2 * group[-1] + 2]
        after = arrived[1][1:2] if sums is None and len(groups) > 1 else []
        sums = gate_up(x_blocks, chosen, sums, group is groups[-1], after)
    hidden = sums[0]

    def returned(parts, after=()):
        terms = down(column, parts, hidden, down_weight, width, experts, after)
        return [swap(block, "expert", e) for e, block in enumerate(terms)]

    if not doubling:
        mixed = combine(pick, mix, returned([everything]), [])[0]
        return lax.psum_scatter(mixed, "tensor", scatter_dimension=1, tiled=True)
    low, high = combine(pick, mix, returned([across(3)]), [], cuts=2)
    passed = swap(low, "tensor", 1)
    far = (swap(high, "tensor", 3), width // 2)
    pair = returned([across(2), across(1)])
    onwards = combine(pick, mix, pair, [(passed, 0)], slices=2)[0]
    over = (swap(onwards, "tensor", 2), 0)
    beside = (swap(combine(pick, mix, pair, [], slices=2, index=1)[0], "tensor", 1), 0)
    return combine(pick, mix, returned([across(0)], [passed]), [beside, over, far])[0]


def solution(mesh):
    in_specs = (
        P(("groups", "expert"), "tensor"),
        P(("groups", "expert"), None),
        P(("groups", "expert"), None),
        P("expert", None, "tensor"),
        P("expert", None, "tensor"),
        P("expert", "tensor", None),
    )
    out_specs = P(("groups", "expert"), "tensor")
    return jax.shard_map(
        per_device, mesh=mesh, in_specs=in_specs, out_specs=out_specs, check_vma=False
    )
```

```python
import functools

import jax
import jax.numpy as jnp
from jax import lax
from jax.experimental import pallas as pl
from jax.experimental.pallas import tpu as pltpu
from jax.sharding import PartitionSpec as P

F32 = jnp.float32
BF16 = jnp.bfloat16
MIB = 1024 * 1024


def params(mib=6):
    return pltpu.CompilerParams(vmem_limit_bytes=mib * MIB)


def cost(flops, moved):
    return pl.CostEstimate(flops=flops, bytes_accessed=moved, transcendentals=0)


def pinned(arrays):
    return [pltpu.with_memory_space_constraint(array, pltpu.VMEM) for array in arrays]


def routing_kernel(me_ref, ids_ref, logits_ref, placed_ref, pick_ref, mix_ref, *, experts):
    rows = ids_ref.shape[1]
    capacity = placed_ref.shape[0] // experts
    relative = lax.bitwise_xor(ids_ref[...], me_ref[0])
    lane = lax.broadcasted_iota(jnp.int32, (experts, rows), 0)
    names = [lane == relative[k : k + 1] for k in range(2)]
    named = names[0] | names[1]
    row = lax.broadcasted_iota(jnp.int32, (rows, rows), 0)
    column = lax.broadcasted_iota(jnp.int32, (rows, rows), 1)
    before = jnp.dot(
        jnp.where(named, 1.0, 0.0).astype(BF16),
        jnp.where(row < column, 1.0, 0.0).astype(BF16),
        preferred_element_type=F32,
    ).astype(jnp.int32)
    slot = lax.broadcasted_iota(jnp.int32, (capacity, rows), 0)
    for d in range(experts):
        here = slice(d * capacity, (d + 1) * capacity)
        both = None
        for k in range(2):
            position = jnp.where(names[k], before, -1)
            hit = jnp.where(position[d : d + 1] == slot, 1.0, 0.0)
            pick_ref[here, k * rows : (k + 1) * rows] = hit.astype(BF16)
            both = hit if k == 0 else both + hit
        placed_ref[here, :] = both.astype(BF16)
    share = 1.0 / (1.0 + jnp.exp(logits_ref[1:2] - logits_ref[0:1]))
    share = jnp.sum(jnp.where(row == column, share, 0.0), axis=1, keepdims=True)
    mix_ref[:, 0:1] = share
    mix_ref[:, 1:2] = 1.0 - share


def place(me, expert_ids, route_logits, experts, capacity):
    rows = expert_ids.shape[0]
    return pl.pallas_call(
        functools.partial(routing_kernel, experts=experts),
        out_shape=[
            jax.ShapeDtypeStruct((experts * capacity, rows), BF16),
            jax.ShapeDtypeStruct((experts * capacity, 2 * rows), BF16),
            jax.ShapeDtypeStruct((rows, 2), F32),
        ],
        in_specs=[pl.BlockSpec(memory_space=pltpu.SMEM)]
        + [pl.BlockSpec(memory_space=pltpu.VMEM)] * 2,
        out_specs=[pl.BlockSpec(memory_space=pltpu.VMEM)] * 3,
        compiler_params=params(),
        name="routing",
    )(me.reshape(1), expert_ids.T, route_logits.T)


def dispatch_kernel(placed_ref, *refs, count, waits, echo):
    inputs, outputs = refs[:count], refs[count + waits :]
    if echo:
        outputs[-1][...] = inputs[0][...]
        outputs = outputs[:-1]
    capacity, wide = outputs[0].shape
    width = wide // count
    for i, block in enumerate(inputs):
        for d, out in enumerate(outputs):
            out[:, i * width : (i + 1) * width] = jnp.dot(
                placed_ref[d * capacity : (d + 1) * capacity, :],
                block[...],
                preferred_element_type=F32,
            ).astype(BF16)


def dispatch(placed, slices, experts, capacity, after, echo=False):
    rows, width = slices[0].shape
    wide = width * len(slices)
    return pl.pallas_call(
        functools.partial(
            dispatch_kernel, count=len(slices), waits=len(after), echo=echo
        ),
        out_shape=[jax.ShapeDtypeStruct((capacity, wide), BF16)] * experts
        + [jax.ShapeDtypeStruct((rows, width), BF16)] * echo,
        in_specs=[pl.BlockSpec(memory_space=pltpu.VMEM)] * (1 + len(slices))
        + [pl.BlockSpec(memory_space=pl.ANY)] * len(after),
        out_specs=[pl.BlockSpec(memory_space=pltpu.VMEM)] * (experts + echo),
        cost_estimate=cost(2 * experts * capacity * rows * wide, 6 * rows * wide),
        compiler_params=params(),
        name="dispatch",
    )(placed, *slices, *after)


def across(distance):
    return lambda column: lax.bitwise_xor(column, distance)


def everything(column):
    return 0


def prefetch_kernel(column_ref, after_ref, *refs, parts):
    half = len(refs) // 2
    copies = []
    for i, part in enumerate(parts):
        source, target, sem = refs[i], refs[half + i], refs[-1].at[i]
        count = target.shape[0]
        start = pl.multiple_of(part(column_ref[0]) * count, count)
        copies.append(pltpu.make_async_copy(source.at[0, pl.ds(start, count)], target, sem))
    for copy in copies:
        copy.start()
    for copy in copies:
        copy.wait()


def prefetch(column, fetches, after):
    sources = [pltpu.with_memory_space_constraint(w, pltpu.HBM) for w, _, _ in fetches]
    shapes = [pltpu.VMEM((count, w.shape[2]), w.dtype) for w, _, count in fetches]
    return pl.pallas_call(
        functools.partial(prefetch_kernel, parts=[part for _, part, _ in fetches]),
        out_shape=shapes,
        in_specs=[pl.BlockSpec(memory_space=pltpu.SMEM)]
        + [pl.BlockSpec(memory_space=pl.ANY)] * (1 + len(sources)),
        out_specs=[pl.BlockSpec(memory_space=pltpu.VMEM)] * len(shapes),
        scratch_shapes=[pltpu.SemaphoreType.DMA((len(shapes),))],
        cost_estimate=cost(0, sum(2 * count * w.shape[2] for w, _, count in fetches)),
        compiler_params=params(),
        name="prefetch",
    )(column.reshape(1), after, *sources)


def gate_up_kernel(column_ref, *refs, experts, slices, first, last, waits, parts):
    x_refs = refs[: experts * slices]
    weights = refs[experts * slices : (experts + 2) * slices]
    rest = refs[(experts + 2) * slices :]
    if not first:
        old_gate, old_up = rest[:2]
        rest = rest[2:]
    rest = rest[waits:]
    sources, outs = rest[: len(parts)], rest[len(parts) :]
    copies = []
    for i, part in enumerate(parts):
        target = outs[len(outs) - 1 - len(parts) + i]
        count = target.shape[0]
        start = pl.multiple_of(part(column_ref[0]) * count, count)
        source = sources[i].at[0, pl.ds(start, count)]
        copies.append(pltpu.make_async_copy(source, target, outs[-1].at[i]))
    for copy in copies:
        copy.start()
    x = [
        jnp.concatenate([r[...] for r in x_refs[i * experts : (i + 1) * experts]], axis=0)
        for i in range(slices)
    ]
    hidden = weights[0].shape[1]
    tile = min(512, hidden)

    def step(columns):
        sums = []
        for kind in range(2):
            total = None if first else (old_gate, old_up)[kind][:, columns]
            for i in range(slices):
                term = jnp.dot(
                    x[i], weights[2 * i + kind][:, columns], preferred_element_type=F32
                )
                total = term if total is None else total + term
            sums.append(total)
        gate, up = sums
        if last:
            outs[0][:, columns] = (gate / (1.0 + jnp.exp(-gate)) * up).astype(BF16)
        else:
            outs[0][:, columns] = gate
            outs[1][:, columns] = up

    if copies:

        @pl.loop(0, hidden // tile)
        def _(n):
            step(pl.ds(pl.multiple_of(n * tile, tile), tile))

    else:
        for n in range(hidden // tile):
            step(slice(n * tile, (n + 1) * tile))
    for copy in copies:
        copy.wait()


def gate_up(column, x_slices, weights, sums, last, after, fetches):
    experts = len(x_slices[0])
    x_blocks = [block for blocks in x_slices for block in blocks]
    rows = experts * x_blocks[0].shape[0]
    hidden = weights[0].shape[1]
    first = sums is None
    old = [] if first else pinned(sums)
    before = 1 + len(x_blocks) + len(weights)
    sources = [pltpu.with_memory_space_constraint(w, pltpu.HBM) for w, _, _ in fetches]
    if last:
        out_shape = [pltpu.VMEM((rows, hidden), BF16)]
    else:
        out_shape = [pltpu.VMEM((rows, hidden), F32)] * 2
    shapes = out_shape + [pltpu.VMEM((count, w.shape[2]), w.dtype) for w, _, count in fetches]
    results = pl.pallas_call(
        functools.partial(
            gate_up_kernel,
            experts=experts,
            slices=len(x_slices),
            first=first,
            last=last,
            waits=len(after),
            parts=[part for _, part, _ in fetches],
        ),
        out_shape=shapes,
        in_specs=[pl.BlockSpec(memory_space=pltpu.SMEM)]
        + [pl.BlockSpec(memory_space=pltpu.VMEM)] * (before - 1 + len(old))
        + [pl.BlockSpec(memory_space=pl.ANY)] * (len(after) + len(sources)),
        out_specs=[pl.BlockSpec(memory_space=pltpu.VMEM)] * len(shapes),
        scratch_shapes=[pltpu.SemaphoreType.DMA((len(fetches),))] if fetches else [],
        input_output_aliases={} if first or last else {before: 0, before + 1: 1},
        cost_estimate=cost(
            2 * rows * hidden * sum(w.shape[0] for w in weights),
            sum(2 * w.size for w in weights),
        ),
        compiler_params=params(),
        name="gate_up",
    )(column.reshape(1), *x_blocks, *pinned(weights), *old, *after, *sources)
    return results[: len(out_shape)], list(results[len(out_shape) :])


def down_kernel(column_ref, h_ref, w_ref, *refs, part, waits):
    out_refs = refs[waits:]
    capacity, width = out_refs[0].shape
    tile = min(256, width)
    for n in range(width // tile):
        start = pl.multiple_of(part(column_ref[0]) * width + n * tile, tile)
        y = jnp.dot(h_ref[...], w_ref[0, :, pl.ds(start, tile)], preferred_element_type=F32)
        columns = slice(n * tile, (n + 1) * tile)
        for d, out in enumerate(out_refs):
            out[:, columns] = y[d * capacity : (d + 1) * capacity].astype(BF16)


def down(column, part, hidden, down_w, width, experts, after):
    rows, depth = hidden.shape
    capacity = rows // experts
    return pl.pallas_call(
        functools.partial(down_kernel, part=part, waits=len(after)),
        out_shape=[jax.ShapeDtypeStruct((capacity, width), BF16)] * experts,
        in_specs=[pl.BlockSpec(memory_space=pltpu.SMEM)]
        + [pl.BlockSpec(memory_space=pltpu.VMEM)] * 2
        + [pl.BlockSpec(memory_space=pl.ANY)] * len(after),
        out_specs=[pl.BlockSpec(memory_space=pltpu.VMEM)] * experts,
        cost_estimate=cost(2 * rows * depth * width, 2 * depth * width + 2 * rows * width),
        compiler_params=params(),
        name="down",
    )(column.reshape(1), *pinned([hidden, down_w]), *after)


def combine_kernel(pick_ref, mix_ref, *refs, experts, starts):
    y_refs, added = refs[:experts], refs[experts : experts + len(starts)]
    outs = refs[experts + len(starts) :]
    width = y_refs[0].shape[1]
    rows, part = outs[0].shape
    y = jnp.concatenate([r[...] for r in y_refs], axis=0)
    picked = lax.dot_general(
        pick_ref[...], y, (((0,), (0,)), ((), ())), preferred_element_type=F32
    )
    mixed = picked[:rows] * mix_ref[:, 0:1] + picked[rows:] * mix_ref[:, 1:2]
    for other, start in zip(added, starts):
        value = other[...].astype(F32)
        stop = start + value.shape[1]
        pieces = [mixed[:, :start]] * (start > 0) + [mixed[:, start:stop] + value]
        pieces += [mixed[:, stop:]] * (stop < width)
        mixed = jnp.concatenate(pieces, axis=1) if len(pieces) > 1 else pieces[0]
    for i, out in enumerate(outs):
        out[...] = mixed[:, i * part : (i + 1) * part].astype(BF16)


def combine(pick, mix, blocks, added, cuts=1):
    rows = mix.shape[0]
    width = blocks[0].shape[1]
    operands = 2 + len(blocks) + len(added)
    return pl.pallas_call(
        functools.partial(
            combine_kernel, experts=len(blocks), starts=[start for _, start in added]
        ),
        out_shape=[jax.ShapeDtypeStruct((rows, width // cuts), BF16)] * cuts,
        in_specs=[pl.BlockSpec(memory_space=pltpu.VMEM)] * operands,
        out_specs=[pl.BlockSpec(memory_space=pltpu.VMEM)] * cuts,
        cost_estimate=cost(4 * rows * pick.shape[0] * width, 6 * rows * width),
        compiler_params=params(),
        name="combine",
    )(pick, mix, *blocks, *[array for array, _ in added])


def swap(value, axis, distance):
    if not distance:
        return value
    count = lax.axis_size(axis)
    return lax.ppermute(value, axis, [(i, i ^ distance) for i in range(count)])


def per_device(tokens, expert_ids, route_logits, gate_weight, up_weight, down_weight):
    rows, own_width = tokens.shape
    experts = lax.axis_size("expert")
    shards = lax.axis_size("tensor")
    capacity = rows // 2
    me = lax.axis_index("expert").astype(jnp.int32)
    column = lax.axis_index("tensor").astype(jnp.int32)
    doubling = shards == 4
    width = own_width if doubling else own_width * shards

    if doubling:
        slices = [tokens, swap(tokens, "tensor", 1), swap(tokens, "tensor", 2)]
        parts = [across(distance) for distance in range(4)]
    else:
        slices = [lax.all_gather(tokens, "tensor", axis=1, tiled=True)]
        parts = [everything]
    placed, pick, mix = place(me, expert_ids, route_logits, experts, capacity)

    fetches = [(w, part, width) for part in parts for w in (gate_weight, up_weight)]
    arrived, weights = [], []
    for i in range(len(parts)):
        echo = i == 2
        after = pinned(weights[:1]) + (arrived[0][2:] if echo else [])
        outgoing = dispatch(placed, [slices[i]], experts, capacity, after, echo)
        blocks = outgoing[:experts]
        arrived.append([swap(block, "expert", e) for e, block in enumerate(blocks)])
        if echo:
            slices.append(swap(outgoing[-1], "tensor", 1))
        if not weights:
            weights = list(prefetch(column, fetches[:4], outgoing[0]))
    sums = None
    for group in [slice(0, 2), slice(2, 3), slice(3, 4)][: max(1, len(parts) - 1)]:
        first = sums is None
        last = group.stop >= len(parts)
        after = arrived[2][1:2] + arrived[3][1:2] if first and not last else []
        chosen = weights[2 * group.start : 2 * group.stop]
        later = fetches[4:] if first else []
        sums, brought = gate_up(column, arrived[group], chosen, sums, last, after, later)
        weights += brought
    hidden = sums[0]

    def returned(part, after=()):
        terms = down(column, part, hidden, down_weight, width, experts, after)
        return [swap(block, "expert", e) for e, block in enumerate(terms)]

    if not doubling:
        mixed = combine(pick, mix, returned(everything), [])[0]
        return lax.psum_scatter(mixed, "tensor", scatter_dimension=1, tiled=True)
    low, high = combine(pick, mix, returned(across(3)), [], cuts=2)
    passed = swap(low, "tensor", 1)
    far = (swap(high, "tensor", 3), width // 2)
    onwards = combine(pick, mix, returned(across(2)), [(passed, 0)])[0]
    over = (swap(onwards, "tensor", 2), 0)
    near = combine(pick, mix, returned(across(1), [low]), [])[0]
    beside = (swap(near, "tensor", 1), 0)
    return combine(pick, mix, returned(across(0), [passed]), [beside, over, far])[0]


def solution(mesh):
    in_specs = (
        P(("groups", "expert"), "tensor"),
        P(("groups", "expert"), None),
        P(("groups", "expert"), None),
        P("expert", None, "tensor"),
        P("expert", None, "tensor"),
        P("expert", "tensor", None),
    )
    out_specs = P(("groups", "expert"), "tensor")
    return jax.shard_map(
        per_device, mesh=mesh, in_specs=in_specs, out_specs=out_specs, check_vma=False
    )
```

```python
import functools

import jax
import jax.numpy as jnp
from jax import lax
from jax.experimental import pallas as pl
from jax.experimental.pallas import tpu as pltpu
from jax.sharding import PartitionSpec as P

F32 = jnp.float32
BF16 = jnp.bfloat16
MIB = 1024 * 1024


def params(mib=6):
    return pltpu.CompilerParams(vmem_limit_bytes=mib * MIB)


def cost(flops, moved):
    return pl.CostEstimate(flops=flops, bytes_accessed=moved, transcendentals=0)


def pinned(arrays):
    return [pltpu.with_memory_space_constraint(array, pltpu.VMEM) for array in arrays]


def routing_kernel(me_ref, ids_ref, logits_ref, placed_ref, pick_ref, mix_ref, *, experts):
    rows = ids_ref.shape[1]
    capacity = placed_ref.shape[0] // experts
    relative = lax.bitwise_xor(ids_ref[...], me_ref[0])
    lane = lax.broadcasted_iota(jnp.int32, (experts, rows), 0)
    names = [lane == relative[k : k + 1] for k in range(2)]
    named = names[0] | names[1]
    row = lax.broadcasted_iota(jnp.int32, (rows, rows), 0)
    column = lax.broadcasted_iota(jnp.int32, (rows, rows), 1)
    before = jnp.dot(
        jnp.where(named, 1.0, 0.0).astype(BF16),
        jnp.where(row < column, 1.0, 0.0).astype(BF16),
        preferred_element_type=F32,
    ).astype(jnp.int32)
    slot = lax.broadcasted_iota(jnp.int32, (capacity, rows), 0)
    for d in range(experts):
        here = slice(d * capacity, (d + 1) * capacity)
        both = None
        for k in range(2):
            position = jnp.where(names[k], before, -1)
            hit = jnp.where(position[d : d + 1] == slot, 1.0, 0.0)
            pick_ref[here, k * rows : (k + 1) * rows] = hit.astype(BF16)
            both = hit if k == 0 else both + hit
        placed_ref[here, :] = both.astype(BF16)
    share = 1.0 / (1.0 + jnp.exp(logits_ref[1:2] - logits_ref[0:1]))
    share = jnp.sum(jnp.where(row == column, share, 0.0), axis=1, keepdims=True)
    mix_ref[:, 0:1] = share
    mix_ref[:, 1:2] = 1.0 - share


def place(me, expert_ids, route_logits, experts, capacity):
    rows = expert_ids.shape[0]
    return pl.pallas_call(
        functools.partial(routing_kernel, experts=experts),
        out_shape=[
            jax.ShapeDtypeStruct((experts * capacity, rows), BF16),
            jax.ShapeDtypeStruct((experts * capacity, 2 * rows), BF16),
            jax.ShapeDtypeStruct((rows, 2), F32),
        ],
        in_specs=[pl.BlockSpec(memory_space=pltpu.SMEM)]
        + [pl.BlockSpec(memory_space=pltpu.VMEM)] * 2,
        out_specs=[pl.BlockSpec(memory_space=pltpu.VMEM)] * 3,
        compiler_params=params(),
        name="routing",
    )(me.reshape(1), expert_ids.T, route_logits.T)


def dispatch_kernel(placed_ref, *refs, count, waits, echo):
    inputs, outputs = refs[:count], refs[count + waits :]
    if echo:
        outputs[-1][...] = inputs[0][...]
        outputs = outputs[:-1]
    capacity, wide = outputs[0].shape
    width = wide // count
    for i, block in enumerate(inputs):
        for d, out in enumerate(outputs):
            out[:, i * width : (i + 1) * width] = jnp.dot(
                placed_ref[d * capacity : (d + 1) * capacity, :],
                block[...],
                preferred_element_type=F32,
            ).astype(BF16)


def dispatch(placed, slices, experts, capacity, after, echo=False):
    rows, width = slices[0].shape
    wide = width * len(slices)
    return pl.pallas_call(
        functools.partial(
            dispatch_kernel, count=len(slices), waits=len(after), echo=echo
        ),
        out_shape=[jax.ShapeDtypeStruct((capacity, wide), BF16)] * experts
        + [jax.ShapeDtypeStruct((rows, width), BF16)] * echo,
        in_specs=[pl.BlockSpec(memory_space=pltpu.VMEM)] * (1 + len(slices))
        + [pl.BlockSpec(memory_space=pl.ANY)] * len(after),
        out_specs=[pl.BlockSpec(memory_space=pltpu.VMEM)] * (experts + echo),
        cost_estimate=cost(2 * experts * capacity * rows * wide, 6 * rows * wide),
        compiler_params=params(),
        name="dispatch",
    )(placed, *slices, *after)


def across(distance):
    return lambda column: lax.bitwise_xor(column, distance)


def everything(column):
    return 0


def prefetch_kernel(column_ref, after_ref, *refs, parts):
    half = len(refs) // 2
    copies = []
    for i, part in enumerate(parts):
        source, target, sem = refs[i], refs[half + i], refs[-1].at[i]
        count = target.shape[0]
        start = pl.multiple_of(part(column_ref[0]) * count, count)
        copies.append(pltpu.make_async_copy(source.at[0, pl.ds(start, count)], target, sem))
    for copy in copies:
        copy.start()
    for copy in copies:
        copy.wait()


def prefetch(column, fetches, after):
    sources = [pltpu.with_memory_space_constraint(w, pltpu.HBM) for w, _, _ in fetches]
    shapes = [pltpu.VMEM((count, w.shape[2]), w.dtype) for w, _, count in fetches]
    return pl.pallas_call(
        functools.partial(prefetch_kernel, parts=[part for _, part, _ in fetches]),
        out_shape=shapes,
        in_specs=[pl.BlockSpec(memory_space=pltpu.SMEM)]
        + [pl.BlockSpec(memory_space=pl.ANY)] * (1 + len(sources)),
        out_specs=[pl.BlockSpec(memory_space=pltpu.VMEM)] * len(shapes),
        scratch_shapes=[pltpu.SemaphoreType.DMA((len(shapes),))],
        cost_estimate=cost(0, sum(2 * count * w.shape[2] for w, _, count in fetches)),
        compiler_params=params(),
        name="prefetch",
    )(column.reshape(1), after, *sources)


def gate_up_kernel(column_ref, *refs, experts, slices, first, last, waits, parts):
    x_refs = refs[: experts * slices]
    weights = refs[experts * slices : (experts + 2) * slices]
    rest = refs[(experts + 2) * slices :]
    if not first:
        old_gate, old_up = rest[:2]
        rest = rest[2:]
    rest = rest[waits:]
    sources, outs = rest[: len(parts)], rest[len(parts) :]
    copies = []
    for i, part in enumerate(parts):
        target = outs[len(outs) - 1 - len(parts) + i]
        count = target.shape[0]
        start = pl.multiple_of(part(column_ref[0]) * count, count)
        source = sources[i].at[0, pl.ds(start, count)]
        copies.append(pltpu.make_async_copy(source, target, outs[-1].at[i]))
    for copy in copies:
        copy.start()
    x = [
        jnp.concatenate([r[...] for r in x_refs[i * experts : (i + 1) * experts]], axis=0)
        for i in range(slices)
    ]
    hidden = weights[0].shape[1]
    tile = min(512, hidden)

    def step(columns):
        sums = []
        for kind in range(2):
            total = None if first else (old_gate, old_up)[kind][:, columns]
            for i in range(slices):
                term = jnp.dot(
                    x[i], weights[2 * i + kind][:, columns], preferred_element_type=F32
                )
                total = term if total is None else total + term
            sums.append(total)
        gate, up = sums
        if last:
            outs[0][:, columns] = (gate / (1.0 + jnp.exp(-gate)) * up).astype(BF16)
        else:
            outs[0][:, columns] = gate
            outs[1][:, columns] = up

    if copies:

        @pl.loop(0, hidden // tile)
        def _(n):
            step(pl.ds(pl.multiple_of(n * tile, tile), tile))

    else:
        for n in range(hidden // tile):
            step(slice(n * tile, (n + 1) * tile))
    for copy in copies:
        copy.wait()


def gate_up(column, x_slices, weights, sums, last, after, fetches):
    experts = len(x_slices[0])
    x_blocks = [block for blocks in x_slices for block in blocks]
    rows = experts * x_blocks[0].shape[0]
    hidden = weights[0].shape[1]
    first = sums is None
    old = [] if first else pinned(sums)
    before = 1 + len(x_blocks) + len(weights)
    sources = [pltpu.with_memory_space_constraint(w, pltpu.HBM) for w, _, _ in fetches]
    if last:
        out_shape = [pltpu.VMEM((rows, hidden), BF16)]
    else:
        out_shape = [pltpu.VMEM((rows, hidden), F32)] * 2
    shapes = out_shape + [pltpu.VMEM((count, w.shape[2]), w.dtype) for w, _, count in fetches]
    results = pl.pallas_call(
        functools.partial(
            gate_up_kernel,
            experts=experts,
            slices=len(x_slices),
            first=first,
            last=last,
            waits=len(after),
            parts=[part for _, part, _ in fetches],
        ),
        out_shape=shapes,
        in_specs=[pl.BlockSpec(memory_space=pltpu.SMEM)]
        + [pl.BlockSpec(memory_space=pltpu.VMEM)] * (before - 1 + len(old))
        + [pl.BlockSpec(memory_space=pl.ANY)] * (len(after) + len(sources)),
        out_specs=[pl.BlockSpec(memory_space=pltpu.VMEM)] * len(shapes),
        scratch_shapes=[pltpu.SemaphoreType.DMA((len(fetches),))] if fetches else [],
        input_output_aliases={} if first or last else {before: 0, before + 1: 1},
        cost_estimate=cost(
            2 * rows * hidden * sum(w.shape[0] for w in weights),
            sum(2 * w.size for w in weights),
        ),
        compiler_params=params(),
        name="gate_up",
    )(column.reshape(1), *x_blocks, *pinned(weights), *old, *after, *sources)
    return results[: len(out_shape)], list(results[len(out_shape) :])


def down_kernel(column_ref, h_ref, w_ref, *refs, part, waits):
    out_refs = refs[waits:]
    capacity, width = out_refs[0].shape
    tile = min(256, width)
    for n in range(width // tile):
        start = pl.multiple_of(part(column_ref[0]) * width + n * tile, tile)
        y = jnp.dot(h_ref[...], w_ref[0, :, pl.ds(start, tile)], preferred_element_type=F32)
        columns = slice(n * tile, (n + 1) * tile)
        for d, out in enumerate(out_refs):
            out[:, columns] = y[d * capacity : (d + 1) * capacity].astype(BF16)


def down(column, part, hidden, down_w, width, experts, after):
    rows, depth = hidden.shape
    capacity = rows // experts
    return pl.pallas_call(
        functools.partial(down_kernel, part=part, waits=len(after)),
        out_shape=[jax.ShapeDtypeStruct((capacity, width), BF16)] * experts,
        in_specs=[pl.BlockSpec(memory_space=pltpu.SMEM)]
        + [pl.BlockSpec(memory_space=pltpu.VMEM)] * 2
        + [pl.BlockSpec(memory_space=pl.ANY)] * len(after),
        out_specs=[pl.BlockSpec(memory_space=pltpu.VMEM)] * experts,
        cost_estimate=cost(2 * rows * depth * width, 2 * depth * width + 2 * rows * width),
        compiler_params=params(),
        name="down",
    )(column.reshape(1), *pinned([hidden, down_w]), *after)


def combine_kernel(pick_ref, mix_ref, *refs, experts, starts):
    y_refs, added = refs[:experts], refs[experts : experts + len(starts)]
    outs = refs[experts + len(starts) :]
    width = y_refs[0].shape[1]
    rows, part = outs[0].shape
    y = jnp.concatenate([r[...] for r in y_refs], axis=0)
    picked = lax.dot_general(
        pick_ref[...], y, (((0,), (0,)), ((), ())), preferred_element_type=F32
    )
    mixed = picked[:rows] * mix_ref[:, 0:1] + picked[rows:] * mix_ref[:, 1:2]
    for other, start in zip(added, starts):
        value = other[...].astype(F32)
        stop = start + value.shape[1]
        pieces = [mixed[:, :start]] * (start > 0) + [mixed[:, start:stop] + value]
        pieces += [mixed[:, stop:]] * (stop < width)
        mixed = jnp.concatenate(pieces, axis=1) if len(pieces) > 1 else pieces[0]
    for i, out in enumerate(outs):
        out[...] = mixed[:, i * part : (i + 1) * part].astype(BF16)


def combine(pick, mix, blocks, added, cuts=1):
    rows = mix.shape[0]
    width = blocks[0].shape[1]
    operands = 2 + len(blocks) + len(added)
    return pl.pallas_call(
        functools.partial(
            combine_kernel, experts=len(blocks), starts=[start for _, start in added]
        ),
        out_shape=[jax.ShapeDtypeStruct((rows, width // cuts), BF16)] * cuts,
        in_specs=[pl.BlockSpec(memory_space=pltpu.VMEM)] * operands,
        out_specs=[pl.BlockSpec(memory_space=pltpu.VMEM)] * cuts,
        cost_estimate=cost(4 * rows * pick.shape[0] * width, 6 * rows * width),
        compiler_params=params(),
        name="combine",
    )(pick, mix, *blocks, *[array for array, _ in added])


def swap(value, axis, distance):
    if not distance:
        return value
    count = lax.axis_size(axis)
    return lax.ppermute(value, axis, [(i, i ^ distance) for i in range(count)])


def per_device(tokens, expert_ids, route_logits, gate_weight, up_weight, down_weight):
    rows, own_width = tokens.shape
    experts = lax.axis_size("expert")
    shards = lax.axis_size("tensor")
    capacity = rows // 2
    me = lax.axis_index("expert").astype(jnp.int32)
    column = lax.axis_index("tensor").astype(jnp.int32)
    doubling = shards == 4
    width = own_width if doubling else own_width * shards

    if doubling:
        slices = [tokens, swap(tokens, "tensor", 2), swap(tokens, "tensor", 1)]
        parts = [across(distance) for distance in (0, 2, 1, 3)]
    else:
        slices = [lax.all_gather(tokens, "tensor", axis=1, tiled=True)]
        parts = [everything]
    placed, pick, mix = place(me, expert_ids, route_logits, experts, capacity)

    fetches = [(w, part, width) for part in parts for w in (gate_weight, up_weight)]
    arrived, weights = [], []
    for i in range(len(parts)):
        echo = i == 1
        after = pinned(weights[:1])
        if echo:
            after += arrived[0][2:]
        elif i == 2:
            after += arrived[1][1:2]
        elif i == 3:
            after += arrived[2][2:]
        outgoing = dispatch(placed, [slices[i]], experts, capacity, after, echo)
        blocks = outgoing[:experts]
        arrived.append([swap(block, "expert", e) for e, block in enumerate(blocks)])
        if echo:
            slices.append(swap(outgoing[-1], "tensor", 1))
        if not weights:
            weights = list(prefetch(column, fetches[:4], outgoing[0]))
    sums = None
    for group in [slice(0, 2), slice(2, 3), slice(3, 4)][: max(1, len(parts) - 1)]:
        first = sums is None
        last = group.stop >= len(parts)
        after = arrived[2][1:2] if first and not last else []
        chosen = weights[2 * group.start : 2 * group.stop]
        later = fetches[4:] if first else []
        sums, brought = gate_up(column, arrived[group], chosen, sums, last, after, later)
        weights += brought
    hidden = sums[0]

    def returned(part, after=()):
        terms = down(column, part, hidden, down_weight, width, experts, after)
        return [swap(block, "expert", e) for e, block in enumerate(terms)]

    if not doubling:
        mixed = combine(pick, mix, returned(everything), [])[0]
        return lax.psum_scatter(mixed, "tensor", scatter_dimension=1, tiled=True)
    low, high = combine(pick, mix, returned(across(3)), [], cuts=2)
    passed = swap(low, "tensor", 1)
    far = (swap(high, "tensor", 3), width // 2)
    onwards = combine(pick, mix, returned(across(2)), [(passed, 0)])[0]
    over = (swap(onwards, "tensor", 2), 0)
    near = combine(pick, mix, returned(across(1), [low]), [])[0]
    beside = (swap(near, "tensor", 1), 0)
    return combine(pick, mix, returned(across(0), [passed]), [beside, over, far])[0]


def solution(mesh):
    in_specs = (
        P(("groups", "expert"), "tensor"),
        P(("groups", "expert"), None),
        P(("groups", "expert"), None),
        P("expert", None, "tensor"),
        P("expert", None, "tensor"),
        P("expert", "tensor", None),
    )
    out_specs = P(("groups", "expert"), "tensor")
    return jax.shard_map(
        per_device, mesh=mesh, in_specs=in_specs, out_specs=out_specs, check_vma=False
    )
```

```python
import functools

import jax
import jax.numpy as jnp
from jax import lax
from jax.experimental import pallas as pl
from jax.experimental.pallas import tpu as pltpu
from jax.sharding import PartitionSpec as P

F32 = jnp.float32
BF16 = jnp.bfloat16
MIB = 1024 * 1024


def params(mib=6):
    return pltpu.CompilerParams(vmem_limit_bytes=mib * MIB)


def cost(flops, moved):
    return pl.CostEstimate(flops=flops, bytes_accessed=moved, transcendentals=0)


def pinned(arrays):
    return [pltpu.with_memory_space_constraint(array, pltpu.VMEM) for array in arrays]


def routing_kernel(me_ref, ids_ref, logits_ref, placed_ref, pick_ref, mix_ref, *, experts):
    rows = ids_ref.shape[1]
    capacity = placed_ref.shape[0] // experts
    relative = lax.bitwise_xor(ids_ref[...], me_ref[0])
    lane = lax.broadcasted_iota(jnp.int32, (experts, rows), 0)
    names = [lane == relative[k : k + 1] for k in range(2)]
    named = names[0] | names[1]
    row = lax.broadcasted_iota(jnp.int32, (rows, rows), 0)
    column = lax.broadcasted_iota(jnp.int32, (rows, rows), 1)
    before = jnp.dot(
        jnp.where(named, 1.0, 0.0).astype(BF16),
        jnp.where(row < column, 1.0, 0.0).astype(BF16),
        preferred_element_type=F32,
    ).astype(jnp.int32)
    slot = lax.broadcasted_iota(jnp.int32, (capacity, rows), 0)
    for d in range(experts):
        here = slice(d * capacity, (d + 1) * capacity)
        both = None
        for k in range(2):
            position = jnp.where(names[k], before, -1)
            hit = jnp.where(position[d : d + 1] == slot, 1.0, 0.0)
            pick_ref[here, k * rows : (k + 1) * rows] = hit.astype(BF16)
            both = hit if k == 0 else both + hit
        placed_ref[here, :] = both.astype(BF16)
    share = 1.0 / (1.0 + jnp.exp(logits_ref[1:2] - logits_ref[0:1]))
    share = jnp.sum(jnp.where(row == column, share, 0.0), axis=1, keepdims=True)
    mix_ref[:, 0:1] = share
    mix_ref[:, 1:2] = 1.0 - share


def place(me, expert_ids, route_logits, experts, capacity):
    rows = expert_ids.shape[0]
    return pl.pallas_call(
        functools.partial(routing_kernel, experts=experts),
        out_shape=[
            jax.ShapeDtypeStruct((experts * capacity, rows), BF16),
            jax.ShapeDtypeStruct((experts * capacity, 2 * rows), BF16),
            jax.ShapeDtypeStruct((rows, 2), F32),
        ],
        in_specs=[pl.BlockSpec(memory_space=pltpu.SMEM)]
        + [pl.BlockSpec(memory_space=pltpu.VMEM)] * 2,
        out_specs=[pl.BlockSpec(memory_space=pltpu.VMEM)] * 3,
        compiler_params=params(),
        name="routing",
    )(me.reshape(1), expert_ids.T, route_logits.T)


def dispatch_kernel(placed_ref, *refs, count, waits):
    inputs, outputs = refs[:count], refs[count + waits :]
    capacity, wide = outputs[0].shape
    width = wide // count
    for i, block in enumerate(inputs):
        for d, out in enumerate(outputs):
            out[:, i * width : (i + 1) * width] = jnp.dot(
                placed_ref[d * capacity : (d + 1) * capacity, :],
                block[...],
                preferred_element_type=F32,
            ).astype(BF16)


def dispatch(placed, slices, experts, capacity, after):
    rows, width = slices[0].shape
    wide = width * len(slices)
    return pl.pallas_call(
        functools.partial(dispatch_kernel, count=len(slices), waits=len(after)),
        out_shape=[jax.ShapeDtypeStruct((capacity, wide), BF16)] * experts,
        in_specs=[pl.BlockSpec(memory_space=pltpu.VMEM)] * (1 + len(slices))
        + [pl.BlockSpec(memory_space=pl.ANY)] * len(after),
        out_specs=[pl.BlockSpec(memory_space=pltpu.VMEM)] * experts,
        cost_estimate=cost(2 * experts * capacity * rows * wide, 6 * rows * wide),
        compiler_params=params(),
        name="dispatch",
    )(placed, *slices, *pinned(after))


def across(distance):
    return lambda column: lax.bitwise_xor(column, distance)


def everything(column):
    return 0


def prefetch_kernel(column_ref, after_ref, *refs, parts):
    half = len(refs) // 2
    copies = []
    for i, part in enumerate(parts):
        source, target, sem = refs[i], refs[half + i], refs[-1].at[i]
        count = target.shape[0]
        start = pl.multiple_of(part(column_ref[0]) * count, count)
        copies.append(pltpu.make_async_copy(source.at[0, pl.ds(start, count)], target, sem))
    for copy in copies:
        copy.start()
    for copy in copies:
        copy.wait()


def prefetch(column, fetches, after):
    sources = [pltpu.with_memory_space_constraint(w, pltpu.HBM) for w, _, _ in fetches]
    shapes = [pltpu.VMEM((count, w.shape[2]), w.dtype) for w, _, count in fetches]
    return pl.pallas_call(
        functools.partial(prefetch_kernel, parts=[part for _, part, _ in fetches]),
        out_shape=shapes,
        in_specs=[pl.BlockSpec(memory_space=pltpu.SMEM)]
        + [pl.BlockSpec(memory_space=pl.ANY)] * (1 + len(sources)),
        out_specs=[pl.BlockSpec(memory_space=pltpu.VMEM)] * len(shapes),
        scratch_shapes=[pltpu.SemaphoreType.DMA((len(shapes),))],
        cost_estimate=cost(0, sum(2 * count * w.shape[2] for w, _, count in fetches)),
        compiler_params=params(),
        name="prefetch",
    )(column.reshape(1), after, *sources)


def gate_up_kernel(*refs, experts, slices, first, last, waits):
    x_refs = refs[:experts]
    weights = refs[experts : experts + 2 * slices]
    rest = refs[experts + 2 * slices :]
    if not first:
        old_gate, old_up = rest[:2]
        rest = rest[2:]
    rest = rest[waits:]
    x = jnp.concatenate([r[...] for r in x_refs], axis=0)
    width, hidden = weights[0].shape
    tile = min(512, hidden)
    for n in range(hidden // tile):
        columns = slice(n * tile, (n + 1) * tile)
        sums = []
        for kind in range(2):
            total = None if first else (old_gate, old_up)[kind][:, columns]
            for i in range(slices):
                term = jnp.dot(
                    x[:, i * width : (i + 1) * width],
                    weights[2 * i + kind][:, columns],
                    preferred_element_type=F32,
                )
                total = term if total is None else total + term
            sums.append(total)
        gate, up = sums
        if last:
            rest[0][:, columns] = (gate / (1.0 + jnp.exp(-gate)) * up).astype(BF16)
        else:
            rest[0][:, columns] = gate
            rest[1][:, columns] = up


def gate_up(x_blocks, weights, sums, last, after):
    experts = len(x_blocks)
    rows = experts * x_blocks[0].shape[0]
    hidden = weights[0].shape[1]
    first = sums is None
    old = [] if first else pinned(sums)
    before = experts + len(weights)
    if last:
        out_shape = [pltpu.VMEM((rows, hidden), BF16)]
    else:
        out_shape = [pltpu.VMEM((rows, hidden), F32)] * 2
    return pl.pallas_call(
        functools.partial(
            gate_up_kernel,
            experts=experts,
            slices=len(weights) // 2,
            first=first,
            last=last,
            waits=len(after),
        ),
        out_shape=out_shape,
        in_specs=[pl.BlockSpec(memory_space=pltpu.VMEM)] * (before + len(old))
        + [pl.BlockSpec(memory_space=pl.ANY)] * len(after),
        out_specs=[pl.BlockSpec(memory_space=pltpu.VMEM)] * len(out_shape),
        input_output_aliases={} if first or last else {before: 0, before + 1: 1},
        cost_estimate=cost(
            2 * rows * hidden * sum(w.shape[0] for w in weights),
            sum(2 * w.size for w in weights),
        ),
        compiler_params=params(),
        name="gate_up",
    )(*x_blocks, *pinned(weights), *old, *after)


def down_kernel(column_ref, h_ref, w_ref, *refs, part, waits):
    out_refs = refs[waits:]
    capacity, width = out_refs[0].shape
    tile = min(256, width)
    for n in range(width // tile):
        start = pl.multiple_of(part(column_ref[0]) * width + n * tile, tile)
        y = jnp.dot(h_ref[...], w_ref[0, :, pl.ds(start, tile)], preferred_element_type=F32)
        columns = slice(n * tile, (n + 1) * tile)
        for d, out in enumerate(out_refs):
            out[:, columns] = y[d * capacity : (d + 1) * capacity].astype(BF16)


def down(column, part, hidden, down_w, width, experts, after):
    rows, depth = hidden.shape
    capacity = rows // experts
    return pl.pallas_call(
        functools.partial(down_kernel, part=part, waits=len(after)),
        out_shape=[jax.ShapeDtypeStruct((capacity, width), BF16)] * experts,
        in_specs=[pl.BlockSpec(memory_space=pltpu.SMEM)]
        + [pl.BlockSpec(memory_space=pltpu.VMEM)] * 2
        + [pl.BlockSpec(memory_space=pl.ANY)] * len(after),
        out_specs=[pl.BlockSpec(memory_space=pltpu.VMEM)] * experts,
        cost_estimate=cost(2 * rows * depth * width, 2 * depth * width + 2 * rows * width),
        compiler_params=params(),
        name="down",
    )(column.reshape(1), *pinned([hidden, down_w]), *after)


def combine_kernel(pick_ref, mix_ref, *refs, experts, starts):
    y_refs, added = refs[:experts], refs[experts : experts + len(starts)]
    outs = refs[experts + len(starts) :]
    width = y_refs[0].shape[1]
    rows, part = outs[0].shape
    y = jnp.concatenate([r[...] for r in y_refs], axis=0)
    picked = lax.dot_general(
        pick_ref[...], y, (((0,), (0,)), ((), ())), preferred_element_type=F32
    )
    mixed = picked[:rows] * mix_ref[:, 0:1] + picked[rows:] * mix_ref[:, 1:2]
    for other, start in zip(added, starts):
        value = other[...].astype(F32)
        stop = start + value.shape[1]
        pieces = [mixed[:, :start]] * (start > 0) + [mixed[:, start:stop] + value]
        pieces += [mixed[:, stop:]] * (stop < width)
        mixed = jnp.concatenate(pieces, axis=1) if len(pieces) > 1 else pieces[0]
    for i, out in enumerate(outs):
        out[...] = mixed[:, i * part : (i + 1) * part].astype(BF16)


def combine(pick, mix, blocks, added, cuts=1):
    rows = mix.shape[0]
    width = blocks[0].shape[1]
    operands = 2 + len(blocks) + len(added)
    return pl.pallas_call(
        functools.partial(
            combine_kernel, experts=len(blocks), starts=[start for _, start in added]
        ),
        out_shape=[jax.ShapeDtypeStruct((rows, width // cuts), BF16)] * cuts,
        in_specs=[pl.BlockSpec(memory_space=pltpu.VMEM)] * operands,
        out_specs=[pl.BlockSpec(memory_space=pltpu.VMEM)] * cuts,
        cost_estimate=cost(4 * rows * pick.shape[0] * width, 6 * rows * width),
        compiler_params=params(),
        name="combine",
    )(pick, mix, *blocks, *[array for array, _ in added])


def swap(value, axis, distance):
    if not distance:
        return value
    count = lax.axis_size(axis)
    return lax.ppermute(value, axis, [(i, i ^ distance) for i in range(count)])


def per_device(tokens, expert_ids, route_logits, gate_weight, up_weight, down_weight):
    rows, own_width = tokens.shape
    experts = lax.axis_size("expert")
    shards = lax.axis_size("tensor")
    capacity = rows // 2
    me = lax.axis_index("expert").astype(jnp.int32)
    column = lax.axis_index("tensor").astype(jnp.int32)
    doubling = shards == 4
    width = own_width if doubling else own_width * shards

    if doubling:
        across_two = swap(tokens, "tensor", 2)
        slices = [tokens, swap(tokens, "tensor", 1), across_two, swap(across_two, "tensor", 1)]
        parts = [across(distance) for distance in range(4)]
        groups = [[0, 1], [2], [3]]
    else:
        slices = [lax.all_gather(tokens, "tensor", axis=1, tiled=True)]
        parts = [everything]
        groups = [[0]]
    placed, pick, mix = place(me, expert_ids, route_logits, experts, capacity)

    def fetch(chosen, after):
        fetches = [(w, parts[i], width) for i in chosen for w in (gate_weight, up_weight)]
        return list(prefetch(column, fetches, after))

    weights, arrived = fetch(groups[0], placed), []
    for group in groups:
        after = weights[-1:] if len(arrived) < 2 else []
        outgoing = dispatch(placed, [slices[i] for i in group], experts, capacity, after)
        arrived.append([swap(block, "expert", e) for e, block in enumerate(outgoing)])
        if len(arrived) == 1 and len(groups) > 1:
            weights += fetch([2, 3], outgoing[0])
    sums = None
    for group, x_blocks in zip(groups, arrived):
        chosen = weights[2 * group[0] : 2 * group[-1] + 2]
        after = arrived[1][1:2] if sums is None and len(groups) > 1 else []
        sums = gate_up(x_blocks, chosen, sums, group is groups[-1], after)
    hidden = sums[0]

    def returned(part, after=()):
        terms = down(column, part, hidden, down_weight, width, experts, after)
        return [swap(block, "expert", e) for e, block in enumerate(terms)]

    if not doubling:
        mixed = combine(pick, mix, returned(everything), [])[0]
        return lax.psum_scatter(mixed, "tensor", scatter_dimension=1, tiled=True)
    first, second = returned(across(3)), returned(across(2))
    low, high = combine(pick, mix, first, [], cuts=2)
    passed = swap(low, "tensor", 1)
    far = (swap(high, "tensor", 3), width // 2)
    onwards = combine(pick, mix, second, [(passed, 0)])[0]
    over = (swap(onwards, "tensor", 2), 0)
    near = combine(pick, mix, returned(across(1), second[1:2]), [])[0]
    beside = (swap(near, "tensor", 1), 0)
    return combine(pick, mix, returned(across(0), [passed]), [beside, over, far])[0]


def solution(mesh):
    in_specs = (
        P(("groups", "expert"), "tensor"),
        P(("groups", "expert"), None),
        P(("groups", "expert"), None),
        P("expert", None, "tensor"),
        P("expert", None, "tensor"),
        P("expert", "tensor", None),
    )
    out_specs = P(("groups", "expert"), "tensor")
    return jax.shard_map(
        per_device, mesh=mesh, in_specs=in_specs, out_specs=out_specs, check_vma=False
    )
```
